32 devices in a mesh: geo: 4 (over x, core), dist: 8 (over z, y).
Axes of the slice: x: 2, y: 2, z: 4, core: 2. Of those that a mesh axis runs over, the one named last changes fastest.
Arguments:
- estimates: bfloat16 [3072, 7424], P(('geo', 'dist')), may hold values from -4 to 4
- factors: bfloat16 [3072, 7424], P(('geo', 'dist')), may hold values from -0.625 to 0.625
- variances: bfloat16 [3072, 116], P(('geo', 'dist')), may hold values from 0.019897461 to 0.5
- intersection_tracts: int32 [1024, 32], P('dist'), may hold values from 0 to 3071, as said below
- intersection_weights: int32 [1024, 32], P('dist'), may hold values from 1 to 256
Outputs:
- marginal: float32 [1024, 7424], P('dist')
- covariance: float32 [1024, 13456], P('dist')
The draws below stay inside these ranges and needn't reach their ends.
Inputs may be any that keep to these rules, and one draw needn't show every extreme that they name: `intersection_tracts`: each district's intersections are 32 different tracts among 64 consecutive ones, counted cyclically over the region.
All inputs are finite; a program needn't handle non-finite values.
Results may differ from the reference program's by a relative error of at most 0.0003.
Values may be sent and summed in bfloat16 or wider, within the bound.
No kernel may reach another device: no remote copies, remote signals or barrier semaphores. Data moves between devices by JAX's collectives and lax.ppermute only.
A program may use at most 128 MiB of HBM per device.

```python
import math
import jax
import jax.numpy as jnp
from jax import lax

AGE_GROUPS = 116
RANK = 64
COLUMNS = 64
INTERSECTIONS = 32
WINDOW = 64
DIST_DEV = 128
TRACTS = 3072
DISTRICTS = 1024


def draw_intersection_tracts(key, part):
    first_key, second_key = jax.random.split(jax.random.fold_in(key, 7))
    starts = jax.random.randint(first_key, (DISTRICTS,), 0, TRACTS)
    starts = starts.at[0].set(TRACTS - 1).at[1].set(0)
    row_keys = jax.random.split(second_key, DISTRICTS)

    def inner_offsets(row_key):
        return jax.random.permutation(row_key, WINDOW - 2)[:INTERSECTIONS - 2] + 1
    inner = jax.vmap(inner_offsets)(row_keys)
    lowest = jnp.zeros((DISTRICTS, 1), jnp.int32)
    highest = jnp.full((DISTRICTS, 1), WINDOW - 1, jnp.int32)
    offsets = jnp.concatenate([lowest, highest, inner.astype(jnp.int32)], axis=1)
    return ((starts[:, None] + offsets) % TRACTS).astype(jnp.int32)


def plant(entries, own_key, smallest, largest):
    longest = entries.shape.index(max(entries.shape))
    spots = []
    for shift in (0, 1):
        where = [jax.random.randint(jax.random.fold_in(own_key, axis), (), 0, length) for axis, length in enumerate(entries.shape)]
        where[longest] = (where[longest] + shift) % entries.shape[longest]
        spots.append(tuple(where))
    return entries.at[spots[0]].set(smallest).at[spots[1]].set(largest)


def block_levels(key, dims, cuts, smallest, largest):
    gain = 1.0
    for position, parts in cuts:
        draws = jax.random.uniform(jax.random.fold_in(jax.random.fold_in(key, 6), position), (parts,), jnp.float32, smallest / len(cuts), largest / len(cuts))
        gain = gain * jnp.repeat(jnp.exp(draws), dims[position] // parts).reshape((-1,) + (1,) * (len(dims) - 1 - position))
    return gain


def gaussian(rng, dims, width, reach, cuts=(), held_as=jnp.bfloat16):
    factor_of = block_levels(rng, dims, cuts, -0.22, 0.18) if cuts else 1.0
    result = jax.random.normal(rng, dims, jnp.float32) * width * factor_of
    return jnp.minimum(jnp.maximum(result, -reach), reach).astype(held_as)


def setup_inputs(seed: int = 0) -> dict:
    splits = jax.random.split(jax.random.key(seed), 6)
    estimates = gaussian(splits[0], (TRACTS, AGE_GROUPS * COLUMNS), 0.3, 4.0, ((0, 32),))
    factors = gaussian(splits[1], (TRACTS, AGE_GROUPS * RANK), 0.04, 0.625, ((0, 32),))
    variances = jnp.clip(jnp.exp(math.log(0.5) - 3.224016 * jax.random.uniform(splits[2], (TRACTS, AGE_GROUPS), jnp.float32) ** block_levels(splits[2], (TRACTS, AGE_GROUPS), ((0, 32),), -0.2, 0.2)), 0.019897461, 0.5).astype(jnp.bfloat16)
    intersection_tracts = draw_intersection_tracts(jax.random.fold_in(splits[5], 71), 0)
    intersection_weights = plant(jax.random.randint(splits[4], (DISTRICTS, INTERSECTIONS), 1, 257), jax.random.fold_in(splits[4], 1), 1, 256).astype(jnp.int32)
    return {"estimates": estimates, "factors": factors, "variances": variances, "intersection_tracts": intersection_tracts, "intersection_weights": intersection_weights}


def district_block(estimates, factors, variances, tracts, weights):
    share = weights.astype(jnp.float32) / 256.0
    est_rows = jnp.take(estimates, tracts, axis=0).astype(jnp.float32)
    fac_rows = jnp.take(factors, tracts, axis=0).astype(jnp.float32)
    var_rows = jnp.take(variances, tracts, axis=0).astype(jnp.float32)
    marginal = jnp.einsum("bk,bkc->bc", share, est_rows, precision=lax.Precision.HIGHEST)
    loading = jnp.einsum("bk,bkc->bc", share, fac_rows, precision=lax.Precision.HIGHEST)
    noise = jnp.einsum("bk,bkc->bc", share * share, var_rows, precision=lax.Precision.HIGHEST)
    count = tracts.shape[0]
    shaped = loading.reshape(count, AGE_GROUPS, RANK)
    outer = jnp.einsum("dik,djk->dij", shaped, shaped, precision=lax.Precision.HIGHEST)
    outer = outer + noise[:, :, None] * jnp.eye(AGE_GROUPS, dtype=jnp.float32)[None, :, :]
    return marginal, outer.reshape(count, AGE_GROUPS * AGE_GROUPS)


def reference(estimates, factors, variances, intersection_tracts, intersection_weights):
    blocks = DISTRICTS // DIST_DEV
    tracts = intersection_tracts.reshape(blocks, DIST_DEV, INTERSECTIONS)
    weights = intersection_weights.reshape(blocks, DIST_DEV, INTERSECTIONS)

    def one_block(pair):
        return district_block(estimates, factors, variances, pair[0], pair[1])

    marginal, covariance = lax.map(one_block, (tracts, weights))
    return (marginal.reshape(DISTRICTS, AGE_GROUPS * COLUMNS),
            covariance.reshape(DISTRICTS, AGE_GROUPS * AGE_GROUPS))
```

```python
import functools
import jax
import jax.numpy as jnp
from jax import lax
from jax.experimental import pallas as pl
from jax.experimental.pallas import tpu as pltpu
from jax.sharding import PartitionSpec as P

LANES = 128
CORES = 2
DEPTH = 4
TOP = 32767.0
VMEM_BYTES = 48 * 1024 * 1024


def tile(i, count=1):
    return pl.ds(i * LANES, count * LANES)


def encode(read, write, count):
    top = jnp.abs(read(0))
    for i in range(1, count):
        top = jnp.maximum(top, jnp.abs(read(i)))
    power = jnp.floor(jnp.log2(jnp.maximum(top, 1e-30))) + 1.0
    gain = jnp.exp2(-power) * TOP
    for i in range(count):
        level = jnp.clip(jnp.round(read(i) * gain), -TOP, TOP)
        write(i, level.astype(jnp.int32).astype(jnp.int16))
    write(count, power.astype(jnp.int32).astype(jnp.int16))


def step_of(power):
    return jnp.exp2(power.astype(jnp.int32).astype(jnp.float32)) * (1.0 / TOP)


def decode(level, step):
    return level.astype(jnp.int32).astype(jnp.float32) * step


def weights_kernel(tract_ref, ids_ref, weight_ref, out_ref):
    tracts = tract_ref[0:1, :]
    rows = ids_ref.shape[0]
    for r in range(0, rows, 8):
        ids = ids_ref[r:r + 8, :]
        share = weight_ref[r:r + 8, :].astype(jnp.float32) * (1.0 / 256.0)
        total = jnp.zeros((8, tracts.shape[1]), jnp.float32)
        for k in range(ids.shape[1]):
            total = total + jnp.where(ids[:, k:k + 1] == tracts, share[:, k:k + 1], 0.0)
        out_ref[r:r + 8, :] = total.astype(jnp.bfloat16)


def build_weights(tracts, ids, weights):
    rows, each = ids.shape
    width = tracts.shape[1]
    step = 128
    return pl.pallas_call(
        weights_kernel,
        grid=(rows // step,),
        in_specs=[
            pl.BlockSpec((8, width), lambda i: (0, 0)),
            pl.BlockSpec((step, each), lambda i: (i, 0)),
            pl.BlockSpec((step, each), lambda i: (i, 0)),
        ],
        out_specs=pl.BlockSpec((step, width), lambda i: (i, 0)),
        out_shape=jax.ShapeDtypeStruct((rows, width), jnp.bfloat16),
        compiler_params=pltpu.CompilerParams(vmem_limit_bytes=VMEM_BYTES),
        cost_estimate=pl.CostEstimate(flops=rows * width * each * 3, bytes_accessed=rows * width * 2, transcendentals=0),
        name="build_weights",
    )(tracts, ids, weights)


def sums_kernel(parts, has_var, flag_ref, w_ref, *refs):
    data = refs[:parts]
    own_ref = refs[parts]
    outs = refs[parts + 1:parts + DEPTH]
    acc_ref = refs[parts + DEPTH]
    depth = data[0].shape[0]
    count = acc_ref.shape[1] // LANES
    k = pl.program_id(0)

    def weighted(get, columns):
        total = None
        for j in range(parts):
            part = jnp.dot(get(j), data[j][:, columns], preferred_element_type=jnp.float32)
            total = part if total is None else total + part
        return total

    def weights(j):
        return w_ref[:, j * depth:(j + 1) * depth]

    acc_ref[...] = weighted(weights, slice(None))
    if has_var:
        @pl.when(flag_ref[0] == 1)
        def _():
            def square(j):
                w = weights(j).astype(jnp.float32)
                return w * w

            def high(j):
                return square(j).astype(jnp.bfloat16)

            def low(j):
                s = square(j)
                return (s - s.astype(jnp.bfloat16).astype(jnp.float32)).astype(jnp.bfloat16)

            last = tile(count - 1)
            acc_ref[:, last] = weighted(high, last) + weighted(low, last)

    @pl.when(k == 0)
    def _():
        own_ref[...] = acc_ref[...]

    for i in range(1, DEPTH):
        out = outs[i - 1]

        @pl.when(k == i)
        def _(out=out):
            def write(t, value):
                out[:, tile(t)] = value
            encode(lambda t: acc_ref[:, tile(t)], write, count)


def partial_sums(flag, w, data, has_var):
    rows = w.shape[0] // DEPTH
    depth, columns = data[0].shape
    count = columns // LANES
    parts = len(data)
    coded = jax.ShapeDtypeStruct((rows, (count + 1) * LANES), jnp.int16)
    whole = lambda i, s: (0, 0)
    return pl.pallas_call(
        functools.partial(sums_kernel, parts, has_var),
        grid_spec=pltpu.PrefetchScalarGridSpec(
            num_scalar_prefetch=1,
            grid=(DEPTH,),
            in_specs=[pl.BlockSpec((rows, w.shape[1]), lambda i, s: (i, 0))]
            + [pl.BlockSpec((depth, columns), whole)] * parts,
            out_specs=[pl.BlockSpec((rows, columns), whole)]
            + [pl.BlockSpec(coded.shape, whole)] * (DEPTH - 1),
            scratch_shapes=[pltpu.VMEM((rows, columns), jnp.float32)],
        ),
        out_shape=[jax.ShapeDtypeStruct((rows, columns), jnp.float32)] + [coded] * (DEPTH - 1),
        compiler_params=pltpu.CompilerParams(vmem_limit_bytes=VMEM_BYTES),
        cost_estimate=pl.CostEstimate(
            flops=2 * rows * DEPTH * w.shape[1] * columns,
            bytes_accessed=2 * depth * parts * columns + rows * columns * 10,
            transcendentals=0,
        ),
        name="partial_sums",
    )(flag, w, *data)


def combine_kernel(own_ref, *refs):
    others, out_ref, acc_ref = refs[:-2], refs[-2], refs[-1]
    count = acc_ref.shape[1] // LANES
    steps = [step_of(o[:, tile(count)]) for o in others]
    for t in range(count):
        total = own_ref[:, tile(t)]
        for o, step in zip(others, steps):
            total = total + decode(o[:, tile(t)], step)
        acc_ref[:, tile(t)] = total

    def write(t, value):
        out_ref[:, tile(t)] = value
    encode(lambda t: acc_ref[:, tile(t)], write, count)


def combine(own, others):
    rows, columns = own.shape
    wide = columns + LANES
    step = 32
    return pl.pallas_call(
        combine_kernel,
        grid=(rows // step,),
        in_specs=[pl.BlockSpec((step, columns), lambda i: (i, 0))]
        + [pl.BlockSpec((step, wide), lambda i: (i, 0))] * len(others),
        out_specs=pl.BlockSpec((step, wide), lambda i: (i, 0)),
        out_shape=jax.ShapeDtypeStruct((rows, wide), jnp.int16),
        scratch_shapes=[pltpu.VMEM((step, columns), jnp.float32)],
        compiler_params=pltpu.CompilerParams(vmem_limit_bytes=VMEM_BYTES),
        cost_estimate=pl.CostEstimate(flops=rows * columns * 16, bytes_accessed=rows * columns * 12, transcendentals=0),
        name="combine",
    )(own, *others)


def place(order_ref, pieces, dest_ref, each, total, groups):
    count = pieces[0].shape[1] // LANES - 1

    def store(r, start):
        step = step_of(pieces[r][:, tile(count)])
        for t in range(count):
            where = pl.ds(pl.multiple_of((start + t) * LANES, LANES), LANES)
            dest_ref[:, where] = decode(pieces[r][:, tile(t)], step)

    for last in (True, False):
        for r in range(groups):
            group = order_ref[r]

            @pl.when((group == groups - 1) == last)
            def _(r=r, group=group):
                store(r, jnp.minimum(group * each, total - each))


def marginal_kernel(each, total, order_ref, *refs):
    place(order_ref, refs[:-1], refs[-1], each, total, len(refs) - 1)


def marginal(order, pieces, each, total):
    rows, wide = pieces[0].shape
    step = 32
    return pl.pallas_call(
        functools.partial(marginal_kernel, each, total),
        grid_spec=pltpu.PrefetchScalarGridSpec(
            num_scalar_prefetch=1,
            grid=(rows // step,),
            in_specs=[pl.BlockSpec((step, wide), lambda i, s: (i, 0))] * len(pieces),
            out_specs=pl.BlockSpec((step, total * LANES), lambda i, s: (i, 0)),
        ),
        out_shape=jax.ShapeDtypeStruct((rows, total * LANES), jnp.float32),
        compiler_params=pltpu.CompilerParams(vmem_limit_bytes=VMEM_BYTES),
        cost_estimate=pl.CostEstimate(
            flops=rows * total * LANES * 2, bytes_accessed=rows * total * LANES * 6, transcendentals=0
        ),
        name="marginal",
    )(order, *pieces)


def covariance_kernel(each, total, ages, rank, order_ref, *refs):
    pieces, out_ref = refs[:-4], refs[-4]
    load_ref, age_ref, cov_ref = refs[-3:]
    pitch = age_ref.shape[0] // 8
    place(order_ref, pieces, load_ref, each, total, len(pieces))
    per_tile = LANES // rank
    wide = cov_ref.shape[1]
    row_id = lax.broadcasted_iota(jnp.int32, (ages, ages), 0)
    col_id = lax.broadcasted_iota(jnp.int32, (ages, ages), 1)
    diagonal = row_id == col_id
    contract = (((1,), (1,)), ((), ()))
    for base in range(0, load_ref.shape[0], 8):
        rows = slice(base, base + 8)
        for t in range(ages // per_tile):
            value = load_ref[rows, tile(t)]
            for p in range(per_tile):
                age_ref[pl.ds(per_tile * t + p, 8, stride=pitch), :] = (
                    value if p == 0 else pltpu.roll(value, LANES - p * rank, 1)
                )
        for d in range(8):
            mine = age_ref[d * pitch:d * pitch + ages, :rank]
            high = mine.astype(jnp.bfloat16)
            low = (mine - high.astype(jnp.float32)).astype(jnp.bfloat16)
            outer = (
                lax.dot_general(high, high, contract, preferred_element_type=jnp.float32)
                + lax.dot_general(high, low, contract, preferred_element_type=jnp.float32)
                + lax.dot_general(low, high, contract, preferred_element_type=jnp.float32)
            )
            noise = load_ref[base + d:base + d + 1, (total - 1) * LANES:(total - 1) * LANES + ages]
            outer = outer + jnp.where(diagonal, noise, 0.0)
            cov_ref[d * pitch:d * pitch + ages, :ages] = outer
        for i in range(ages):
            out_ref[rows, i * ages:(i + 1) * ages] = cov_ref[pl.ds(i, 8, stride=pitch), :][:, :ages]


def covariance(order, pieces, each, total, ages, rank):
    rows, wide = pieces[0].shape
    step = 16
    pitch = -(-ages // 8) * 8
    return pl.pallas_call(
        functools.partial(covariance_kernel, each, total, ages, rank),
        grid_spec=pltpu.PrefetchScalarGridSpec(
            num_scalar_prefetch=1,
            grid=(rows // step,),
            in_specs=[pl.BlockSpec((step, wide), lambda i, s: (i, 0))] * len(pieces),
            out_specs=pl.BlockSpec((step, ages * ages), lambda i, s: (i, 0)),
            scratch_shapes=[
                pltpu.VMEM((step, total * LANES), jnp.float32),
                pltpu.VMEM((8 * pitch, LANES), jnp.float32),
                pltpu.VMEM((8 * pitch, LANES), jnp.float32),
            ],
        ),
        out_shape=jax.ShapeDtypeStruct((rows, ages * ages), jnp.float32),
        compiler_params=pltpu.CompilerParams(vmem_limit_bytes=VMEM_BYTES),
        cost_estimate=pl.CostEstimate(
            flops=rows * ages * ages * rank * 32, bytes_accessed=rows * ages * ages * 4, transcendentals=0
        ),
        name="covariance",
    )(order, *pieces)


def shards(groups, parts, estimates, factors, variances, intersection_tracts, intersection_weights):
    xs = groups // CORES
    ys = parts // DEPTH
    rows = estimates.shape[0]
    ages = variances.shape[1]
    rank = factors.shape[1] // ages
    geo = lax.axis_index("geo")
    dist = lax.axis_index("dist")
    x, core = geo // CORES, geo % CORES
    z, y = dist // ys, dist % ys
    shifts = [(dx, dc) for dx in range(xs) for dc in range(CORES)]

    def geo_shift(value, dx, dc):
        if dx == 0 and dc == 0:
            return value
        perm = [(a * CORES + b, (a + dx) % xs * CORES + (b + dc) % CORES) for a in range(xs) for b in range(CORES)]
        return lax.ppermute(value, "geo", perm)

    def y_shift(value, dy):
        if dy == 0:
            return value
        perm = [(a * ys + b, a * ys + (b + dy) % ys) for a in range(DEPTH) for b in range(ys)]
        return lax.ppermute(value, "dist", perm)

    def z_shift(value, dz):
        if dz % DEPTH == 0:
            return value
        perm = [(a * ys + b, (a + dz) % DEPTH * ys + b) for a in range(DEPTH) for b in range(ys)]
        return lax.ppermute(value, "dist", perm)

    queries = jnp.concatenate([intersection_tracts, intersection_weights], axis=1)
    queries = jnp.concatenate([z_shift(queries, -k) for k in range(DEPTH)], axis=0)
    each = intersection_tracts.shape[1]

    bases = [
        (((x - dx) % xs * CORES + (core - dc) % CORES) * parts + z * ys + (y - dy) % ys) * rows
        for dy in range(ys) for dx, dc in shifts
    ]
    tracts = jnp.concatenate([base + jnp.arange(rows, dtype=jnp.int32) for base in bases])
    tracts = jnp.broadcast_to(tracts[None, :], (8, tracts.shape[0]))
    w = build_weights(tracts, queries[:, :each], queries[:, each:])

    variances = jnp.pad(variances, ((0, 0), (0, -ages % LANES)))
    loads = jnp.concatenate([factors, variances], axis=1)
    order = jnp.stack([(x - dx) % xs * CORES + (core - dc) % CORES for dx, dc in shifts]).astype(jnp.int32)
    flag = (geo == groups - 1).astype(jnp.int32).reshape(1)

    def collect(array, has_var):
        total = array.shape[1] // LANES
        count = -(-total // groups)
        pieces = []
        for dx, dc in shifts:
            target = (x + dx) % xs * CORES + (core + dc) % CORES
            start = jnp.minimum(target * count, total - count) * LANES
            piece = lax.dynamic_slice(array, (0, start), (rows, count * LANES))
            pieces.append(geo_shift(piece, dx, dc))
        data = [
            jnp.concatenate([y_shift(piece, dy) for piece in pieces], axis=0) for dy in range(ys)
        ]
        own, *outs = partial_sums(flag, w, data, has_var)
        others = [z_shift(out, k + 1) for k, out in enumerate(outs)]
        mine = combine(own, others)
        rowwise = [geo_shift(mine, dx, 0) for dx in range(xs)]
        gathered = [geo_shift(rowwise[dx], 0, dc) for dx, dc in shifts]
        return gathered, count, total

    load_pieces, load_count, load_total = collect(loads, True)
    mean_pieces, mean_count, mean_total = collect(estimates, False)
    cov = covariance(order, load_pieces, load_count, load_total, ages, rank)
    mean = marginal(order, mean_pieces, mean_count, mean_total)
    return mean, cov


def solution(mesh):
    return jax.shard_map(
        functools.partial(shards, mesh.shape["geo"], mesh.shape["dist"]),
        mesh=mesh,
        in_specs=(
            P(("geo", "dist"), None),
            P(("geo", "dist"), None),
            P(("geo", "dist"), None),
            P("dist", None),
            P("dist", None),
        ),
        out_specs=(P("dist", None), P("dist", None)),
        check_vma=False,
    )
```

```python
import functools
import jax
import jax.numpy as jnp
from jax import lax
from jax.experimental import pallas as pl
from jax.experimental.pallas import tpu as pltpu
from jax.sharding import PartitionSpec as P

LANES = 128
CORES = 2
DEPTH = 4
SCALES = 16
TOP = 32767.0
VMEM_BYTES = 48 * 1024 * 1024
BEFORE = (((0,), (0,)), ((), ()))
AFTER = (((1,), (1,)), ((), ()))


def params():
    return pltpu.CompilerParams(vmem_limit_bytes=VMEM_BYTES)


def cost(flops, moved):
    return pl.CostEstimate(flops=flops, bytes_accessed=moved, transcendentals=0)


def twice(value):
    return jnp.concatenate([value, value], axis=0)


def encode(src, src_base, dst, dst_base, height):
    half = height // 2
    powers = []
    for h in range(2):
        top = jnp.abs(src[pl.ds(src_base + h * half, 8), :])
        for r in range(8, half, 8):
            top = jnp.maximum(top, jnp.abs(src[pl.ds(src_base + h * half + r, 8), :]))
        power = jnp.floor(jnp.log2(jnp.maximum(top, 1e-30))) + 1.0
        gain = twice(jnp.exp2(-power) * TOP)
        for r in range(h * half, (h + 1) * half, 16):
            level = jnp.clip(jnp.round(src[pl.ds(src_base + r, 16), :] * gain), -TOP, TOP)
            dst[pl.ds(dst_base + r, 16), :] = level.astype(jnp.int32).astype(jnp.int16)
        powers.append(power)
    both = jnp.concatenate(powers, axis=0)
    dst[pl.ds(dst_base + height, SCALES), :] = both.astype(jnp.int32).astype(jnp.int16)


def steps_of(coded, base, height):
    power = coded[pl.ds(base + height, SCALES), :].astype(jnp.int32).astype(jnp.float32)
    step = jnp.exp2(power) * (1.0 / TOP)
    return [twice(step[:8]), twice(step[8:])]


def decode(coded, row, step):
    return coded[pl.ds(row, 16), :].astype(jnp.int32).astype(jnp.float32) * step


def weights_kernel(rows, base_ref, query_ref, out_ref):
    each = query_ref.shape[0] // 2
    row_id = lax.broadcasted_iota(jnp.int32, (16, LANES), 0)

    def piece(j, carry):
        for u in range(DEPTH):
            lanes = slice(u * LANES, (u + 1) * LANES)
            for r in range(0, rows, 16):
                tract = row_id + (base_ref[j] + r)
                total = jnp.zeros((16, LANES), jnp.float32)
                for k in range(each):
                    share = query_ref[each + k:each + k + 1, lanes].astype(jnp.float32) * (1.0 / 256.0)
                    total = jnp.where(query_ref[k:k + 1, lanes] == tract, share, total)
                where = pl.ds(pl.multiple_of(j * rows + r, 16), 16)
                out_ref[where, lanes] = total.astype(jnp.bfloat16)
        return carry

    lax.fori_loop(0, out_ref.shape[0] // rows, piece, 0)


def build_weights(bases, queries, rows):
    pieces = bases.shape[0]
    width = queries.shape[1]
    shape = (pieces * rows, width)
    return pl.pallas_call(
        functools.partial(weights_kernel, rows),
        grid_spec=pltpu.PrefetchScalarGridSpec(
            num_scalar_prefetch=1,
            grid=(1,),
            in_specs=[pl.BlockSpec(queries.shape, lambda i, s: (0, 0))],
            out_specs=pl.BlockSpec(shape, lambda i, s: (0, 0)),
        ),
        out_shape=jax.ShapeDtypeStruct(shape, jnp.bfloat16),
        compiler_params=params(),
        cost_estimate=cost(shape[0] * width * queries.shape[0], shape[0] * width * 2),
        name="build_weights",
    )(bases, queries)


def sums_kernel(parts, has_var, flag_ref, w_ref, *refs):
    data = refs[:parts]
    own_ref, near_ref, far_ref, acc_ref = refs[parts:]
    depth, columns = data[0].shape
    coded = columns + SCALES

    def weighted(get, t):
        total = None
        for j in range(parts):
            part = lax.dot_general(
                data[j][:, t * LANES:(t + 1) * LANES],
                get(w_ref[j * depth:(j + 1) * depth, :]),
                BEFORE,
                preferred_element_type=jnp.float32,
            )
            total = part if total is None else total + part
        return total

    def put(t, value):
        where = slice(t * LANES, (t + 1) * LANES)
        own_ref[where, :] = value[:, :LANES]
        for u in range(1, DEPTH):
            acc_ref[u - 1, where, :] = value[:, u * LANES:(u + 1) * LANES]

    for t in range(columns // LANES):
        put(t, weighted(lambda w: w, t))

    if has_var:
        @pl.when(flag_ref[0] == 1)
        def _():
            def square(w):
                wide = w.astype(jnp.float32)
                return wide * wide

            def high(w):
                return square(w).astype(jnp.bfloat16)

            def low(w):
                s = square(w)
                return (s - s.astype(jnp.bfloat16).astype(jnp.float32)).astype(jnp.bfloat16)

            t = columns // LANES - 1
            put(t, weighted(high, t) + weighted(low, t))

    encode(acc_ref.at[0], 0, near_ref, 0, columns)
    encode(acc_ref.at[1], 0, far_ref, 0, columns)
    encode(acc_ref.at[2], 0, far_ref, coded, columns)


def partial_sums(flag, w, data, has_var):
    depth, columns = data[0].shape
    parts = len(data)
    coded = columns + SCALES
    whole = lambda i, s: (0, 0)
    shapes = [
        jax.ShapeDtypeStruct((columns, LANES), jnp.float32),
        jax.ShapeDtypeStruct((coded, LANES), jnp.int16),
        jax.ShapeDtypeStruct((2 * coded, LANES), jnp.int16),
    ]
    return pl.pallas_call(
        functools.partial(sums_kernel, parts, has_var),
        grid_spec=pltpu.PrefetchScalarGridSpec(
            num_scalar_prefetch=1,
            grid=(1,),
            in_specs=[pl.BlockSpec(w.shape, whole)] + [pl.BlockSpec((depth, columns), whole)] * parts,
            out_specs=[pl.BlockSpec(s.shape, whole) for s in shapes],
            scratch_shapes=[pltpu.VMEM((DEPTH - 1, columns, LANES), jnp.float32)],
        ),
        out_shape=shapes,
        compiler_params=params(),
        cost_estimate=cost(2 * w.shape[0] * w.shape[1] * columns, 2 * depth * parts * columns + columns * LANES * 10),
        name="partial_sums",
    )(flag, w, *data)


def middle_kernel(own_ref, other_ref, near_ref, end_ref, acc_ref):
    height = acc_ref.shape[0]
    for u, out in enumerate((near_ref, end_ref)):
        base = u * (height + SCALES)
        mine = steps_of(own_ref, base, height)
        theirs = steps_of(other_ref, base, height)
        for r in range(0, height, 16):
            h = r * 2 // height
            acc_ref[r:r + 16, :] = decode(own_ref, base + r, mine[h]) + decode(other_ref, base + r, theirs[h])
        encode(acc_ref, 0, out, 0, height)


def middle(own, other):
    coded = own.shape[0] // 2
    shape = jax.ShapeDtypeStruct((coded, LANES), jnp.int16)
    return pl.pallas_call(
        middle_kernel,
        out_shape=[shape, shape],
        scratch_shapes=[pltpu.VMEM((coded - SCALES, LANES), jnp.float32)],
        compiler_params=params(),
        cost_estimate=cost(coded * LANES * 32, coded * LANES * 12),
        name="middle",
    )(own, other)


def combine_kernel(own_ref, *refs):
    others, out_ref, acc_ref = refs[:-2], refs[-2], refs[-1]
    height = acc_ref.shape[0]
    steps = [steps_of(o, 0, height) for o in others]
    for r in range(0, height, 16):
        total = own_ref[r:r + 16, :]
        for o, step in zip(others, steps):
            total = total + decode(o, r, step[r * 2 // height])
        acc_ref[r:r + 16, :] = total
    encode(acc_ref, 0, out_ref, 0, height)


def combine(own, others):
    height = own.shape[0]
    shape = (height + SCALES, LANES)
    return pl.pallas_call(
        combine_kernel,
        out_shape=jax.ShapeDtypeStruct(shape, jnp.int16),
        scratch_shapes=[pltpu.VMEM((height, LANES), jnp.float32)],
        compiler_params=params(),
        cost_estimate=cost(height * LANES * 16, height * LANES * 12),
        name="combine",
    )(own, *others)


def each_piece(place_ref, pieces, tiles, do):
    groups = place_ref.shape[0] // 2
    for upper in (1, 0):
        for r in range(groups):
            @pl.when(place_ref[groups + r] == upper)
            def _(r=r):
                first = 0
                for c, count in enumerate(tiles):
                    do((place_ref[r] + first) * LANES, pieces[c * groups + r], count * LANES)
                    first += count


def marginal_kernel(tiles, place_ref, *refs):
    pieces, out_ref, tile_ref = refs[:-2], refs[-2], refs[-1]

    def do(start, piece, height):
        steps = steps_of(piece, 0, height)
        for t in range(0, height, LANES):
            for r in range(0, LANES, 16):
                tile_ref[r:r + 16, :] = decode(piece, t + r, steps[(t + r) * 2 // height])
            out_ref[:, pl.ds(pl.multiple_of(start + t, LANES), LANES)] = tile_ref[...].T

    each_piece(place_ref, pieces, tiles, do)


def marginal(places, pieces, tiles, total):
    shape = (LANES, total * LANES)
    return pl.pallas_call(
        functools.partial(marginal_kernel, tiles),
        grid_spec=pltpu.PrefetchScalarGridSpec(
            num_scalar_prefetch=1,
            grid=(1,),
            in_specs=[pl.BlockSpec(p.shape, lambda i, s: (0, 0)) for p in pieces],
            out_specs=pl.BlockSpec(shape, lambda i, s: (0, 0)),
            scratch_shapes=[pltpu.VMEM((LANES, LANES), jnp.float32)],
        ),
        out_shape=jax.ShapeDtypeStruct(shape, jnp.float32),
        compiler_params=params(),
        cost_estimate=cost(shape[0] * shape[1] * 4, shape[0] * shape[1] * 6),
        name="marginal",
    )(places, *pieces)


def covariance_kernel(tiles, total, ages, rank, place_ref, *refs):
    pieces, out_ref = refs[:-4], refs[-4]
    load_ref, age_ref, cov_ref = refs[-3:]
    pitch = -(-ages // 8) * 8
    left = lax.broadcasted_iota(jnp.int32, (LANES, LANES), 1) < rank

    def do(start, piece, height):
        steps = steps_of(piece, 0, height)
        for r in range(0, height, 16):
            load_ref[pl.ds(pl.multiple_of(start + r, 16), 16), :] = decode(piece, r, steps[r * 2 // height])

    each_piece(place_ref, pieces, tiles, do)

    def turn(t, carry):
        value = load_ref[pl.ds(pl.multiple_of(t * LANES, LANES), LANES), :].T
        swapped = pltpu.roll(value, rank, 1)
        age_ref[pl.ds(2 * t, LANES, stride=pitch), :] = jnp.where(left, value, swapped)
        age_ref[pl.ds(2 * t + 1, LANES, stride=pitch), :] = jnp.where(left, swapped, value)
        return carry

    lax.fori_loop(0, ages * rank // LANES, turn, 0)

    def outer(d, carry):
        start = pl.multiple_of(d * pitch, 8)
        mine = age_ref[pl.ds(start, LANES), :]
        high = mine.astype(jnp.bfloat16).astype(jnp.float32)
        low = mine - high
        mixed = jnp.where(left, high, low).astype(jnp.bfloat16)
        product = lax.dot_general(
            jnp.concatenate([mixed, mixed], axis=1),
            jnp.concatenate([high.astype(jnp.bfloat16), low.astype(jnp.bfloat16)], axis=1),
            AFTER,
            preferred_element_type=jnp.float32,
        )
        cov_ref[pl.ds(start, pitch), :] = product[:pitch]
        return carry

    lax.fori_loop(0, LANES, outer, 0, unroll=4)

    def store(m, carry):
        base = pl.multiple_of(m * (2 * ages), 8)
        for p in range(2):
            value = cov_ref[pl.ds(2 * m + p, LANES, stride=pitch), :].T
            out_ref[pl.ds(base + p * ages, ages), :] = value[:ages]
        return carry

    lax.fori_loop(0, ages // 2, store, 0)
    for i in range(ages):
        row = i * (ages + 1)
        out_ref[row:row + 1, :] += load_ref[(total - 1) * LANES + i:(total - 1) * LANES + i + 1, :]


def covariance(places, pieces, tiles, total, ages, rank):
    pitch = -(-ages // 8) * 8
    shape = (ages * ages, LANES)
    tall = (LANES * pitch + LANES - pitch, LANES)
    return pl.pallas_call(
        functools.partial(covariance_kernel, tiles, total, ages, rank),
        grid_spec=pltpu.PrefetchScalarGridSpec(
            num_scalar_prefetch=1,
            grid=(1,),
            in_specs=[pl.BlockSpec(p.shape, lambda i, s: (0, 0)) for p in pieces],
            out_specs=pl.BlockSpec(shape, lambda i, s: (0, 0)),
            scratch_shapes=[
                pltpu.VMEM((total * LANES, LANES), jnp.float32),
                pltpu.VMEM(tall, jnp.float32),
                pltpu.VMEM(tall, jnp.float32),
            ],
        ),
        out_shape=jax.ShapeDtypeStruct(shape, jnp.float32),
        compiler_params=params(),
        cost_estimate=cost(LANES * ages * ages * rank * 32, shape[0] * shape[1] * 4),
        name="covariance",
    )(places, *pieces)


def shards(groups, parts, estimates, factors, variances, intersection_tracts, intersection_weights):
    xs = groups // CORES
    ys = parts // DEPTH
    rows = estimates.shape[0]
    ages = variances.shape[1]
    rank = factors.shape[1] // ages
    geo = lax.axis_index("geo")
    dist = lax.axis_index("dist")
    x, core = geo // CORES, geo % CORES
    z, y = dist // ys, dist % ys

    def geo_shift(value, dx, dc):
        if dx == 0 and dc == 0:
            return value
        perm = [(a * CORES + b, (a + dx) % xs * CORES + (b + dc) % CORES) for a in range(xs) for b in range(CORES)]
        return lax.ppermute(value, "geo", perm)

    def y_shift(value, dy):
        if dy == 0:
            return value
        perm = [(a * ys + b, a * ys + (b + dy) % ys) for a in range(DEPTH) for b in range(ys)]
        return lax.ppermute(value, "dist", perm)

    def z_send(value, pairs):
        perm = [(a * ys + b, c * ys + b) for a, c in pairs for b in range(ys)]
        return lax.ppermute(value, "dist", perm)

    near = ((0, 1), (1, 0), (2, 3), (3, 2))
    mirror = ((0, 3), (1, 2), (2, 1), (3, 0))
    across = ((0, 2), (1, 3), (2, 0), (3, 1))
    queries = jnp.concatenate([intersection_tracts.T, intersection_weights.T], axis=0)
    in_middle = (z == 1) | (z == 2)
    at_mirror, at_across = z_send(queries, mirror), z_send(queries, across)
    queries = jnp.concatenate(
        [
            queries,
            z_send(queries, near),
            jnp.where(in_middle, at_mirror, at_across),
            jnp.where(in_middle, at_across, at_mirror),
        ],
        axis=1,
    )

    bases = jnp.stack([
        (((x - dx) % xs * CORES + (core - dc) % CORES) * parts + z * ys + (y - dy) % ys) * rows
        for dy in range(ys) for dx in range(xs) for dc in range(CORES)
    ]).astype(jnp.int32)
    w = build_weights(bases, queries, rows)
    flag = ((core == CORES - 1) & (x == xs - 1)).astype(jnp.int32).reshape(1)

    variances = jnp.pad(variances, ((0, 0), (0, -ages % LANES)))
    loads = jnp.concatenate([factors, variances], axis=1)

    def halves(array):
        total = array.shape[1] // LANES
        width = -(-total // groups) * xs

        def half(c):
            return lax.dynamic_slice(array, (0, jnp.where(c == 0, 0, total - width) * LANES), (rows, width * LANES))

        return jnp.concatenate([half(core), geo_shift(half(1 - core), 0, 1)], axis=0)

    def collect(both, first, count, each, has_var):
        def part(group):
            return lax.dynamic_slice(
                both, (0, (group * each + first) * LANES), (both.shape[0], count * LANES)
            )
        by_x = [geo_shift(part((x + dx) % xs), dx, 0) for dx in range(xs)]
        data = [y_shift(value, dy) for dy in range(ys) for value in by_x]
        own, close, far = partial_sums(flag, w, data, has_var)
        far_in = z_send(far, ((0, 1), (3, 2)))
        close_in = z_send(close, near)
        to_middle, to_end = middle(far, far_in)
        middle_in = z_send(to_middle, ((1, 2), (2, 1)))
        end_in = z_send(to_end, ((1, 3), (2, 0)))
        mine = combine(own, [close_in, middle_in, end_in])
        along = [geo_shift(mine, dx, 0) for dx in range(xs)]
        return [geo_shift(along[dx], 0, dc) for dx in range(xs) for dc in range(CORES)]

    def places(total):
        each = -(-total // groups)
        starts, uppers = [], []
        for dx in range(xs):
            for dc in range(CORES):
                c, a = (core - dc) % CORES, (x - dx) % xs
                starts.append(jnp.where(c == 0, 0, total - each * xs) + a * each)
                uppers.append(c)
        return jnp.stack(starts + uppers).astype(jnp.int32)

    def split(each):
        return (each // 2, each - each // 2)

    load_total = loads.shape[1] // LANES
    mean_total = estimates.shape[1] // LANES
    load_each, mean_each = -(-load_total // groups), -(-mean_total // groups)
    load_tiles = split(load_each)
    mean_tiles = split(mean_each)[::-1]
    load_half = halves(loads)
    mean_half = halves(estimates)
    load_pieces, mean_pieces = [], []
    first = 0
    for i, count in enumerate(load_tiles):
        load_pieces += collect(load_half, first, count, load_each, i == len(load_tiles) - 1)
        first += count
    first = 0
    for count in mean_tiles:
        mean_pieces += collect(mean_half, first, count, mean_each, False)
        first += count
    cov = covariance(places(load_total), load_pieces, load_tiles, load_total, ages, rank)
    mean = marginal(places(mean_total), mean_pieces, mean_tiles, mean_total)
    return mean, cov.T


def solution(mesh):
    return jax.shard_map(
        functools.partial(shards, mesh.shape["geo"], mesh.shape["dist"]),
        mesh=mesh,
        in_specs=(
            P(("geo", "dist"), None),
            P(("geo", "dist"), None),
            P(("geo", "dist"), None),
            P("dist", None),
            P("dist", None),
        ),
        out_specs=(P("dist", None), P("dist", None)),
        check_vma=False,
    )
```

```python
import functools
import jax
import jax.numpy as jnp
from jax import lax
from jax.experimental import pallas as pl
from jax.experimental.pallas import tpu as pltpu
from jax.sharding import PartitionSpec as P

LANES = 128
CORES = 2
DEPTH = 4
SCALES = 16
TOP = 32767.0
VMEM_BYTES = 48 * 1024 * 1024
BEFORE = (((0,), (0,)), ((), ()))
AFTER = (((1,), (1,)), ((), ()))


def params():
    return pltpu.CompilerParams(vmem_limit_bytes=VMEM_BYTES)


def cost(flops, moved):
    return pl.CostEstimate(flops=flops, bytes_accessed=moved, transcendentals=0)


def after(value, *others):
    return lax.optimization_barrier((value, *others))[0]


def twice(value):
    return jnp.concatenate([value, value], axis=0)


def encode(src, src_base, dst, dst_base, height):
    half = height // 2
    powers = []
    for h in range(2):
        top = jnp.abs(src[pl.ds(src_base + h * half, 8), :])
        for r in range(8, half, 8):
            top = jnp.maximum(top, jnp.abs(src[pl.ds(src_base + h * half + r, 8), :]))
        power = jnp.floor(jnp.log2(jnp.maximum(top, 1e-30))) + 1.0
        gain = twice(jnp.exp2(-power) * TOP)
        for r in range(h * half, (h + 1) * half, 16):
            level = jnp.clip(jnp.round(src[pl.ds(src_base + r, 16), :] * gain), -TOP, TOP)
            dst[pl.ds(dst_base + r, 16), :] = level.astype(jnp.int32).astype(jnp.int16)
        powers.append(power)
    both = jnp.concatenate(powers, axis=0)
    dst[pl.ds(dst_base + height, SCALES), :] = both.astype(jnp.int32).astype(jnp.int16)


def steps_of(coded, base, height):
    power = coded[pl.ds(base + height, SCALES), :].astype(jnp.int32).astype(jnp.float32)
    step = jnp.exp2(power) * (1.0 / TOP)
    return [twice(step[:8]), twice(step[8:])]


def decode(coded, row, step):
    return coded[pl.ds(row, 16), :].astype(jnp.int32).astype(jnp.float32) * step


def weights_kernel(rows, base_ref, query_ref, out_ref):
    each = query_ref.shape[0] // 2
    row_id = lax.broadcasted_iota(jnp.int32, (16, LANES), 0)

    def piece(j, carry):
        for u in range(DEPTH):
            lanes = slice(u * LANES, (u + 1) * LANES)
            for r in range(0, rows, 16):
                tract = row_id + (base_ref[j] + r)
                total = jnp.zeros((16, LANES), jnp.float32)
                for k in range(each):
                    share = query_ref[each + k:each + k + 1, lanes].astype(jnp.float32) * (1.0 / 256.0)
                    total = jnp.where(query_ref[k:k + 1, lanes] == tract, share, total)
                where = pl.ds(pl.multiple_of(j * rows + r, 16), 16)
                out_ref[where, lanes] = total.astype(jnp.bfloat16)
        return carry

    lax.fori_loop(0, out_ref.shape[0] // rows, piece, 0)


def build_weights(bases, queries, rows):
    pieces = bases.shape[0]
    width = queries.shape[1]
    shape = (pieces * rows, width)
    return pl.pallas_call(
        functools.partial(weights_kernel, rows),
        grid_spec=pltpu.PrefetchScalarGridSpec(
            num_scalar_prefetch=1,
            grid=(1,),
            in_specs=[pl.BlockSpec(queries.shape, lambda i, s: (0, 0))],
            out_specs=pl.BlockSpec(shape, lambda i, s: (0, 0)),
        ),
        out_shape=jax.ShapeDtypeStruct(shape, jnp.bfloat16),
        compiler_params=params(),
        cost_estimate=cost(shape[0] * width * queries.shape[0], shape[0] * width * 2),
        name="build_weights",
    )(bases, queries)


def sums_kernel(parts, has_var, flag_ref, w_ref, *refs):
    data = refs[:parts]
    own_ref, near_ref, far_ref, acc_ref = refs[parts:]
    depth, columns = data[0].shape
    coded = columns + SCALES

    def weighted(get, t):
        total = None
        for j in range(parts):
            part = lax.dot_general(
                data[j][:, t * LANES:(t + 1) * LANES],
                get(w_ref[j * depth:(j + 1) * depth, :]),
                BEFORE,
                preferred_element_type=jnp.float32,
            )
            total = part if total is None else total + part
        return total

    def put(t, value):
        where = slice(t * LANES, (t + 1) * LANES)
        own_ref[where, :] = value[:, :LANES]
        for u in range(1, DEPTH):
            acc_ref[u - 1, where, :] = value[:, u * LANES:(u + 1) * LANES]

    for t in range(columns // LANES):
        put(t, weighted(lambda w: w, t))

    if has_var:
        @pl.when(flag_ref[0] == 1)
        def _():
            def square(w):
                wide = w.astype(jnp.float32)
                return wide * wide

            def high(w):
                return square(w).astype(jnp.bfloat16)

            def low(w):
                s = square(w)
                return (s - s.astype(jnp.bfloat16).astype(jnp.float32)).astype(jnp.bfloat16)

            t = columns // LANES - 1
            put(t, weighted(high, t) + weighted(low, t))

    encode(acc_ref.at[0], 0, near_ref, 0, columns)
    encode(acc_ref.at[1], 0, far_ref, 0, columns)
    encode(acc_ref.at[2], 0, far_ref, coded, columns)


def partial_sums(flag, w, data, has_var):
    depth, columns = data[0].shape
    parts = len(data)
    coded = columns + SCALES
    whole = lambda i, s: (0, 0)
    shapes = [
        jax.ShapeDtypeStruct((columns, LANES), jnp.float32),
        jax.ShapeDtypeStruct((coded, LANES), jnp.int16),
        jax.ShapeDtypeStruct((2 * coded, LANES), jnp.int16),
    ]
    return pl.pallas_call(
        functools.partial(sums_kernel, parts, has_var),
        grid_spec=pltpu.PrefetchScalarGridSpec(
            num_scalar_prefetch=1,
            grid=(1,),
            in_specs=[pl.BlockSpec(w.shape, whole)] + [pl.BlockSpec((depth, columns), whole)] * parts,
            out_specs=[pl.BlockSpec(s.shape, whole) for s in shapes],
            scratch_shapes=[pltpu.VMEM((DEPTH - 1, columns, LANES), jnp.float32)],
        ),
        out_shape=shapes,
        compiler_params=params(),
        cost_estimate=cost(2 * w.shape[0] * w.shape[1] * columns, 2 * depth * parts * columns + columns * LANES * 10),
        name="partial_sums",
    )(flag, w, *data)


def middle_kernel(own_ref, other_ref, near_ref, end_ref, acc_ref):
    height = acc_ref.shape[0]
    for u, out in enumerate((near_ref, end_ref)):
        base = u * (height + SCALES)
        mine = steps_of(own_ref, base, height)
        theirs = steps_of(other_ref, base, height)
        for r in range(0, height, 16):
            h = r * 2 // height
            acc_ref[r:r + 16, :] = decode(own_ref, base + r, mine[h]) + decode(other_ref, base + r, theirs[h])
        encode(acc_ref, 0, out, 0, height)


def middle(own, other):
    coded = own.shape[0] // 2
    shape = jax.ShapeDtypeStruct((coded, LANES), jnp.int16)
    return pl.pallas_call(
        middle_kernel,
        out_shape=[shape, shape],
        scratch_shapes=[pltpu.VMEM((coded - SCALES, LANES), jnp.float32)],
        compiler_params=params(),
        cost_estimate=cost(coded * LANES * 32, coded * LANES * 12),
        name="middle",
    )(own, other)


def combine_kernel(own_ref, *refs):
    others, out_ref, acc_ref = refs[:-2], refs[-2], refs[-1]
    height = acc_ref.shape[0]
    steps = [steps_of(o, 0, height) for o in others]
    for r in range(0, height, 16):
        total = own_ref[r:r + 16, :]
        for o, step in zip(others, steps):
            total = total + decode(o, r, step[r * 2 // height])
        acc_ref[r:r + 16, :] = total
    encode(acc_ref, 0, out_ref, 0, height)


def combine(own, others):
    height = own.shape[0]
    shape = (height + SCALES, LANES)
    return pl.pallas_call(
        combine_kernel,
        out_shape=jax.ShapeDtypeStruct(shape, jnp.int16),
        scratch_shapes=[pltpu.VMEM((height, LANES), jnp.float32)],
        compiler_params=params(),
        cost_estimate=cost(height * LANES * 16, height * LANES * 12),
        name="combine",
    )(own, *others)


def each_piece(place_ref, pieces, tiles, do):
    groups = place_ref.shape[0] // 2
    for upper in (1, 0):
        for r in range(groups):
            @pl.when(place_ref[groups + r] == upper)
            def _(r=r):
                first = 0
                for c, count in enumerate(tiles):
                    do((place_ref[r] + first) * LANES, pieces[c * groups + r], count * LANES)
                    first += count


def marginal_kernel(tiles, place_ref, *refs):
    pieces, out_ref, tile_ref = refs[:-2], refs[-2], refs[-1]

    def do(start, piece, height):
        steps = steps_of(piece, 0, height)
        for t in range(0, height, LANES):
            for r in range(0, LANES, 16):
                tile_ref[r:r + 16, :] = decode(piece, t + r, steps[(t + r) * 2 // height])
            out_ref[:, pl.ds(pl.multiple_of(start + t, LANES), LANES)] = tile_ref[...].T

    each_piece(place_ref, pieces, tiles, do)


def marginal(places, pieces, tiles, total):
    shape = (LANES, total * LANES)
    return pl.pallas_call(
        functools.partial(marginal_kernel, tiles),
        grid_spec=pltpu.PrefetchScalarGridSpec(
            num_scalar_prefetch=1,
            grid=(1,),
            in_specs=[pl.BlockSpec(p.shape, lambda i, s: (0, 0)) for p in pieces],
            out_specs=pl.BlockSpec(shape, lambda i, s: (0, 0)),
            scratch_shapes=[pltpu.VMEM((LANES, LANES), jnp.float32)],
        ),
        out_shape=jax.ShapeDtypeStruct(shape, jnp.float32),
        compiler_params=params(),
        cost_estimate=cost(shape[0] * shape[1] * 4, shape[0] * shape[1] * 6),
        name="marginal",
    )(places, *pieces)


def covariance_kernel(tiles, total, ages, rank, place_ref, *refs):
    pieces, out_ref = refs[:-4], refs[-4]
    load_ref, age_ref, cov_ref = refs[-3:]
    pitch = -(-ages // 8) * 8
    left = lax.broadcasted_iota(jnp.int32, (LANES, LANES), 1) < rank

    def do(start, piece, height):
        steps = steps_of(piece, 0, height)
        for r in range(0, height, 16):
            load_ref[pl.ds(pl.multiple_of(start + r, 16), 16), :] = decode(piece, r, steps[r * 2 // height])

    each_piece(place_ref, pieces, tiles, do)

    def turn(t, carry):
        value = load_ref[pl.ds(pl.multiple_of(t * LANES, LANES), LANES), :].T
        swapped = pltpu.roll(value, rank, 1)
        age_ref[pl.ds(2 * t, LANES, stride=pitch), :] = jnp.where(left, value, swapped)
        age_ref[pl.ds(2 * t + 1, LANES, stride=pitch), :] = jnp.where(left, swapped, value)
        return carry

    lax.fori_loop(0, ages * rank // LANES, turn, 0, unroll=True)

    def outer(d, carry):
        start = pl.multiple_of(d * pitch, 8)
        mine = age_ref[pl.ds(start, LANES), :]
        high = mine.astype(jnp.bfloat16).astype(jnp.float32)
        low = mine - high
        mixed = jnp.where(left, high, low).astype(jnp.bfloat16)
        product = lax.dot_general(
            jnp.concatenate([mixed, mixed], axis=1),
            jnp.concatenate([high.astype(jnp.bfloat16), low.astype(jnp.bfloat16)], axis=1),
            AFTER,
            preferred_element_type=jnp.float32,
        )
        cov_ref[pl.ds(start, pitch), :] = product[:pitch]
        return carry

    lax.fori_loop(0, LANES, outer, 0, unroll=16)

    def store(m, carry):
        base = pl.multiple_of(m * (2 * ages), 8)
        for p in range(2):
            value = cov_ref[pl.ds(2 * m + p, LANES, stride=pitch), :].T
            out_ref[pl.ds(base + p * ages, ages), :] = value[:ages]
        return carry

    lax.fori_loop(0, ages // 2, store, 0, unroll=True)
    for i in range(ages):
        row = i * (ages + 1)
        out_ref[row:row + 1, :] += load_ref[(total - 1) * LANES + i:(total - 1) * LANES + i + 1, :]


def covariance(places, pieces, tiles, total, ages, rank):
    pitch = -(-ages // 8) * 8
    shape = (ages * ages, LANES)
    tall = (LANES * pitch + LANES - pitch, LANES)
    return pl.pallas_call(
        functools.partial(covariance_kernel, tiles, total, ages, rank),
        grid_spec=pltpu.PrefetchScalarGridSpec(
            num_scalar_prefetch=1,
            grid=(1,),
            in_specs=[pl.BlockSpec(p.shape, lambda i, s: (0, 0)) for p in pieces],
            out_specs=pl.BlockSpec(shape, lambda i, s: (0, 0)),
            scratch_shapes=[
                pltpu.VMEM((total * LANES, LANES), jnp.float32),
                pltpu.VMEM(tall, jnp.float32),
                pltpu.VMEM(tall, jnp.float32),
            ],
        ),
        out_shape=jax.ShapeDtypeStruct(shape, jnp.float32),
        compiler_params=params(),
        cost_estimate=cost(LANES * ages * ages * rank * 32, shape[0] * shape[1] * 4),
        name="covariance",
    )(places, *pieces)


def shards(groups, parts, estimates, factors, variances, intersection_tracts, intersection_weights):
    xs = groups // CORES
    ys = parts // DEPTH
    rows = estimates.shape[0]
    ages = variances.shape[1]
    rank = factors.shape[1] // ages
    geo = lax.axis_index("geo")
    dist = lax.axis_index("dist")
    x, core = geo // CORES, geo % CORES
    z, y = dist // ys, dist % ys

    def geo_shift(value, dx, dc):
        if dx == 0 and dc == 0:
            return value
        perm = [(a * CORES + b, (a + dx) % xs * CORES + (b + dc) % CORES) for a in range(xs) for b in range(CORES)]
        return lax.ppermute(value, "geo", perm)

    def y_shift(value, dy):
        if dy == 0:
            return value
        perm = [(a * ys + b, a * ys + (b + dy) % ys) for a in range(DEPTH) for b in range(ys)]
        return lax.ppermute(value, "dist", perm)

    def z_send(value, pairs):
        perm = [(a * ys + b, c * ys + b) for a, c in pairs for b in range(ys)]
        return lax.ppermute(value, "dist", perm)

    near = ((0, 1), (1, 0), (2, 3), (3, 2))
    mirror = ((0, 3), (1, 2), (2, 1), (3, 0))
    across = ((0, 2), (1, 3), (2, 0), (3, 1))
    queries = jnp.concatenate([intersection_tracts.T, intersection_weights.T], axis=0)
    in_middle = (z == 1) | (z == 2)
    at_mirror, at_across = z_send(queries, mirror), z_send(queries, across)
    queries = jnp.concatenate(
        [
            queries,
            z_send(queries, near),
            jnp.where(in_middle, at_mirror, at_across),
            jnp.where(in_middle, at_across, at_mirror),
        ],
        axis=1,
    )

    bases = jnp.stack([
        (((x - dx) % xs * CORES + (core - dc) % CORES) * parts + z * ys + (y - dy) % ys) * rows
        for dy in range(ys) for dx in range(xs) for dc in range(CORES)
    ]).astype(jnp.int32)
    w = build_weights(bases, queries, rows)
    flag = ((core == CORES - 1) & (x == xs - 1)).astype(jnp.int32).reshape(1)

    variances = jnp.pad(variances, ((0, 0), (0, -ages % LANES)))
    loads = jnp.concatenate([factors, variances], axis=1)

    def half(array, c):
        total = array.shape[1] // LANES
        width = -(-total // groups) * xs
        return lax.dynamic_slice(array, (0, jnp.where(c == 0, 0, total - width) * LANES), (rows, width * LANES))

    def swap(array):
        return geo_shift(half(array, 1 - core), 0, 1)

    def part(both, group, each, first, count):
        return lax.dynamic_slice(both, (0, (group * each + first) * LANES), (both.shape[0], count * LANES))

    def along_x(both, chunk, *done):
        mine = part(both, x, *chunk)
        others = [geo_shift(after(part(both, (x + dx) % xs, *chunk), *done), dx, 0) for dx in range(1, xs)]
        return [mine] + others

    def along_y(by_x, *done):
        mine = [after(by_x[0], *done)] + by_x[1:]
        return mine + [y_shift(value, dy) for dy in range(1, ys) for value in mine]

    def along_z(data, has_var, *done):
        own, close, far = partial_sums(flag, after(w, *done), data, has_var)
        far_in = z_send(far, ((0, 1), (3, 2)))
        close_in = z_send(close, near)
        to_middle, to_end = middle(far, far_in)
        middle_in = z_send(to_middle, ((1, 2), (2, 1)))
        end_in = z_send(to_end, ((1, 3), (2, 0)))
        return far, own, [close_in, middle_in, end_in]

    def spread(own, others, *done):
        mine = combine(after(own, *done), others)
        along = [geo_shift(mine, dx, 0) for dx in range(xs)]
        return [geo_shift(along[dx], 0, dc) for dx in range(xs) for dc in range(CORES)]

    def places(total):
        each = -(-total // groups)
        starts, uppers = [], []
        for dx in range(xs):
            for dc in range(CORES):
                c, a = (core - dc) % CORES, (x - dx) % xs
                starts.append(jnp.where(c == 0, 0, total - each * xs) + a * each)
                uppers.append(c)
        return jnp.stack(starts + uppers).astype(jnp.int32)

    def split(each):
        return (each // 2, each - each // 2)

    load_total = loads.shape[1] // LANES
    mean_total = estimates.shape[1] // LANES
    load_each, mean_each = -(-load_total // groups), -(-mean_total // groups)
    load_tiles = split(load_each)
    mean_tiles = split(mean_each)[::-1]

    def chunks(each, tiles):
        return [(each, sum(tiles[:i]), count) for i, count in enumerate(tiles)]

    load_chunks, mean_chunks = chunks(load_each, load_tiles), chunks(mean_each, mean_tiles)
    load_both = jnp.concatenate([half(loads, core), swap(loads)], axis=0)
    by_x, by_y, by_z = [], [], []
    for chunk in load_chunks:
        by_x.append(along_x(load_both, chunk, *by_x[-1:], queries))
    mean_both = jnp.concatenate([half(estimates, core), swap(after(estimates, by_x[0]))], axis=0)
    for chunk in mean_chunks:
        by_x.append(along_x(mean_both, chunk, *by_x[-1:]))
    for values in by_x:
        by_y.append(along_y(values, *by_y[-1:]))
    for i, values in enumerate(by_y):
        done = [far for far, _, _ in by_z[-1:]]
        by_z.append(along_z(values, i == len(load_chunks) - 1, *done))
    load_pieces, mean_pieces = [], []
    for _, own, others in by_z[:len(load_chunks)]:
        load_pieces += spread(own, others, *load_pieces[:1])
    cov = covariance(places(load_total), load_pieces, load_tiles, load_total, ages, rank)
    for _, own, others in by_z[len(load_chunks):]:
        mean_pieces += spread(own, others, cov, *mean_pieces[:1])
    mean = marginal(places(mean_total), mean_pieces, mean_tiles, mean_total)
    return mean, cov.T


def solution(mesh):
    return jax.shard_map(
        functools.partial(shards, mesh.shape["geo"], mesh.shape["dist"]),
        mesh=mesh,
        in_specs=(
            P(("geo", "dist"), None),
            P(("geo", "dist"), None),
            P(("geo", "dist"), None),
            P("dist", None),
            P("dist", None),
        ),
        out_specs=(P("dist", None), P("dist", None)),
        check_vma=False,
    )
```

```python
import functools
import jax
import jax.numpy as jnp
from jax import lax
from jax.experimental import pallas as pl
from jax.experimental.pallas import tpu as pltpu
from jax.sharding import PartitionSpec as P

LANES = 128
CORES = 2
DEPTH = 4
LOAD_FIRST = 5
MEAN_FIRST = 10
SCALES = 16
TOP = 32767.0
VMEM_BYTES = 48 * 1024 * 1024
BEFORE = (((0,), (0,)), ((), ()))
AFTER = (((1,), (1,)), ((), ()))


def params():
    return pltpu.CompilerParams(vmem_limit_bytes=VMEM_BYTES)


def cost(flops, moved):
    return pl.CostEstimate(flops=flops, bytes_accessed=moved, transcendentals=0)


def after(value, *others):
    return lax.optimization_barrier((value, *others))[0]


def split(each, first):
    first = each // 2 if first >= each else first
    return (first, each - first)


def twice(value):
    return jnp.concatenate([value, value], axis=0)


def encode(src, src_base, dst, dst_base, height):
    half = height // 2
    powers = []
    for h in range(2):
        top = jnp.abs(src[pl.ds(src_base + h * half, 8), :])
        for r in range(8, half, 8):
            top = jnp.maximum(top, jnp.abs(src[pl.ds(src_base + h * half + r, 8), :]))
        power = jnp.floor(jnp.log2(jnp.maximum(top, 1e-30))) + 1.0
        gain = twice(jnp.exp2(-power) * TOP)
        for r in range(h * half, (h + 1) * half, 16):
            level = jnp.clip(jnp.round(src[pl.ds(src_base + r, 16), :] * gain), -TOP, TOP)
            dst[pl.ds(dst_base + r, 16), :] = level.astype(jnp.int32).astype(jnp.int16)
        powers.append(power)
    both = jnp.concatenate(powers, axis=0)
    dst[pl.ds(dst_base + height, SCALES), :] = both.astype(jnp.int32).astype(jnp.int16)


def steps_of(coded, base, height):
    power = coded[pl.ds(base + height, SCALES), :].astype(jnp.int32).astype(jnp.float32)
    step = jnp.exp2(power) * (1.0 / TOP)
    return [twice(step[:8]), twice(step[8:])]


def decode(coded, row, step):
    return coded[pl.ds(row, 16), :].astype(jnp.int32).astype(jnp.float32) * step


def weights_kernel(rows, base_ref, query_ref, out_ref):
    each = query_ref.shape[0] // 2
    row_id = lax.broadcasted_iota(jnp.int32, (16, LANES), 0)

    def piece(j, carry):
        for u in range(DEPTH):
            lanes = slice(u * LANES, (u + 1) * LANES)
            for r in range(0, rows, 16):
                tract = row_id + (base_ref[j] + r)
                total = jnp.zeros((16, LANES), jnp.float32)
                for k in range(each):
                    share = query_ref[each + k:each + k + 1, lanes].astype(jnp.float32) * (1.0 / 256.0)
                    total = jnp.where(query_ref[k:k + 1, lanes] == tract, share, total)
                where = pl.ds(pl.multiple_of(j * rows + r, 16), 16)
                out_ref[where, lanes] = total.astype(jnp.bfloat16)
        return carry

    lax.fori_loop(0, out_ref.shape[0] // rows, piece, 0)


def build_weights(bases, queries, rows):
    pieces = bases.shape[0]
    width = queries.shape[1]
    shape = (pieces * rows, width)
    return pl.pallas_call(
        functools.partial(weights_kernel, rows),
        grid_spec=pltpu.PrefetchScalarGridSpec(
            num_scalar_prefetch=1,
            grid=(1,),
            in_specs=[pl.BlockSpec(queries.shape, lambda i, s: (0, 0))],
            out_specs=pl.BlockSpec(shape, lambda i, s: (0, 0)),
        ),
        out_shape=jax.ShapeDtypeStruct(shape, jnp.bfloat16),
        compiler_params=params(),
        cost_estimate=cost(shape[0] * width * queries.shape[0] * 200, shape[0] * width * 2),
        name="build_weights",
    )(bases, queries)


def sums_kernel(parts, has_var, flag_ref, w_ref, *refs):
    data = refs[:parts]
    own_ref, near_ref, far_ref, acc_ref = refs[parts:]
    depth, columns = data[0].shape
    coded = columns + SCALES

    def weighted(get, t):
        total = None
        for j in range(parts):
            part = lax.dot_general(
                data[j][:, t * LANES:(t + 1) * LANES],
                get(w_ref[j * depth:(j + 1) * depth, :]),
                BEFORE,
                preferred_element_type=jnp.float32,
            )
            total = part if total is None else total + part
        return total

    def put(t, value):
        where = slice(t * LANES, (t + 1) * LANES)
        own_ref[where, :] = value[:, :LANES]
        for u in range(1, DEPTH):
            acc_ref[u - 1, where, :] = value[:, u * LANES:(u + 1) * LANES]

    for t in range(columns // LANES):
        put(t, weighted(lambda w: w, t))

    if has_var:
        @pl.when(flag_ref[0] == 1)
        def _():
            def square(w):
                wide = w.astype(jnp.float32)
                return wide * wide

            def high(w):
                return square(w).astype(jnp.bfloat16)

            def low(w):
                s = square(w)
                return (s - s.astype(jnp.bfloat16).astype(jnp.float32)).astype(jnp.bfloat16)

            t = columns // LANES - 1
            put(t, weighted(high, t) + weighted(low, t))

    encode(acc_ref.at[0], 0, near_ref, 0, columns)
    encode(acc_ref.at[1], 0, far_ref, 0, columns)
    encode(acc_ref.at[2], 0, far_ref, coded, columns)


def partial_sums(flag, w, data, has_var):
    depth, columns = data[0].shape
    parts = len(data)
    coded = columns + SCALES
    whole = lambda i, s: (0, 0)
    shapes = [
        jax.ShapeDtypeStruct((columns, LANES), jnp.float32),
        jax.ShapeDtypeStruct((coded, LANES), jnp.int16),
        jax.ShapeDtypeStruct((2 * coded, LANES), jnp.int16),
    ]
    return pl.pallas_call(
        functools.partial(sums_kernel, parts, has_var),
        grid_spec=pltpu.PrefetchScalarGridSpec(
            num_scalar_prefetch=1,
            grid=(1,),
            in_specs=[pl.BlockSpec(w.shape, whole)] + [pl.BlockSpec((depth, columns), whole)] * parts,
            out_specs=[pl.BlockSpec(s.shape, whole) for s in shapes],
            scratch_shapes=[pltpu.VMEM((DEPTH - 1, columns, LANES), jnp.float32)],
        ),
        out_shape=shapes,
        compiler_params=params(),
        cost_estimate=cost(2 * w.shape[0] * w.shape[1] * columns, 2 * depth * parts * columns + columns * LANES * 10),
        name="partial_sums",
    )(flag, w, *data)


def middle_kernel(own_ref, other_ref, near_ref, end_ref, acc_ref):
    height = acc_ref.shape[0]
    for u, out in enumerate((near_ref, end_ref)):
        base = u * (height + SCALES)
        mine = steps_of(own_ref, base, height)
        theirs = steps_of(other_ref, base, height)
        for r in range(0, height, 16):
            h = r * 2 // height
            acc_ref[r:r + 16, :] = decode(own_ref, base + r, mine[h]) + decode(other_ref, base + r, theirs[h])
        encode(acc_ref, 0, out, 0, height)


def middle(own, other):
    coded = own.shape[0] // 2
    shape = jax.ShapeDtypeStruct((coded, LANES), jnp.int16)
    return pl.pallas_call(
        middle_kernel,
        out_shape=[shape, shape],
        scratch_shapes=[pltpu.VMEM((coded - SCALES, LANES), jnp.float32)],
        compiler_params=params(),
        cost_estimate=cost(coded * LANES * 32, coded * LANES * 12),
        name="middle",
    )(own, other)


def combine_kernel(own_ref, *refs):
    others, out_ref, acc_ref = refs[:-2], refs[-2], refs[-1]
    height = acc_ref.shape[0]
    steps = [steps_of(o, 0, height) for o in others]
    for r in range(0, height, 16):
        total = own_ref[r:r + 16, :]
        for o, step in zip(others, steps):
            total = total + decode(o, r, step[r * 2 // height])
        acc_ref[r:r + 16, :] = total
    encode(acc_ref, 0, out_ref, 0, height)


def combine(own, others):
    height = own.shape[0]
    shape = (height + SCALES, LANES)
    return pl.pallas_call(
        combine_kernel,
        out_shape=jax.ShapeDtypeStruct(shape, jnp.int16),
        scratch_shapes=[pltpu.VMEM((height, LANES), jnp.float32)],
        compiler_params=params(),
        cost_estimate=cost(height * LANES * 16, height * LANES * 12),
        name="combine",
    )(own, *others)


def each_piece(place_ref, pieces, tiles, do):
    groups = place_ref.shape[0] // 2
    for upper in (1, 0):
        for r in range(groups):
            @pl.when(place_ref[groups + r] == upper)
            def _(r=r):
                first = 0
                for c, count in enumerate(tiles):
                    do((place_ref[r] + first) * LANES, pieces[c * groups + r], count * LANES)
                    first += count


def marginal_kernel(tiles, place_ref, *refs):
    pieces, out_ref, tile_ref = refs[:-2], refs[-2], refs[-1]

    def do(start, piece, height):
        steps = steps_of(piece, 0, height)
        for t in range(0, height, LANES):
            for r in range(0, LANES, 16):
                tile_ref[r:r + 16, :] = decode(piece, t + r, steps[(t + r) * 2 // height])
            out_ref[:, pl.ds(pl.multiple_of(start + t, LANES), LANES)] = tile_ref[...].T

    each_piece(place_ref, pieces, tiles, do)


def marginal(places, pieces, tiles, total):
    shape = (LANES, total * LANES)
    return pl.pallas_call(
        functools.partial(marginal_kernel, tiles),
        grid_spec=pltpu.PrefetchScalarGridSpec(
            num_scalar_prefetch=1,
            grid=(1,),
            in_specs=[pl.BlockSpec(p.shape, lambda i, s: (0, 0)) for p in pieces],
            out_specs=pl.BlockSpec(shape, lambda i, s: (0, 0)),
            scratch_shapes=[pltpu.VMEM((LANES, LANES), jnp.float32)],
        ),
        out_shape=jax.ShapeDtypeStruct(shape, jnp.float32),
        compiler_params=params(),
        cost_estimate=cost(shape[0] * shape[1] * 4, shape[0] * shape[1] * 6),
        name="marginal",
    )(places, *pieces)


def covariance_kernel(tiles, total, ages, rank, place_ref, *refs):
    pieces, out_ref = refs[:-4], refs[-4]
    load_ref, age_ref, cov_ref = refs[-3:]
    pitch = -(-ages // 8) * 8
    left = lax.broadcasted_iota(jnp.int32, (LANES, LANES), 1) < rank

    def do(start, piece, height):
        steps = steps_of(piece, 0, height)
        for r in range(0, height, 16):
            load_ref[pl.ds(pl.multiple_of(start + r, 16), 16), :] = decode(piece, r, steps[r * 2 // height])

    each_piece(place_ref, pieces, tiles, do)

    def turn(t, carry):
        tile = t + t // (total // CORES - 1)
        value = load_ref[pl.ds(pl.multiple_of(tile * LANES, LANES), LANES), :].T
        swapped = pltpu.roll(value, rank, 1)
        age_ref[pl.ds(2 * t, LANES, stride=pitch), :] = jnp.where(left, value, swapped)
        age_ref[pl.ds(2 * t + 1, LANES, stride=pitch), :] = jnp.where(left, swapped, value)
        return carry

    lax.fori_loop(0, ages * rank // LANES, turn, 0, unroll=True)

    def outer(d, carry):
        start = pl.multiple_of(d * pitch, 8)
        mine = age_ref[pl.ds(start, LANES), :]
        high = mine.astype(jnp.bfloat16).astype(jnp.float32)
        low = mine - high
        mixed = jnp.where(left, high, low).astype(jnp.bfloat16)
        product = lax.dot_general(
            jnp.concatenate([mixed, mixed], axis=1),
            jnp.concatenate([high.astype(jnp.bfloat16), low.astype(jnp.bfloat16)], axis=1),
            AFTER,
            preferred_element_type=jnp.float32,
        )
        cov_ref[pl.ds(start, pitch), :] = product[:pitch]
        return carry

    lax.fori_loop(0, LANES, outer, 0, unroll=16)

    def store(m, carry):
        base = pl.multiple_of(m * (2 * ages), 8)
        for p in range(2):
            value = cov_ref[pl.ds(2 * m + p, LANES, stride=pitch), :].T
            out_ref[pl.ds(base + p * ages, ages), :] = value[:ages]
        return carry

    lax.fori_loop(0, ages // 2, store, 0, unroll=True)
    for i in range(ages):
        row = i * (ages + 1)
        out_ref[row:row + 1, :] += load_ref[(total - 1) * LANES + i:(total - 1) * LANES + i + 1, :]


def covariance(places, pieces, tiles, total, ages, rank):
    pitch = -(-ages // 8) * 8
    shape = (ages * ages, LANES)
    tall = (LANES * pitch + LANES - pitch, LANES)
    return pl.pallas_call(
        functools.partial(covariance_kernel, tiles, total, ages, rank),
        grid_spec=pltpu.PrefetchScalarGridSpec(
            num_scalar_prefetch=1,
            grid=(1,),
            in_specs=[pl.BlockSpec(p.shape, lambda i, s: (0, 0)) for p in pieces],
            out_specs=pl.BlockSpec(shape, lambda i, s: (0, 0)),
            scratch_shapes=[
                pltpu.VMEM((total * LANES, LANES), jnp.float32),
                pltpu.VMEM(tall, jnp.float32),
                pltpu.VMEM(tall, jnp.float32),
            ],
        ),
        out_shape=jax.ShapeDtypeStruct(shape, jnp.float32),
        compiler_params=params(),
        cost_estimate=cost(LANES * ages * ages * rank * 140, shape[0] * shape[1] * 4),
        name="covariance",
    )(places, *pieces)


def shards(groups, parts, estimates, factors, variances, intersection_tracts, intersection_weights):
    xs = groups // CORES
    ys = parts // DEPTH
    rows = estimates.shape[0]
    ages = variances.shape[1]
    rank = factors.shape[1] // ages
    geo = lax.axis_index("geo")
    dist = lax.axis_index("dist")
    x, core = geo // CORES, geo % CORES
    z, y = dist // ys, dist % ys

    def geo_shift(value, dx, dc):
        if dx == 0 and dc == 0:
            return value
        perm = [(a * CORES + b, (a + dx) % xs * CORES + (b + dc) % CORES) for a in range(xs) for b in range(CORES)]
        return lax.ppermute(value, "geo", perm)

    def y_shift(value, dy):
        if dy == 0:
            return value
        perm = [(a * ys + b, a * ys + (b + dy) % ys) for a in range(DEPTH) for b in range(ys)]
        return lax.ppermute(value, "dist", perm)

    def z_send(value, pairs):
        perm = [(a * ys + b, c * ys + b) for a, c in pairs for b in range(ys)]
        return lax.ppermute(value, "dist", perm)

    near = ((0, 1), (1, 0), (2, 3), (3, 2))
    mirror = ((0, 3), (1, 2), (2, 1), (3, 0))
    across = ((0, 2), (1, 3), (2, 0), (3, 1))
    queries = jnp.concatenate([intersection_tracts.T, intersection_weights.T], axis=0)
    in_middle = (z == 1) | (z == 2)
    at_mirror, at_across = z_send(queries, mirror), z_send(queries, across)
    queries = jnp.concatenate(
        [
            queries,
            z_send(queries, near),
            jnp.where(in_middle, at_mirror, at_across),
            jnp.where(in_middle, at_across, at_mirror),
        ],
        axis=1,
    )

    bases = jnp.stack([
        (((x - dx) % xs * CORES + (core - dc) % CORES) * parts + z * ys + (y - dy) % ys) * rows
        for dy in range(ys) for dx in range(xs) for dc in range(CORES)
    ]).astype(jnp.int32)
    w = build_weights(bases, queries, rows)
    flag = (x == xs - 1).astype(jnp.int32).reshape(1)
    last_tile = jnp.pad(variances, ((0, 0), (0, -ages % LANES)))

    def half(array, c, *more):
        width = array.shape[1] // CORES
        return jnp.concatenate([lax.dynamic_slice(array, (0, c * width), (rows, width)), *more], axis=1)

    def exchange(array, *more):
        return jnp.concatenate(
            [half(array, core, *more), geo_shift(half(array, 1 - core, *more), 0, 1)], axis=0
        )

    def start_of(group, tiles):
        return jnp.minimum(group * each_of(tiles), tiles - each_of(tiles))

    def each_of(tiles):
        return -(-tiles // xs)

    def along_x(both, first, count, *done):
        def part(group):
            start = (start_of(group, both.shape[1] // LANES) + first) * LANES
            return lax.dynamic_slice(both, (0, start), (both.shape[0], count * LANES))

        others = [geo_shift(after(part((x + dx) % xs), *done), dx, 0) for dx in range(1, xs)]
        return [part(x)] + others

    def along_y(by_x, *done):
        if done:
            by_x = [after(value, other) for value, other in zip(by_x, done)]
        return by_x + [y_shift(value, dy) for dy in range(1, ys) for value in by_x]

    def along_z(data, has_var, before_sums, before_middle):
        own, close, far = partial_sums(flag, after(w, *before_sums), data, has_var)
        far_in = z_send(far, ((0, 1), (3, 2)))
        close_in = z_send(close, near)
        to_middle, to_end = middle(after(far, *before_middle), far_in)
        middle_in = z_send(to_middle, ((1, 2), (2, 1)))
        end_in = z_send(to_end, ((1, 3), (2, 0)))
        return (far, to_end), own, [close_in, middle_in, end_in]

    def spread(own, others, *done):
        mine = combine(after(own, *done), others)
        along = [geo_shift(mine, dx, 0) for dx in range(xs)]
        return [geo_shift(along[dx], 0, dc) for dx in range(xs) for dc in range(CORES)]

    def places(tiles):
        starts, lasts = [], []
        for dx in range(xs):
            for dc in range(CORES):
                group = (x - dx) % xs
                starts.append((core - dc) % CORES * tiles + start_of(group, tiles))
                lasts.append(group == xs - 1)
        return jnp.stack(starts + lasts).astype(jnp.int32)

    mean_width = estimates.shape[1] // LANES // CORES
    load_width = factors.shape[1] // LANES // CORES + 1
    load_tiles = split(each_of(load_width), LOAD_FIRST)
    mean_tiles = split(each_of(mean_width), MEAN_FIRST)
    by_x, by_y, by_z = [], [], []

    def feed(both, tiles):
        for i, count in enumerate(tiles):
            by_x.append(along_x(both, sum(tiles[:i]), count, *[values[-1] for values in by_x[-1:]]))

    feed(exchange(factors, last_tile), load_tiles)
    feed(exchange(after(estimates, w)), mean_tiles)
    for values in by_x:
        by_y.append(along_y(values, *[done for done in by_y[-1][-xs:]] if by_y else []))
    count = len(by_y)
    for i, values in enumerate(by_y):
        before_sums = [other[-1] for other in by_x[i + 1:i + 2]]
        if by_z:
            far, to_end = by_z[-1][0]
            before_sums.append(far if i == count - 1 else to_end)
        before_middle = [other[xs] for other in by_y[i + 1:i + 2]] + [other[-1] for other in by_y[i + 1:i + 2] if i == count - 2]
        by_z.append(along_z(values, i == len(load_tiles) - 1, before_sums, before_middle))
    load_pieces, mean_pieces = [], []
    for i, (_, own, others) in enumerate(by_z[:len(load_tiles)]):
        moved = [other[-1] for other in by_y[i + 1:i + 2]] + [other[-1] for other in by_y[i + 2:i + 3] if i > 0]
        load_pieces += spread(own, others, *moved, *load_pieces[-1:])
    load_pieces[0] = after(load_pieces[0], by_z[-1][0][1])
    cov = covariance(places(load_width), load_pieces, load_tiles, load_width * CORES, ages, rank)
    for _, own, others in by_z[len(load_tiles):]:
        mean_pieces += spread(own, others, cov, *by_z[-1][2])
    mean = marginal(places(mean_width), mean_pieces, mean_tiles, mean_width * CORES)
    return mean, cov.T


def solution(mesh):
    return jax.shard_map(
        functools.partial(shards, mesh.shape["geo"], mesh.shape["dist"]),
        mesh=mesh,
        in_specs=(
            P(("geo", "dist"), None),
            P(("geo", "dist"), None),
            P(("geo", "dist"), None),
            P("dist", None),
            P("dist", None),
        ),
        out_specs=(P("dist", None), P("dist", None)),
        check_vma=False,
    )
```

```python
import functools
import jax
import jax.numpy as jnp
from jax import lax
from jax.experimental import pallas as pl
from jax.experimental.pallas import tpu as pltpu
from jax.sharding import PartitionSpec as P

LANES = 128
CORES = 2
DEPTH = 4
LOAD_FIRST = 8
MEAN_FIRST = 10
SCALES = 16
TOP = 32767.0
VMEM_BYTES = 48 * 1024 * 1024
BEFORE = (((0,), (0,)), ((), ()))
AFTER = (((1,), (1,)), ((), ()))


def params():
    return pltpu.CompilerParams(vmem_limit_bytes=VMEM_BYTES)


def cost(flops, moved):
    return pl.CostEstimate(flops=flops // 64, bytes_accessed=moved // 64, transcendentals=0)


def after(value, *others):
    return lax.optimization_barrier((value, *others))[0]


def split(each, first):
    first = each // 2 if first >= each else first
    return (first, each - first)


def twice(value):
    return jnp.concatenate([value, value], axis=0)


def encode(src, src_base, dst, dst_base, height):
    half = height // 2
    powers = []
    for h in range(2):
        top = jnp.abs(src[pl.ds(src_base + h * half, 8), :])
        for r in range(8, half, 8):
            top = jnp.maximum(top, jnp.abs(src[pl.ds(src_base + h * half + r, 8), :]))
        power = jnp.floor(jnp.log2(jnp.maximum(top, 1e-30))) + 1.0
        gain = twice(jnp.exp2(-power) * TOP)
        for r in range(h * half, (h + 1) * half, 16):
            level = jnp.clip(jnp.round(src[pl.ds(src_base + r, 16), :] * gain), -TOP, TOP)
            dst[pl.ds(dst_base + r, 16), :] = level.astype(jnp.int32).astype(jnp.int16)
        powers.append(power)
    both = jnp.concatenate(powers, axis=0)
    dst[pl.ds(dst_base + height, SCALES), :] = both.astype(jnp.int32).astype(jnp.int16)


def steps_of(coded, base, height):
    power = coded[pl.ds(base + height, SCALES), :].astype(jnp.int32).astype(jnp.float32)
    step = jnp.exp2(power) * (1.0 / TOP)
    return [twice(step[:8]), twice(step[8:])]


def decode(coded, row, step):
    return coded[pl.ds(row, 16), :].astype(jnp.int32).astype(jnp.float32) * step


def weights_kernel(rows, base_ref, query_ref, out_ref):
    each = query_ref.shape[0] // 2
    row_id = lax.broadcasted_iota(jnp.int32, (16, LANES), 0)

    def piece(j, carry):
        for u in range(DEPTH):
            lanes = slice(u * LANES, (u + 1) * LANES)
            for r in range(0, rows, 16):
                tract = row_id + (base_ref[j] + r)
                total = jnp.zeros((16, LANES), jnp.float32)
                for k in range(each):
                    share = query_ref[each + k:each + k + 1, lanes].astype(jnp.float32) * (1.0 / 256.0)
                    total = jnp.where(query_ref[k:k + 1, lanes] == tract, share, total)
                where = pl.ds(pl.multiple_of(j * rows + r, 16), 16)
                out_ref[where, lanes] = total.astype(jnp.bfloat16)
        return carry

    lax.fori_loop(0, out_ref.shape[0] // rows, piece, 0)


def build_weights(bases, queries, rows):
    pieces = bases.shape[0]
    width = queries.shape[1]
    shape = (pieces * rows, width)
    return pl.pallas_call(
        functools.partial(weights_kernel, rows),
        grid_spec=pltpu.PrefetchScalarGridSpec(
            num_scalar_prefetch=1,
            grid=(1,),
            in_specs=[pl.BlockSpec(queries.shape, lambda i, s: (0, 0))],
            out_specs=pl.BlockSpec(shape, lambda i, s: (0, 0)),
        ),
        out_shape=jax.ShapeDtypeStruct(shape, jnp.bfloat16),
        compiler_params=params(),
        cost_estimate=cost(shape[0] * width * queries.shape[0], shape[0] * width * 2),
        name="build_weights",
    )(bases, queries)


def sums_kernel(offsets, has_var, flag_ref, w_ref, *refs):
    parts = len(offsets)
    data = refs[:parts]
    own_ref, near_ref, far_ref, acc_ref = refs[parts:]
    columns = own_ref.shape[0]
    coded = columns + SCALES
    rows = [0]
    for d in data:
        rows.append(rows[-1] + d.shape[0])

    def weighted(get, t):
        total = None
        for j in range(parts):
            part = lax.dot_general(
                data[j][:, (offsets[j] + t) * LANES:(offsets[j] + t + 1) * LANES],
                get(w_ref[rows[j]:rows[j + 1], :]),
                BEFORE,
                preferred_element_type=jnp.float32,
            )
            total = part if total is None else total + part
        return total

    def put(t, value):
        where = slice(t * LANES, (t + 1) * LANES)
        own_ref[where, :] = value[:, :LANES]
        for u in range(1, DEPTH):
            acc_ref[u - 1, where, :] = value[:, u * LANES:(u + 1) * LANES]

    for t in range(columns // LANES):
        put(t, weighted(lambda w: w, t))

    if has_var:
        @pl.when(flag_ref[0] == 1)
        def _():
            def square(w):
                wide = w.astype(jnp.float32)
                return wide * wide

            def high(w):
                return square(w).astype(jnp.bfloat16)

            def low(w):
                s = square(w)
                return (s - s.astype(jnp.bfloat16).astype(jnp.float32)).astype(jnp.bfloat16)

            t = columns // LANES - 1
            put(t, weighted(high, t) + weighted(low, t))

    encode(acc_ref.at[0], 0, near_ref, 0, columns)
    encode(acc_ref.at[1], 0, far_ref, 0, columns)
    encode(acc_ref.at[2], 0, far_ref, coded, columns)


def partial_sums(flag, w, data, count, has_var):
    columns = count * LANES
    offsets = tuple(first for _, first in data)
    data = [array for array, _ in data]
    coded = columns + SCALES
    whole = lambda i, s: (0, 0)
    shapes = [
        jax.ShapeDtypeStruct((columns, LANES), jnp.float32),
        jax.ShapeDtypeStruct((coded, LANES), jnp.int16),
        jax.ShapeDtypeStruct((2 * coded, LANES), jnp.int16),
    ]
    return pl.pallas_call(
        functools.partial(sums_kernel, offsets, has_var),
        grid_spec=pltpu.PrefetchScalarGridSpec(
            num_scalar_prefetch=1,
            grid=(1,),
            in_specs=[pl.BlockSpec(w.shape, whole)] + [pl.BlockSpec(d.shape, whole) for d in data],
            out_specs=[pl.BlockSpec(s.shape, whole) for s in shapes],
            scratch_shapes=[pltpu.VMEM((DEPTH - 1, columns, LANES), jnp.float32)],
        ),
        out_shape=shapes,
        compiler_params=params(),
        cost_estimate=cost(2 * w.shape[0] * w.shape[1] * columns, 2 * w.shape[0] * columns + columns * LANES * 10),
        name="partial_sums",
    )(flag, w, *data)


def middle_kernel(own_ref, other_ref, near_ref, end_ref, acc_ref):
    height = acc_ref.shape[0]
    for u, out in enumerate((near_ref, end_ref)):
        base = u * (height + SCALES)
        mine = steps_of(own_ref, base, height)
        theirs = steps_of(other_ref, base, height)
        for r in range(0, height, 16):
            h = r * 2 // height
            acc_ref[r:r + 16, :] = decode(own_ref, base + r, mine[h]) + decode(other_ref, base + r, theirs[h])
        encode(acc_ref, 0, out, 0, height)


def middle(own, other):
    coded = own.shape[0] // 2
    shape = jax.ShapeDtypeStruct((coded, LANES), jnp.int16)
    return pl.pallas_call(
        middle_kernel,
        out_shape=[shape, shape],
        scratch_shapes=[pltpu.VMEM((coded - SCALES, LANES), jnp.float32)],
        compiler_params=params(),
        cost_estimate=cost(coded * LANES * 32, coded * LANES * 12),
        name="middle",
    )(own, other)


def combine_kernel(own_ref, *refs):
    others, out_ref, acc_ref = refs[:-2], refs[-2], refs[-1]
    height = acc_ref.shape[0]
    steps = [steps_of(o, 0, height) for o in others]
    for r in range(0, height, 16):
        total = own_ref[r:r + 16, :]
        for o, step in zip(others, steps):
            total = total + decode(o, r, step[r * 2 // height])
        acc_ref[r:r + 16, :] = total
    encode(acc_ref, 0, out_ref, 0, height)


def combine(own, others):
    height = own.shape[0]
    shape = (height + SCALES, LANES)
    return pl.pallas_call(
        combine_kernel,
        out_shape=jax.ShapeDtypeStruct(shape, jnp.int16),
        scratch_shapes=[pltpu.VMEM((height, LANES), jnp.float32)],
        compiler_params=params(),
        cost_estimate=cost(height * LANES * 16, height * LANES * 12),
        name="combine",
    )(own, *others)


def each_piece(place_ref, pieces, tiles, do):
    groups = place_ref.shape[0] // 2
    for upper in (1, 0):
        for r in range(groups):
            @pl.when(place_ref[groups + r] == upper)
            def _(r=r):
                first = 0
                for c, count in enumerate(tiles):
                    do((place_ref[r] + first) * LANES, pieces[c * groups + r], count * LANES)
                    first += count


def marginal_kernel(tiles, place_ref, *refs):
    pieces, out_ref, tile_ref = refs[:-2], refs[-2], refs[-1]

    def do(start, piece, height):
        steps = steps_of(piece, 0, height)
        for t in range(0, height, LANES):
            for r in range(0, LANES, 16):
                tile_ref[r:r + 16, :] = decode(piece, t + r, steps[(t + r) * 2 // height])
            out_ref[:, pl.ds(pl.multiple_of(start + t, LANES), LANES)] = tile_ref[...].T

    each_piece(place_ref, pieces, tiles, do)


def marginal(places, pieces, tiles, total):
    shape = (LANES, total * LANES)
    return pl.pallas_call(
        functools.partial(marginal_kernel, tiles),
        grid_spec=pltpu.PrefetchScalarGridSpec(
            num_scalar_prefetch=1,
            grid=(1,),
            in_specs=[pl.BlockSpec(p.shape, lambda i, s: (0, 0)) for p in pieces],
            out_specs=pl.BlockSpec(shape, lambda i, s: (0, 0)),
            scratch_shapes=[pltpu.VMEM((LANES, LANES), jnp.float32)],
        ),
        out_shape=jax.ShapeDtypeStruct(shape, jnp.float32),
        compiler_params=params(),
        cost_estimate=cost(shape[0] * shape[1] * 4, shape[0] * shape[1] * 6),
        name="marginal",
    )(places, *pieces)


def covariance_kernel(tiles, total, ages, rank, place_ref, *refs):
    pieces, out_ref = refs[:-4], refs[-4]
    load_ref, age_ref, cov_ref = refs[-3:]
    pitch = -(-ages // 8) * 8
    left = lax.broadcasted_iota(jnp.int32, (LANES, LANES), 1) < rank

    def do(start, piece, height):
        steps = steps_of(piece, 0, height)
        for r in range(0, height, 16):
            load_ref[pl.ds(pl.multiple_of(start + r, 16), 16), :] = decode(piece, r, steps[r * 2 // height])

    each_piece(place_ref, pieces, tiles, do)

    def turn(t, carry):
        tile = t + t // (total // CORES - 1)
        value = load_ref[pl.ds(pl.multiple_of(tile * LANES, LANES), LANES), :].T
        swapped = pltpu.roll(value, rank, 1)
        age_ref[pl.ds(2 * t, LANES, stride=pitch), :] = jnp.where(left, value, swapped)
        age_ref[pl.ds(2 * t + 1, LANES, stride=pitch), :] = jnp.where(left, swapped, value)
        return carry

    lax.fori_loop(0, ages * rank // LANES, turn, 0, unroll=True)

    def outer(d, carry):
        start = pl.multiple_of(d * pitch, 8)
        mine = age_ref[pl.ds(start, LANES), :]
        high = mine.astype(jnp.bfloat16).astype(jnp.float32)
        low = mine - high
        mixed = jnp.where(left, high, low).astype(jnp.bfloat16)
        product = lax.dot_general(
            jnp.concatenate([mixed, mixed], axis=1),
            jnp.concatenate([high.astype(jnp.bfloat16), low.astype(jnp.bfloat16)], axis=1),
            AFTER,
            preferred_element_type=jnp.float32,
        )
        cov_ref[pl.ds(start, pitch), :] = product[:pitch]
        return carry

    lax.fori_loop(0, LANES, outer, 0, unroll=16)

    def store(m, carry):
        base = pl.multiple_of(m * (2 * ages), 8)
        for p in range(2):
            value = cov_ref[pl.ds(2 * m + p, LANES, stride=pitch), :].T
            out_ref[pl.ds(base + p * ages, ages), :] = value[:ages]
        return carry

    lax.fori_loop(0, ages // 2, store, 0, unroll=True)
    for i in range(ages):
        row = i * (ages + 1)
        out_ref[row:row + 1, :] += load_ref[(total - 1) * LANES + i:(total - 1) * LANES + i + 1, :]


def covariance(places, pieces, tiles, total, ages, rank):
    pitch = -(-ages // 8) * 8
    shape = (ages * ages, LANES)
    tall = (LANES * pitch + LANES - pitch, LANES)
    return pl.pallas_call(
        functools.partial(covariance_kernel, tiles, total, ages, rank),
        grid_spec=pltpu.PrefetchScalarGridSpec(
            num_scalar_prefetch=1,
            grid=(1,),
            in_specs=[pl.BlockSpec(p.shape, lambda i, s: (0, 0)) for p in pieces],
            out_specs=pl.BlockSpec(shape, lambda i, s: (0, 0)),
            scratch_shapes=[
                pltpu.VMEM((total * LANES, LANES), jnp.float32),
                pltpu.VMEM(tall, jnp.float32),
                pltpu.VMEM(tall, jnp.float32),
            ],
        ),
        out_shape=jax.ShapeDtypeStruct(shape, jnp.float32),
        compiler_params=params(),
        cost_estimate=cost(LANES * ages * ages * rank * 2, shape[0] * shape[1] * 4),
        name="covariance",
    )(places, *pieces)


def shards(groups, parts, estimates, factors, variances, intersection_tracts, intersection_weights):
    xs = groups // CORES
    ys = parts // DEPTH
    rows = estimates.shape[0]
    ages = variances.shape[1]
    rank = factors.shape[1] // ages
    geo = lax.axis_index("geo")
    dist = lax.axis_index("dist")
    x, core = geo // CORES, geo % CORES
    z, y = dist // ys, dist % ys

    def geo_shift(value, dx, dc):
        if dx == 0 and dc == 0:
            return value
        perm = [(a * CORES + b, (a + dx) % xs * CORES + (b + dc) % CORES) for a in range(xs) for b in range(CORES)]
        return lax.ppermute(value, "geo", perm)

    def y_shift(value, dy):
        if dy == 0:
            return value
        perm = [(a * ys + b, a * ys + (b + dy) % ys) for a in range(DEPTH) for b in range(ys)]
        return lax.ppermute(value, "dist", perm)

    def z_send(value, pairs):
        perm = [(a * ys + b, c * ys + b) for a, c in pairs for b in range(ys)]
        return lax.ppermute(value, "dist", perm)

    near = ((0, 1), (1, 0), (2, 3), (3, 2))
    mirror = ((0, 3), (1, 2), (2, 1), (3, 0))
    across = ((0, 2), (1, 3), (2, 0), (3, 1))
    queries = jnp.concatenate([intersection_tracts.T, intersection_weights.T], axis=0)
    in_middle = (z == 1) | (z == 2)
    at_mirror, at_across = z_send(queries, mirror), z_send(queries, across)
    queries = jnp.concatenate(
        [
            queries,
            z_send(queries, near),
            jnp.where(in_middle, at_mirror, at_across),
            jnp.where(in_middle, at_across, at_mirror),
        ],
        axis=1,
    )

    bases = jnp.stack([
        (((x - dx) % xs * CORES + (core - dc) % CORES) * parts + z * ys + (y - dy) % ys) * rows
        for dy in range(ys) for dx in range(xs) for dc in range(CORES)
    ]).astype(jnp.int32)
    w = build_weights(bases, queries, rows)
    flag = (x == xs - 1).astype(jnp.int32).reshape(1)
    last_tile = jnp.pad(variances, ((0, 0), (0, -ages % LANES)))

    def half(array, c, *more):
        width = array.shape[1] // CORES
        return jnp.concatenate([lax.dynamic_slice(array, (0, c * width), (rows, width)), *more], axis=1)

    def exchange(array, *more):
        return half(array, core, *more), geo_shift(half(array, 1 - core, *more), 0, 1)

    def start_of(group, tiles):
        return jnp.minimum(group * each_of(tiles), tiles - each_of(tiles))

    def each_of(tiles):
        return -(-tiles // xs)

    def part(value, group):
        tiles = value.shape[1] // LANES
        return lax.dynamic_slice(value, (0, start_of(group, tiles) * LANES), (rows, each_of(tiles) * LANES))

    def along_x(both):
        return [[geo_shift(part(b, (x + dx) % xs), dx, 0) for b in both] for dx in range(xs)]

    def joined(pieces, first, count):
        return jnp.concatenate([p[:, first * LANES:(first + count) * LANES] for p in pieces], axis=0)

    def along_y(pieces, *done):
        sent = [after(value, *done) for value in pieces]
        return [[(value, 0) for value in pieces]] + [[(y_shift(value, dy), 0) for value in sent] for dy in range(1, ys)]

    def later(by_y, tiles):
        return [[(value, first + tiles) for value, first in pieces] for pieces in by_y]

    def merge(by_x):
        return [piece for dy in range(ys) for by_y in by_x for piece in by_y[dy]]

    def along_z(data, count, has_var, before_sums, before_middle):
        own, close, far = partial_sums(flag, after(w, *before_sums), data, count, has_var)
        far_in = z_send(far, ((0, 1), (3, 2)))
        close_in = z_send(close, near)
        to_middle, to_end = middle(after(far, *before_middle), far_in)
        middle_in = z_send(to_middle, ((1, 2), (2, 1)))
        end_in = z_send(to_end, ((1, 3), (2, 0)))
        return (far_in, to_end, close_in), own, [close_in, middle_in, end_in]

    def spread(own, others, *done):
        mine = combine(after(own, *done), others)
        along = [geo_shift(mine, dx, 0) for dx in range(xs)]
        return mine, [geo_shift(along[dx], 0, dc) for dx in range(xs) for dc in range(CORES)]

    def places(tiles):
        starts, lasts = [], []
        for dx in range(xs):
            for dc in range(CORES):
                group = (x - dx) % xs
                starts.append((core - dc) % CORES * tiles + start_of(group, tiles))
                lasts.append(group == xs - 1)
        return jnp.stack(starts + lasts).astype(jnp.int32)

    mean_width = estimates.shape[1] // LANES // CORES
    load_width = factors.shape[1] // LANES // CORES + 1
    load_tiles = split(each_of(load_width), LOAD_FIRST)
    mean_tiles = split(each_of(mean_width), MEAN_FIRST)
    (first_a, first_b), (first_c, first_d) = load_tiles, mean_tiles
    load_x = along_x(exchange(factors, last_tile))
    mean_x = along_x(exchange(after(estimates, load_x[0][1])))
    mean_x = [[joined(pieces, 0, first_c + first_d)] for pieces in mean_x]
    own = along_y(load_x[0])
    data_a = merge([own] + [along_y([joined(pieces, 0, first_a)]) for pieces in load_x[1:]])
    data_b = merge([later(own, first_a)] + [along_y([joined(pieces, first_a, first_b)]) for pieces in load_x[1:]])
    (far_a, end_a, close_a), *za = along_z(data_a, first_a, False, (), ())
    data_c = merge([along_y([joined(pieces, 0, first_c)], za[0]) for pieces in mean_x])
    data_d = merge([along_y([joined(pieces, first_c, first_d)], end_a) for pieces in mean_x])
    (far_b, end_b, close_b), *zb = along_z(data_b, first_b, True, (far_a,), (close_a,))
    (far_c, end_c, _), *zc = along_z(data_c, first_c, False, (end_b,), (close_b,))
    mine_a, load_a = spread(*za)
    mine_b, load_b = spread(after(zb[0], zc[0], *[value for value, _ in data_d]), zb[1])
    load_pieces = load_a + [after(load_b[0], end_c)] + load_b[1:]
    cov = covariance(places(load_width), load_pieces, load_tiles, load_width * CORES, ages, rank)
    _, *zd = along_z(data_d, first_d, False, (zc[0],), (cov,))
    _, mean_c = spread(after(zc[0], cov), zc[1])
    _, mean_d = spread(after(zd[0], cov), zd[1])
    mean_pieces = mean_c + mean_d
    mean = marginal(places(mean_width), mean_pieces, mean_tiles, mean_width * CORES)
    return mean, cov.T


def solution(mesh):
    return jax.shard_map(
        functools.partial(shards, mesh.shape["geo"], mesh.shape["dist"]),
        mesh=mesh,
        in_specs=(
            P(("geo", "dist"), None),
            P(("geo", "dist"), None),
            P(("geo", "dist"), None),
            P("dist", None),
            P("dist", None),
        ),
        out_specs=(P("dist", None), P("dist", None)),
        check_vma=False,
    )
```

```python
import functools
import jax
import jax.numpy as jnp
from jax import lax
from jax.experimental import pallas as pl
from jax.experimental.pallas import tpu as pltpu
from jax.sharding import PartitionSpec as P

LANES = 128
CORES = 2
DEPTH = 4
LOAD_FIRST = 7
MEAN_FIRST = 10
SCALES = 16
TOP = 32767.0
VMEM_BYTES = 48 * 1024 * 1024
BEFORE = (((0,), (0,)), ((), ()))
AFTER = (((1,), (1,)), ((), ()))


def params():
    return pltpu.CompilerParams(vmem_limit_bytes=VMEM_BYTES)


def cost(flops, moved):
    return pl.CostEstimate(flops=flops, bytes_accessed=moved, transcendentals=0)


def after(value, *others):
    return lax.optimization_barrier((value, *others))[0]


def split(each, first):
    first = each // 2 if first >= each else first
    return (first, each - first)


def twice(value):
    return jnp.concatenate([value, value], axis=0)


def encode(src, src_base, dst, dst_base, height):
    half = height // 2
    powers = []
    for h in range(2):
        top = jnp.abs(src[pl.ds(src_base + h * half, 8), :])
        for r in range(8, half, 8):
            top = jnp.maximum(top, jnp.abs(src[pl.ds(src_base + h * half + r, 8), :]))
        power = jnp.floor(jnp.log2(jnp.maximum(top, 1e-30))) + 1.0
        gain = twice(jnp.exp2(-power) * TOP)
        for r in range(h * half, (h + 1) * half, 16):
            level = jnp.clip(jnp.round(src[pl.ds(src_base + r, 16), :] * gain), -TOP, TOP)
            dst[pl.ds(dst_base + r, 16), :] = level.astype(jnp.int32).astype(jnp.int16)
        powers.append(power)
    both = jnp.concatenate(powers, axis=0)
    dst[pl.ds(dst_base + height, SCALES), :] = both.astype(jnp.int32).astype(jnp.int16)


def steps_of(coded, base, height):
    power = coded[pl.ds(base + height, SCALES), :].astype(jnp.int32).astype(jnp.float32)
    step = jnp.exp2(power) * (1.0 / TOP)
    return [twice(step[:8]), twice(step[8:])]


def decode(coded, row, step):
    return coded[pl.ds(row, 16), :].astype(jnp.int32).astype(jnp.float32) * step


def weights_kernel(rows, base_ref, query_ref, out_ref):
    each = query_ref.shape[0] // 2
    row_id = lax.broadcasted_iota(jnp.int32, (16, LANES), 0)

    def piece(j, carry):
        for u in range(DEPTH):
            lanes = slice(u * LANES, (u + 1) * LANES)
            for r in range(0, rows, 16):
                tract = row_id + (base_ref[j] + r)
                total = jnp.zeros((16, LANES), jnp.float32)
                for k in range(each):
                    share = query_ref[each + k:each + k + 1, lanes].astype(jnp.float32) * (1.0 / 256.0)
                    total = jnp.where(query_ref[k:k + 1, lanes] == tract, share, total)
                where = pl.ds(pl.multiple_of(j * rows + r, 16), 16)
                out_ref[where, lanes] = total.astype(jnp.bfloat16)
        return carry

    lax.fori_loop(0, out_ref.shape[0] // rows, piece, 0)


def build_weights(bases, queries, rows):
    pieces = bases.shape[0]
    width = queries.shape[1]
    shape = (pieces * rows, width)
    return pl.pallas_call(
        functools.partial(weights_kernel, rows),
        grid_spec=pltpu.PrefetchScalarGridSpec(
            num_scalar_prefetch=1,
            grid=(1,),
            in_specs=[pl.BlockSpec(queries.shape, lambda i, s: (0, 0))],
            out_specs=pl.BlockSpec(shape, lambda i, s: (0, 0)),
        ),
        out_shape=jax.ShapeDtypeStruct(shape, jnp.bfloat16),
        compiler_params=params(),
        cost_estimate=cost(shape[0] * width * queries.shape[0] * 200, shape[0] * width * 2),
        name="build_weights",
    )(bases, queries)


def sums_kernel(offsets, has_var, flag_ref, w_ref, *refs):
    parts = len(offsets)
    data = refs[:parts]
    own_ref, opposite_ref, sent_ref, acc_ref = refs[parts:]
    columns = own_ref.shape[0]
    coded = columns + SCALES
    rows = [0]
    for d in data:
        rows.append(rows[-1] + d.shape[0])

    def weighted(get, t):
        total = None
        for j in range(parts):
            part = lax.dot_general(
                data[j][:, (offsets[j] + t) * LANES:(offsets[j] + t + 1) * LANES],
                get(w_ref[rows[j]:rows[j + 1], :]),
                BEFORE,
                preferred_element_type=jnp.float32,
            )
            total = part if total is None else total + part
        return total

    def put(t, value):
        where = slice(t * LANES, (t + 1) * LANES)
        for u, ref in enumerate((own_ref, opposite_ref, acc_ref.at[0], acc_ref.at[1])):
            ref[where, :] = value[:, u * LANES:(u + 1) * LANES]

    for t in range(columns // LANES):
        put(t, weighted(lambda w: w, t))

    if has_var:
        @pl.when(flag_ref[0] == 1)
        def _():
            def square(w):
                wide = w.astype(jnp.float32)
                return wide * wide

            def high(w):
                return square(w).astype(jnp.bfloat16)

            def low(w):
                s = square(w)
                return (s - s.astype(jnp.bfloat16).astype(jnp.float32)).astype(jnp.bfloat16)

            t = columns // LANES - 1
            put(t, weighted(high, t) + weighted(low, t))

    for u in range(2):
        encode(acc_ref.at[u], 0, sent_ref, u * coded, columns)


def partial_sums(flag, w, data, count, has_var):
    columns = count * LANES
    offsets = tuple(first for _, first in data)
    data = [array for array, _ in data]
    coded = columns + SCALES
    whole = lambda i, s: (0, 0)
    shapes = [
        jax.ShapeDtypeStruct((columns, LANES), jnp.float32),
        jax.ShapeDtypeStruct((columns, LANES), jnp.float32),
        jax.ShapeDtypeStruct((2 * coded, LANES), jnp.int16),
    ]
    return pl.pallas_call(
        functools.partial(sums_kernel, offsets, has_var),
        grid_spec=pltpu.PrefetchScalarGridSpec(
            num_scalar_prefetch=1,
            grid=(1,),
            in_specs=[pl.BlockSpec(w.shape, whole)] + [pl.BlockSpec(d.shape, whole) for d in data],
            out_specs=[pl.BlockSpec(s.shape, whole) for s in shapes],
            scratch_shapes=[pltpu.VMEM((2, columns, LANES), jnp.float32)],
        ),
        out_shape=shapes,
        compiler_params=params(),
        cost_estimate=cost(2 * w.shape[0] * w.shape[1] * columns, 2 * w.shape[0] * columns + columns * LANES * 10),
        name="partial_sums",
    )(flag, w, *data)


def combine_kernel(bases, own_ref, *refs):
    others, out_ref, acc_ref = refs[:-2], refs[-2], refs[-1]
    height = acc_ref.shape[0]
    steps = [steps_of(o, base, height) for o, base in zip(others, bases)]
    for r in range(0, height, 16):
        total = own_ref[r:r + 16, :]
        for o, base, step in zip(others, bases, steps):
            total = total + decode(o, base + r, step[r * 2 // height])
        acc_ref[r:r + 16, :] = total
    encode(acc_ref, 0, out_ref, 0, height)


def combine(own, *others):
    height = own.shape[0]
    shape = (height + SCALES, LANES)
    return pl.pallas_call(
        functools.partial(combine_kernel, [unit * shape[0] for _, unit in others]),
        out_shape=jax.ShapeDtypeStruct(shape, jnp.int16),
        scratch_shapes=[pltpu.VMEM((height, LANES), jnp.float32)],
        compiler_params=params(),
        cost_estimate=cost(height * LANES * 16, height * LANES * 12),
        name="combine",
    )(own, *[array for array, _ in others])


def each_piece(place_ref, pieces, tiles, do):
    groups = place_ref.shape[0] // 2
    for upper in (1, 0):
        for r in range(groups):
            @pl.when(place_ref[groups + r] == upper)
            def _(r=r):
                first = 0
                for c, count in enumerate(tiles):
                    do((place_ref[r] + first) * LANES, pieces[c * groups + r], count * LANES)
                    first += count


def marginal_kernel(tiles, place_ref, *refs):
    pieces, out_ref, tile_ref = refs[:-2], refs[-2], refs[-1]

    def do(start, piece, height):
        steps = steps_of(piece, 0, height)
        for t in range(0, height, LANES):
            for r in range(0, LANES, 16):
                tile_ref[r:r + 16, :] = decode(piece, t + r, steps[(t + r) * 2 // height])
            out_ref[:, pl.ds(pl.multiple_of(start + t, LANES), LANES)] = tile_ref[...].T

    each_piece(place_ref, pieces, tiles, do)


def marginal(places, pieces, tiles, total):
    shape = (LANES, total * LANES)
    return pl.pallas_call(
        functools.partial(marginal_kernel, tiles),
        grid_spec=pltpu.PrefetchScalarGridSpec(
            num_scalar_prefetch=1,
            grid=(1,),
            in_specs=[pl.BlockSpec(p.shape, lambda i, s: (0, 0)) for p in pieces],
            out_specs=pl.BlockSpec(shape, lambda i, s: (0, 0)),
            scratch_shapes=[pltpu.VMEM((LANES, LANES), jnp.float32)],
        ),
        out_shape=jax.ShapeDtypeStruct(shape, jnp.float32),
        compiler_params=params(),
        cost_estimate=cost(shape[0] * shape[1] * 4, shape[0] * shape[1] * 6),
        name="marginal",
    )(places, *pieces)


def covariance_kernel(tiles, total, ages, rank, place_ref, *refs):
    pieces, out_ref = refs[:-4], refs[-4]
    load_ref, age_ref, cov_ref = refs[-3:]
    pitch = -(-ages // 8) * 8
    left = lax.broadcasted_iota(jnp.int32, (LANES, LANES), 1) < rank

    def do(start, piece, height):
        steps = steps_of(piece, 0, height)
        for r in range(0, height, 16):
            load_ref[pl.ds(pl.multiple_of(start + r, 16), 16), :] = decode(piece, r, steps[r * 2 // height])

    each_piece(place_ref, pieces, tiles, do)

    def turn(t, carry):
        tile = t + t // (total // CORES - 1)
        value = load_ref[pl.ds(pl.multiple_of(tile * LANES, LANES), LANES), :].T
        swapped = pltpu.roll(value, rank, 1)
        age_ref[pl.ds(2 * t, LANES, stride=pitch), :] = jnp.where(left, value, swapped)
        age_ref[pl.ds(2 * t + 1, LANES, stride=pitch), :] = jnp.where(left, swapped, value)
        return carry

    lax.fori_loop(0, ages * rank // LANES, turn, 0, unroll=True)

    def outer(d, carry):
        start = pl.multiple_of(d * pitch, 8)
        mine = age_ref[pl.ds(start, LANES), :]
        high = mine.astype(jnp.bfloat16).astype(jnp.float32)
        low = mine - high
        mixed = jnp.where(left, high, low).astype(jnp.bfloat16)
        product = lax.dot_general(
            jnp.concatenate([mixed, mixed], axis=1),
            jnp.concatenate([high.astype(jnp.bfloat16), low.astype(jnp.bfloat16)], axis=1),
            AFTER,
            preferred_element_type=jnp.float32,
        )
        cov_ref[pl.ds(start, pitch), :] = product[:pitch]
        return carry

    lax.fori_loop(0, LANES, outer, 0, unroll=16)

    def store(m, carry):
        base = pl.multiple_of(m * (2 * ages), 8)
        for p in range(2):
            value = cov_ref[pl.ds(2 * m + p, LANES, stride=pitch), :].T
            out_ref[pl.ds(base + p * ages, ages), :] = value[:ages]
        return carry

    lax.fori_loop(0, ages // 2, store, 0, unroll=True)
    for i in range(ages):
        row = i * (ages + 1)
        out_ref[row:row + 1, :] += load_ref[(total - 1) * LANES + i:(total - 1) * LANES + i + 1, :]


def covariance(places, pieces, tiles, total, ages, rank):
    pitch = -(-ages // 8) * 8
    shape = (ages * ages, LANES)
    tall = (LANES * pitch + LANES - pitch, LANES)
    return pl.pallas_call(
        functools.partial(covariance_kernel, tiles, total, ages, rank),
        grid_spec=pltpu.PrefetchScalarGridSpec(
            num_scalar_prefetch=1,
            grid=(1,),
            in_specs=[pl.BlockSpec(p.shape, lambda i, s: (0, 0)) for p in pieces],
            out_specs=pl.BlockSpec(shape, lambda i, s: (0, 0)),
            scratch_shapes=[
                pltpu.VMEM((total * LANES, LANES), jnp.float32),
                pltpu.VMEM(tall, jnp.float32),
                pltpu.VMEM(tall, jnp.float32),
            ],
        ),
        out_shape=jax.ShapeDtypeStruct(shape, jnp.float32),
        compiler_params=params(),
        cost_estimate=cost(LANES * ages * ages * rank * 140, shape[0] * shape[1] * 4),
        name="covariance",
    )(places, *pieces)


def shards(groups, parts, estimates, factors, variances, intersection_tracts, intersection_weights):
    xs = groups // CORES
    ys = parts // DEPTH
    rows = estimates.shape[0]
    ages = variances.shape[1]
    rank = factors.shape[1] // ages
    geo = lax.axis_index("geo")
    dist = lax.axis_index("dist")
    x, core = geo // CORES, geo % CORES
    z, y = dist // ys, dist % ys

    def move(value, dx, dc, dy=0):
        if (dx, dc, dy) == (0, 0, 0):
            return value
        perm = []
        for g in range(groups):
            for d in range(parts):
                to = (g // CORES + dx) % xs * CORES + (g + dc) % CORES
                perm.append((g * parts + d, to * parts + d // ys * ys + (d + dy) % ys))
        return lax.ppermute(value, ("geo", "dist"), perm)

    def z_swap(value, bits):
        perm = [(a * ys + b, (a ^ bits) * ys + b) for a in range(DEPTH) for b in range(ys)]
        return lax.ppermute(value, "dist", perm)

    last_tile = jnp.pad(variances, ((0, 0), (0, -ages % LANES)))

    def half(array, c, *more):
        width = array.shape[1] // CORES
        return jnp.concatenate([lax.dynamic_slice(array, (0, c * width), (rows, width)), *more], axis=1)

    def start_of(group, tiles):
        return jnp.minimum(group * each_of(tiles), tiles - each_of(tiles))

    def each_of(tiles):
        return -(-tiles // xs)

    def groups_of(array, *more):
        both = [half(array, (core + dc) % CORES, *more) for dc in range(CORES)]
        tiles = both[0].shape[1] // LANES
        size = (rows, each_of(tiles) * LANES)
        return [
            [lax.dynamic_slice(b, (0, start_of((x + dx) % xs, tiles) * LANES), size) for b in both] for dx in range(xs)
        ]

    load_cut = groups_of(factors, last_tile)
    load_x = [[move(load_cut[dx][dc], dx, dc) for dc in range(CORES)] for dx in range(xs)]
    load_y = [[(value, 0) for value in load_x[0]]]
    load_y += [[(move(load_cut[0][dc], 0, dc, dy), 0) for dc in range(CORES)] for dy in range(1, ys)]
    queries = jnp.concatenate([intersection_tracts.T, intersection_weights.T], axis=0)
    queries = after(queries, load_x[0][1])
    queries = jnp.concatenate([queries] + [z_swap(queries, bits) for bits in (2, 1, 3)], axis=1)

    bases = jnp.stack([
        (((x - dx) % xs * CORES + (core - dc) % CORES) * parts + z * ys + (y - dy) % ys) * rows
        for dy in range(ys) for dx in range(xs) for dc in range(CORES)
    ]).astype(jnp.int32)
    w = build_weights(bases, queries, rows)
    flag = (x == xs - 1).astype(jnp.int32).reshape(1)
    def joined(pieces, first, count):
        return jnp.concatenate([p[:, first * LANES:(first + count) * LANES] for p in pieces], axis=0)

    def along_y(by_x, first, count, *done):
        out = []
        for pieces in by_x[1:]:
            sent = after(joined(pieces, first, count), *done)
            out.append([[(value, first) for value in pieces]] + [[(move(sent, 0, 0, dy), 0)] for dy in range(1, ys)])
        return out

    def later(by_y, tiles):
        return [[(value, first + tiles) for value, first in pieces] for pieces in by_y]

    def merge(by_x):
        return [piece for dy in range(ys) for by_y in by_x for piece in by_y[dy]]

    def along_z(data, count, has_var, before_sums, before_middle):
        own, opposite, sent = partial_sums(flag, after(w, *before_sums), data, count, has_var)
        near = z_swap(sent, 1)
        far = z_swap(combine(after(opposite, *before_middle), (near, 1)), 2)
        return own, near, far

    def spread(own, near, far):
        mine = combine(own, (near, 0), (far, 0))
        along = [move(mine, dx, 0) for dx in range(xs)]
        return mine, [move(along[dx], 0, dc) for dx in range(xs) for dc in range(CORES)]

    def places(tiles):
        starts, lasts = [], []
        for dx in range(xs):
            for dc in range(CORES):
                group = (x - dx) % xs
                starts.append((core - dc) % CORES * tiles + start_of(group, tiles))
                lasts.append(group == xs - 1)
        return jnp.stack(starts + lasts).astype(jnp.int32)

    mean_width = estimates.shape[1] // LANES // CORES
    load_width = factors.shape[1] // LANES // CORES + 1
    load_tiles = split(each_of(load_width), LOAD_FIRST)
    mean_tiles = split(each_of(mean_width), MEAN_FIRST)
    (first_a, first_b), (first_c, first_d) = load_tiles, mean_tiles
    mean_cut = groups_of(after(estimates, load_x[0][1]))
    mean_x = [[move(mean_cut[dx][dc], dx, dc) for dc in range(CORES)] for dx in range(xs)]
    data_a = merge([load_y] + along_y(load_x, 0, first_a))
    data_b = merge([later(load_y, first_a)] + along_y(load_x, first_a, first_b))
    own_a, near_a, far_a = along_z(data_a, first_a, False, (), ())
    mean_y = [[(value, 0) for value in mean_x[0]]]
    mean_y += [[(move(after(mean_cut[0][dc], own_a), 0, dc, dy), 0) for dc in range(CORES)] for dy in range(1, ys)]
    mean_there = [value for pieces in mean_y[1:] for value, _ in pieces]
    own_b, near_b, far_b = along_z(data_b, first_b, True, (near_a,), mean_there)
    data_c = merge([mean_y] + along_y(mean_x, 0, first_c, *mean_there))
    data_d = merge([later(mean_y, first_c)] + along_y(mean_x, first_c, first_d, *mean_there))
    own_c, opposite_c, sent_c = partial_sums(flag, after(w, far_a, far_b), data_c, first_c, False)
    own_d, opposite_d, sent_d = partial_sums(flag, after(w, own_c), data_d, first_d, False)
    _, load_a = spread(own_a, near_a, far_a)
    _, load_b = spread(own_b, near_b, far_b)
    near_c, near_d = z_swap(sent_c, 1), z_swap(sent_d, 1)
    far_c = z_swap(combine(opposite_c, (near_c, 1)), 2)
    far_d = z_swap(combine(opposite_d, (near_d, 1)), 2)
    mine_c, mean_c = spread(own_c, near_c, far_c)
    mine_d, mean_d = spread(own_d, near_d, far_d)
    load_pieces = load_a + [after(load_b[0], mine_c, mine_d)] + load_b[1:]
    cov = covariance(places(load_width), load_pieces, load_tiles, load_width * CORES, ages, rank)
    mean_pieces = mean_c + mean_d
    mean = marginal(places(mean_width), mean_pieces, mean_tiles, mean_width * CORES)
    return mean, cov.T


def solution(mesh):
    return jax.shard_map(
        functools.partial(shards, mesh.shape["geo"], mesh.shape["dist"]),
        mesh=mesh,
        in_specs=(
            P(("geo", "dist"), None),
            P(("geo", "dist"), None),
            P(("geo", "dist"), None),
            P("dist", None),
            P("dist", None),
        ),
        out_specs=(P("dist", None), P("dist", None)),
        check_vma=False,
    )
```

```python
import functools
import jax
import jax.numpy as jnp
from jax import lax
from jax.experimental import pallas as pl
from jax.experimental.pallas import tpu as pltpu
from jax.sharding import PartitionSpec as P

LANES = 128
CORES = 2
DEPTH = 4
LOAD_FIRST = 7
MEAN_FIRST = 8
SCALES = 16
TOP = 32767.0
VMEM_BYTES = 48 * 1024 * 1024
BEFORE = (((0,), (0,)), ((), ()))
AFTER = (((1,), (1,)), ((), ()))


def params():
    return pltpu.CompilerParams(vmem_limit_bytes=VMEM_BYTES)


def cost(flops, moved):
    return pl.CostEstimate(flops=flops, bytes_accessed=moved, transcendentals=0)


def after(value, *others):
    return lax.optimization_barrier((value, *others))[0]


def split(each, first):
    first = each // 2 if first >= each else first
    return (first, each - first)


def twice(value):
    return jnp.concatenate([value, value], axis=0)


def encode(src, src_base, dst, dst_base, height):
    half = height // 2
    powers = []
    for h in range(2):
        top = jnp.abs(src[pl.ds(src_base + h * half, 8), :])
        for r in range(8, half, 8):
            top = jnp.maximum(top, jnp.abs(src[pl.ds(src_base + h * half + r, 8), :]))
        power = jnp.floor(jnp.log2(jnp.maximum(top, 1e-30))) + 1.0
        gain = twice(jnp.exp2(-power) * TOP)
        for r in range(h * half, (h + 1) * half, 16):
            level = jnp.clip(jnp.round(src[pl.ds(src_base + r, 16), :] * gain), -TOP, TOP)
            dst[pl.ds(dst_base + r, 16), :] = level.astype(jnp.int32).astype(jnp.int16)
        powers.append(power)
    both = jnp.concatenate(powers, axis=0)
    dst[pl.ds(dst_base + height, SCALES), :] = both.astype(jnp.int32).astype(jnp.int16)


def steps_of(coded, base, height):
    power = coded[pl.ds(base + height, SCALES), :].astype(jnp.int32).astype(jnp.float32)
    step = jnp.exp2(power) * (1.0 / TOP)
    return [twice(step[:8]), twice(step[8:])]


def decode(coded, row, step):
    return coded[pl.ds(row, 16), :].astype(jnp.int32).astype(jnp.float32) * step


def weights_kernel(rows, base_ref, query_ref, out_ref):
    each = query_ref.shape[0] // 2
    row_id = lax.broadcasted_iota(jnp.int32, (16, LANES), 0)

    def piece(j, carry):
        for u in range(DEPTH):
            lanes = slice(u * LANES, (u + 1) * LANES)
            for r in range(0, rows, 16):
                tract = row_id + (base_ref[j] + r)
                total = jnp.zeros((16, LANES), jnp.float32)
                for k in range(each):
                    share = query_ref[each + k:each + k + 1, lanes].astype(jnp.float32) * (1.0 / 256.0)
                    total = jnp.where(query_ref[k:k + 1, lanes] == tract, share, total)
                where = pl.ds(pl.multiple_of(j * rows + r, 16), 16)
                out_ref[where, lanes] = total.astype(jnp.bfloat16)
        return carry

    lax.fori_loop(0, out_ref.shape[0] // rows, piece, 0)


def build_weights(bases, queries, rows):
    pieces = bases.shape[0]
    width = queries.shape[1]
    shape = (pieces * rows, width)
    return pl.pallas_call(
        functools.partial(weights_kernel, rows),
        grid_spec=pltpu.PrefetchScalarGridSpec(
            num_scalar_prefetch=1,
            grid=(1,),
            in_specs=[pl.BlockSpec(queries.shape, lambda i, s: (0, 0))],
            out_specs=pl.BlockSpec(shape, lambda i, s: (0, 0)),
        ),
        out_shape=jax.ShapeDtypeStruct(shape, jnp.bfloat16),
        compiler_params=params(),
        cost_estimate=cost(shape[0] * width * queries.shape[0] * 200, shape[0] * width * 2),
        name="build_weights",
    )(bases, queries)


def sums_kernel(offsets, has_var, flag_ref, w_ref, *refs):
    parts = len(offsets)
    data = refs[:parts]
    own_ref, opposite_ref, sent_ref, acc_ref = refs[parts:]
    columns = own_ref.shape[0]
    coded = columns + SCALES
    rows = [0]
    for d in data:
        rows.append(rows[-1] + d.shape[0])

    def weighted(get, t):
        total = None
        for j in range(parts):
            part = lax.dot_general(
                data[j][:, (offsets[j] + t) * LANES:(offsets[j] + t + 1) * LANES],
                get(w_ref[rows[j]:rows[j + 1], :]),
                BEFORE,
                preferred_element_type=jnp.float32,
            )
            total = part if total is None else total + part
        return total

    def put(t, value):
        where = slice(t * LANES, (t + 1) * LANES)
        for u, ref in enumerate((own_ref, opposite_ref, acc_ref.at[0], acc_ref.at[1])):
            ref[where, :] = value[:, u * LANES:(u + 1) * LANES]

    for t in range(columns // LANES):
        put(t, weighted(lambda w: w, t))

    if has_var:
        @pl.when(flag_ref[0] == 1)
        def _():
            def square(w):
                wide = w.astype(jnp.float32)
                return wide * wide

            def high(w):
                return square(w).astype(jnp.bfloat16)

            def low(w):
                s = square(w)
                return (s - s.astype(jnp.bfloat16).astype(jnp.float32)).astype(jnp.bfloat16)

            t = columns // LANES - 1
            put(t, weighted(high, t) + weighted(low, t))

    for u in range(2):
        encode(acc_ref.at[u], 0, sent_ref, u * coded, columns)


def partial_sums(flag, w, data, count, has_var):
    columns = count * LANES
    offsets = tuple(first for _, first in data)
    data = [array for array, _ in data]
    coded = columns + SCALES
    whole = lambda i, s: (0, 0)
    shapes = [
        jax.ShapeDtypeStruct((columns, LANES), jnp.float32),
        jax.ShapeDtypeStruct((columns, LANES), jnp.float32),
        jax.ShapeDtypeStruct((2 * coded, LANES), jnp.int16),
    ]
    return pl.pallas_call(
        functools.partial(sums_kernel, offsets, has_var),
        grid_spec=pltpu.PrefetchScalarGridSpec(
            num_scalar_prefetch=1,
            grid=(1,),
            in_specs=[pl.BlockSpec(w.shape, whole)] + [pl.BlockSpec(d.shape, whole) for d in data],
            out_specs=[pl.BlockSpec(s.shape, whole) for s in shapes],
            scratch_shapes=[pltpu.VMEM((2, columns, LANES), jnp.float32)],
        ),
        out_shape=shapes,
        compiler_params=params(),
        cost_estimate=cost(2 * w.shape[0] * w.shape[1] * columns, 2 * w.shape[0] * columns + columns * LANES * 10),
        name="partial_sums",
    )(flag, w, *data)


def combine_kernel(bases, own_ref, *refs):
    others, out_ref, acc_ref = refs[:-2], refs[-2], refs[-1]
    height = acc_ref.shape[0]
    steps = [steps_of(o, base, height) for o, base in zip(others, bases)]
    for r in range(0, height, 16):
        total = own_ref[r:r + 16, :]
        for o, base, step in zip(others, bases, steps):
            total = total + decode(o, base + r, step[r * 2 // height])
        acc_ref[r:r + 16, :] = total
    encode(acc_ref, 0, out_ref, 0, height)


def combine(own, *others):
    height = own.shape[0]
    shape = (height + SCALES, LANES)
    return pl.pallas_call(
        functools.partial(combine_kernel, [unit * shape[0] for _, unit in others]),
        out_shape=jax.ShapeDtypeStruct(shape, jnp.int16),
        scratch_shapes=[pltpu.VMEM((height, LANES), jnp.float32)],
        compiler_params=params(),
        cost_estimate=cost(height * LANES * 16, height * LANES * 12),
        name="combine",
    )(own, *[array for array, _ in others])


def each_piece(place_ref, pieces, tiles, do):
    groups = place_ref.shape[0] // 2
    for upper in (1, 0):
        for r in range(groups):
            @pl.when(place_ref[groups + r] == upper)
            def _(r=r):
                first = 0
                for c, count in enumerate(tiles):
                    do((place_ref[r] + first) * LANES, pieces[c * groups + r], count * LANES)
                    first += count


def marginal_kernel(tiles, place_ref, *refs):
    pieces, out_ref, tile_ref = refs[:-2], refs[-2], refs[-1]

    def do(start, piece, height):
        steps = steps_of(piece, 0, height)
        for t in range(0, height, LANES):
            for r in range(0, LANES, 16):
                tile_ref[r:r + 16, :] = decode(piece, t + r, steps[(t + r) * 2 // height])
            out_ref[:, pl.ds(pl.multiple_of(start + t, LANES), LANES)] = tile_ref[...].T

    each_piece(place_ref, pieces, tiles, do)


def marginal(places, pieces, tiles, total):
    shape = (LANES, total * LANES)
    return pl.pallas_call(
        functools.partial(marginal_kernel, tiles),
        grid_spec=pltpu.PrefetchScalarGridSpec(
            num_scalar_prefetch=1,
            grid=(1,),
            in_specs=[pl.BlockSpec(p.shape, lambda i, s: (0, 0)) for p in pieces],
            out_specs=pl.BlockSpec(shape, lambda i, s: (0, 0)),
            scratch_shapes=[pltpu.VMEM((LANES, LANES), jnp.float32)],
        ),
        out_shape=jax.ShapeDtypeStruct(shape, jnp.float32),
        compiler_params=params(),
        cost_estimate=cost(shape[0] * shape[1] * 4, shape[0] * shape[1] * 6),
        name="marginal",
    )(places, *pieces)


def covariance_kernel(tiles, total, ages, rank, place_ref, *refs):
    pieces, out_ref = refs[:-4], refs[-4]
    load_ref, age_ref, cov_ref = refs[-3:]
    pitch = -(-ages // 8) * 8
    left = lax.broadcasted_iota(jnp.int32, (LANES, LANES), 1) < rank

    def do(start, piece, height):
        steps = steps_of(piece, 0, height)
        for r in range(0, height, 16):
            load_ref[pl.ds(pl.multiple_of(start + r, 16), 16), :] = decode(piece, r, steps[r * 2 // height])

    each_piece(place_ref, pieces, tiles, do)

    def turn(t, carry):
        tile = t + t // (total // CORES - 1)
        value = load_ref[pl.ds(pl.multiple_of(tile * LANES, LANES), LANES), :].T
        swapped = pltpu.roll(value, rank, 1)
        age_ref[pl.ds(2 * t, LANES, stride=pitch), :] = jnp.where(left, value, swapped)
        age_ref[pl.ds(2 * t + 1, LANES, stride=pitch), :] = jnp.where(left, swapped, value)
        return carry

    lax.fori_loop(0, ages * rank // LANES, turn, 0, unroll=True)

    def outer(d, carry):
        start = pl.multiple_of(d * pitch, 8)
        mine = age_ref[pl.ds(start, LANES), :]
        high = mine.astype(jnp.bfloat16).astype(jnp.float32)
        low = mine - high
        mixed = jnp.where(left, high, low).astype(jnp.bfloat16)
        product = lax.dot_general(
            jnp.concatenate([mixed, mixed], axis=1),
            jnp.concatenate([high.astype(jnp.bfloat16), low.astype(jnp.bfloat16)], axis=1),
            AFTER,
            preferred_element_type=jnp.float32,
        )
        cov_ref[pl.ds(start, pitch), :] = product[:pitch]
        return carry

    lax.fori_loop(0, LANES, outer, 0, unroll=16)

    def store(m, carry):
        base = pl.multiple_of(m * (2 * ages), 8)
        for p in range(2):
            value = cov_ref[pl.ds(2 * m + p, LANES, stride=pitch), :].T
            out_ref[pl.ds(base + p * ages, ages), :] = value[:ages]
        return carry

    lax.fori_loop(0, ages // 2, store, 0, unroll=True)
    for i in range(ages):
        row = i * (ages + 1)
        out_ref[row:row + 1, :] += load_ref[(total - 1) * LANES + i:(total - 1) * LANES + i + 1, :]


def covariance(places, pieces, tiles, total, ages, rank):
    pitch = -(-ages // 8) * 8
    shape = (ages * ages, LANES)
    tall = (LANES * pitch + LANES - pitch, LANES)
    return pl.pallas_call(
        functools.partial(covariance_kernel, tiles, total, ages, rank),
        grid_spec=pltpu.PrefetchScalarGridSpec(
            num_scalar_prefetch=1,
            grid=(1,),
            in_specs=[pl.BlockSpec(p.shape, lambda i, s: (0, 0)) for p in pieces],
            out_specs=pl.BlockSpec(shape, lambda i, s: (0, 0)),
            scratch_shapes=[
                pltpu.VMEM((total * LANES, LANES), jnp.float32),
                pltpu.VMEM(tall, jnp.float32),
                pltpu.VMEM(tall, jnp.float32),
            ],
        ),
        out_shape=jax.ShapeDtypeStruct(shape, jnp.float32),
        compiler_params=params(),
        cost_estimate=cost(LANES * ages * ages * rank * 140, shape[0] * shape[1] * 4),
        name="covariance",
    )(places, *pieces)


def shards(groups, parts, estimates, factors, variances, intersection_tracts, intersection_weights):
    xs = groups // CORES
    ys = parts // DEPTH
    rows = estimates.shape[0]
    ages = variances.shape[1]
    rank = factors.shape[1] // ages
    geo = lax.axis_index("geo")
    dist = lax.axis_index("dist")
    x, core = geo // CORES, geo % CORES
    z, y = dist // ys, dist % ys

    def move(value, dx, dc, dy=0):
        if (dx, dc, dy) == (0, 0, 0):
            return value
        perm = []
        for g in range(groups):
            for d in range(parts):
                to = (g // CORES + dx) % xs * CORES + (g + dc) % CORES
                perm.append((g * parts + d, to * parts + d // ys * ys + (d + dy) % ys))
        return lax.ppermute(value, ("geo", "dist"), perm)

    def z_swap(value, bits):
        perm = [(a * ys + b, (a ^ bits) * ys + b) for a in range(DEPTH) for b in range(ys)]
        return lax.ppermute(value, "dist", perm)

    last_tile = jnp.pad(variances, ((0, 0), (0, -ages % LANES)))

    def half(array, c, *more):
        width = array.shape[1] // CORES
        return jnp.concatenate([lax.dynamic_slice(array, (0, c * width), (rows, width)), *more], axis=1)

    def start_of(group, tiles):
        return jnp.minimum(group * each_of(tiles), tiles - each_of(tiles))

    def each_of(tiles):
        return -(-tiles // xs)

    def exchange(array, *more):
        return [half(array, core, *more), move(half(array, (core + 1) % CORES, *more), 0, 1)]

    def along_x(both):
        tiles = both[0].shape[1] // LANES
        size = (rows, each_of(tiles) * LANES)

        def part(group):
            return jnp.concatenate([lax.dynamic_slice(b, (0, start_of(group, tiles) * LANES), size) for b in both], axis=0)

        return [move(part((x + dx) % xs), dx, 0) for dx in range(xs)]

    queries = jnp.concatenate([intersection_tracts.T, intersection_weights.T], axis=0)
    queries = jnp.concatenate([queries, z_swap(queries, 2)], axis=1)
    queries = jnp.concatenate([queries, z_swap(queries, 1)], axis=1)
    load_both = exchange(factors, last_tile)
    load_x = along_x(load_both)

    bases = jnp.stack([
        (((x - dx) % xs * CORES + (core - dc) % CORES) * parts + z * ys + (y - dy) % ys) * rows
        for dy in range(ys) for dx in range(xs) for dc in range(CORES)
    ]).astype(jnp.int32)
    w = build_weights(bases, queries, rows)
    flag = (x == xs - 1).astype(jnp.int32).reshape(1)
    def along_y(value, first, count, *done):
        sent = after(value[:, first * LANES:(first + count) * LANES], *done)
        return [(value, first)] + [(move(sent, 0, 0, dy), 0) for dy in range(1, ys)]

    def later(by_y, tiles):
        return [(value, first + tiles) for value, first in by_y]

    def merge(by_x):
        return [by_y[dy] for dy in range(ys) for by_y in by_x]

    def along_z(data, count, has_var, *before):
        own, opposite, sent = partial_sums(flag, after(w, *before), data, count, has_var)
        near = z_swap(sent, 1)
        middle = combine(opposite, (near, 1))
        return own, near, middle, z_swap(middle, 2)

    def spread(own, near, far):
        mine = combine(own, (near, 0), (far, 0))
        along = [move(mine, dx, 0) for dx in range(xs)]
        return mine, [move(along[dx], 0, dc) for dx in range(xs) for dc in range(CORES)]

    def places(tiles):
        starts, lasts = [], []
        for dx in range(xs):
            for dc in range(CORES):
                group = (x - dx) % xs
                starts.append((core - dc) % CORES * tiles + start_of(group, tiles))
                lasts.append(group == xs - 1)
        return jnp.stack(starts + lasts).astype(jnp.int32)

    mean_width = estimates.shape[1] // LANES // CORES
    load_width = factors.shape[1] // LANES // CORES + 1
    load_tiles = split(each_of(load_width), LOAD_FIRST)
    mean_tiles = split(each_of(mean_width), MEAN_FIRST)
    (first_a, first_b), (first_c, first_d) = load_tiles, mean_tiles
    mean_x = along_x(exchange(after(estimates, load_both[1])))
    load_y = along_y(load_x[0], 0, first_a + first_b)
    data_a = merge([load_y] + [along_y(value, 0, first_a) for value in load_x[1:]])
    data_b = merge([later(load_y, first_a)] + [along_y(value, first_a, first_b) for value in load_x[1:]])
    own_a, near_a, middle_a, far_a = along_z(data_a, first_a, False)
    mean_y = along_y(mean_x[0], 0, first_c + first_d, data_a[-1][0])
    there = data_b[-1][0]
    own_b, near_b, middle_b, far_b = along_z(data_b, first_b, True)
    data_c = merge([mean_y] + [along_y(value, 0, first_c, there) for value in mean_x[1:]])
    data_d = merge([later(mean_y, first_c)] + [along_y(value, first_c, first_d, there) for value in mean_x[1:]])
    own_c, near_c, middle_c, far_c = along_z(data_c, first_c, False, far_a, middle_b)
    own_d, near_d, middle_d, far_d = along_z(data_d, first_d, False, own_c, far_b)
    _, load_a = spread(own_a, near_a, far_a)
    _, load_b = spread(own_b, near_b, far_b)
    mine_c, mean_c = spread(own_c, near_c, far_c)
    mine_d, mean_d = spread(own_d, near_d, far_d)
    load_pieces = load_a + [after(load_b[0], mine_c, mine_d)] + load_b[1:]
    cov = covariance(places(load_width), load_pieces, load_tiles, load_width * CORES, ages, rank)
    mean_pieces = mean_c + mean_d
    mean = marginal(places(mean_width), mean_pieces, mean_tiles, mean_width * CORES)
    return mean, cov.T


def solution(mesh):
    return jax.shard_map(
        functools.partial(shards, mesh.shape["geo"], mesh.shape["dist"]),
        mesh=mesh,
        in_specs=(
            P(("geo", "dist"), None),
            P(("geo", "dist"), None),
            P(("geo", "dist"), None),
            P("dist", None),
            P("dist", None),
        ),
        out_specs=(P("dist", None), P("dist", None)),
        check_vma=False,
    )
```

```python
import functools
import jax
import jax.numpy as jnp
from jax import lax
from jax.experimental import pallas as pl
from jax.experimental.pallas import tpu as pltpu
from jax.sharding import PartitionSpec as P

LANES = 128
CORES = 2
DEPTH = 4
LOAD_FIRST = 8
MEAN_FIRST = 8
SCALES = 16
TOP = 32767.0
VMEM_BYTES = 48 * 1024 * 1024
BEFORE = (((0,), (0,)), ((), ()))
AFTER = (((1,), (1,)), ((), ()))


def params():
    return pltpu.CompilerParams(vmem_limit_bytes=VMEM_BYTES)


def cost(flops, moved):
    return pl.CostEstimate(flops=flops, bytes_accessed=moved, transcendentals=0)


def after(value, *others):
    return lax.optimization_barrier((value, *others))[0]


def split(each, first):
    first = each // 2 if first >= each else first
    return (first, each - first)


def twice(value):
    return jnp.concatenate([value, value], axis=0)


def encode(src, src_base, dst, dst_base, height):
    half = height // 2
    powers = []
    for h in range(2):
        top = jnp.abs(src[pl.ds(src_base + h * half, 8), :])
        for r in range(8, half, 8):
            top = jnp.maximum(top, jnp.abs(src[pl.ds(src_base + h * half + r, 8), :]))
        power = jnp.floor(jnp.log2(jnp.maximum(top, 1e-30))) + 1.0
        gain = twice(jnp.exp2(-power) * TOP)
        for r in range(h * half, (h + 1) * half, 16):
            level = jnp.clip(jnp.round(src[pl.ds(src_base + r, 16), :] * gain), -TOP, TOP)
            dst[pl.ds(dst_base + r, 16), :] = level.astype(jnp.int32).astype(jnp.int16)
        powers.append(power)
    both = jnp.concatenate(powers, axis=0)
    dst[pl.ds(dst_base + height, SCALES), :] = both.astype(jnp.int32).astype(jnp.int16)


def steps_of(coded, base, height):
    power = coded[pl.ds(base + height, SCALES), :].astype(jnp.int32).astype(jnp.float32)
    step = jnp.exp2(power) * (1.0 / TOP)
    return [twice(step[:8]), twice(step[8:])]


def decode(coded, row, step):
    return coded[pl.ds(row, 16), :].astype(jnp.int32).astype(jnp.float32) * step


def weights_kernel(rows, base_ref, query_ref, out_ref):
    each = query_ref.shape[0] // 2
    row_id = lax.broadcasted_iota(jnp.int32, (16, LANES), 0)

    def piece(j, carry):
        for u in range(DEPTH):
            lanes = slice(u * LANES, (u + 1) * LANES)
            for r in range(0, rows, 16):
                tract = row_id + (base_ref[j] + r)
                total = jnp.zeros((16, LANES), jnp.float32)
                for k in range(each):
                    share = query_ref[each + k:each + k + 1, lanes].astype(jnp.float32) * (1.0 / 256.0)
                    total = jnp.where(query_ref[k:k + 1, lanes] == tract, share, total)
                where = pl.ds(pl.multiple_of(j * rows + r, 16), 16)
                out_ref[where, lanes] = total.astype(jnp.bfloat16)
        return carry

    lax.fori_loop(0, out_ref.shape[0] // rows, piece, 0)


def build_weights(bases, queries, rows):
    pieces = bases.shape[0]
    width = queries.shape[1]
    shape = (pieces * rows, width)
    return pl.pallas_call(
        functools.partial(weights_kernel, rows),
        grid_spec=pltpu.PrefetchScalarGridSpec(
            num_scalar_prefetch=1,
            grid=(1,),
            in_specs=[pl.BlockSpec(queries.shape, lambda i, s: (0, 0))],
            out_specs=pl.BlockSpec(shape, lambda i, s: (0, 0)),
        ),
        out_shape=jax.ShapeDtypeStruct(shape, jnp.bfloat16),
        compiler_params=params(),
        cost_estimate=cost(shape[0] * width * queries.shape[0] * 200, shape[0] * width * 2),
        name="build_weights",
    )(bases, queries)


def sums_kernel(offsets, has_var, flag_ref, w_ref, *refs):
    parts = len(offsets)
    data = refs[:parts]
    own_ref, opposite_ref, sent_ref, acc_ref = refs[parts:]
    columns = own_ref.shape[0]
    coded = columns + SCALES
    rows = [0]
    for d in data:
        rows.append(rows[-1] + d.shape[0])

    def weighted(get, t):
        total = None
        for j in range(parts):
            part = lax.dot_general(
                data[j][:, (offsets[j] + t) * LANES:(offsets[j] + t + 1) * LANES],
                get(w_ref[rows[j]:rows[j + 1], :]),
                BEFORE,
                preferred_element_type=jnp.float32,
            )
            total = part if total is None else total + part
        return total

    def put(t, value):
        where = slice(t * LANES, (t + 1) * LANES)
        for u, ref in enumerate((own_ref, opposite_ref, acc_ref.at[0], acc_ref.at[1])):
            ref[where, :] = value[:, u * LANES:(u + 1) * LANES]

    for t in range(columns // LANES):
        put(t, weighted(lambda w: w, t))

    if has_var:
        @pl.when(flag_ref[0] == 1)
        def _():
            def square(w):
                wide = w.astype(jnp.float32)
                return wide * wide

            def high(w):
                return square(w).astype(jnp.bfloat16)

            def low(w):
                s = square(w)
                return (s - s.astype(jnp.bfloat16).astype(jnp.float32)).astype(jnp.bfloat16)

            t = columns // LANES - 1
            put(t, weighted(high, t) + weighted(low, t))

    for u in range(2):
        encode(acc_ref.at[u], 0, sent_ref, u * coded, columns)


def partial_sums(flag, w, data, count, has_var):
    columns = count * LANES
    offsets = tuple(first for _, first in data)
    data = [array for array, _ in data]
    coded = columns + SCALES
    whole = lambda i, s: (0, 0)
    shapes = [
        jax.ShapeDtypeStruct((columns, LANES), jnp.float32),
        jax.ShapeDtypeStruct((columns, LANES), jnp.float32),
        jax.ShapeDtypeStruct((2 * coded, LANES), jnp.int16),
    ]
    return pl.pallas_call(
        functools.partial(sums_kernel, offsets, has_var),
        grid_spec=pltpu.PrefetchScalarGridSpec(
            num_scalar_prefetch=1,
            grid=(1,),
            in_specs=[pl.BlockSpec(w.shape, whole)] + [pl.BlockSpec(d.shape, whole) for d in data],
            out_specs=[pl.BlockSpec(s.shape, whole) for s in shapes],
            scratch_shapes=[pltpu.VMEM((2, columns, LANES), jnp.float32)],
        ),
        out_shape=shapes,
        compiler_params=params(),
        cost_estimate=cost(2 * w.shape[0] * w.shape[1] * columns, 2 * w.shape[0] * columns + columns * LANES * 10),
        name="partial_sums",
    )(flag, w, *data)


def combine_kernel(bases, own_ref, *refs):
    others, out_ref, acc_ref = refs[:-2], refs[-2], refs[-1]
    height = acc_ref.shape[0]
    steps = [steps_of(o, base, height) for o, base in zip(others, bases)]
    for r in range(0, height, 16):
        total = own_ref[r:r + 16, :]
        for o, base, step in zip(others, bases, steps):
            total = total + decode(o, base + r, step[r * 2 // height])
        acc_ref[r:r + 16, :] = total
    encode(acc_ref, 0, out_ref, 0, height)


def combine(own, *others):
    height = own.shape[0]
    shape = (height + SCALES, LANES)
    return pl.pallas_call(
        functools.partial(combine_kernel, [unit * shape[0] for _, unit in others]),
        out_shape=jax.ShapeDtypeStruct(shape, jnp.int16),
        scratch_shapes=[pltpu.VMEM((height, LANES), jnp.float32)],
        compiler_params=params(),
        cost_estimate=cost(height * LANES * 16, height * LANES * 12),
        name="combine",
    )(own, *[array for array, _ in others])


def each_piece(place_ref, pieces, tiles, do):
    groups = place_ref.shape[0] // 2
    for upper in (1, 0):
        for r in range(groups):
            @pl.when(place_ref[groups + r] == upper)
            def _(r=r):
                first = 0
                for c, count in enumerate(tiles):
                    do((place_ref[r] + first) * LANES, pieces[c * groups + r], count * LANES)
                    first += count


def marginal_kernel(tiles, place_ref, *refs):
    pieces, out_ref, tile_ref = refs[:-2], refs[-2], refs[-1]

    def do(start, piece, height):
        steps = steps_of(piece, 0, height)
        for t in range(0, height, LANES):
            for r in range(0, LANES, 16):
                tile_ref[r:r + 16, :] = decode(piece, t + r, steps[(t + r) * 2 // height])
            out_ref[:, pl.ds(pl.multiple_of(start + t, LANES), LANES)] = tile_ref[...].T

    each_piece(place_ref, pieces, tiles, do)


def marginal(places, pieces, tiles, total):
    shape = (LANES, total * LANES)
    return pl.pallas_call(
        functools.partial(marginal_kernel, tiles),
        grid_spec=pltpu.PrefetchScalarGridSpec(
            num_scalar_prefetch=1,
            grid=(1,),
            in_specs=[pl.BlockSpec(p.shape, lambda i, s: (0, 0)) for p in pieces],
            out_specs=pl.BlockSpec(shape, lambda i, s: (0, 0)),
            scratch_shapes=[pltpu.VMEM((LANES, LANES), jnp.float32)],
        ),
        out_shape=jax.ShapeDtypeStruct(shape, jnp.float32),
        compiler_params=params(),
        cost_estimate=cost(shape[0] * shape[1] * 4, shape[0] * shape[1] * 6),
        name="marginal",
    )(places, *pieces)


def covariance_kernel(tiles, total, ages, rank, place_ref, *refs):
    pieces, out_ref = refs[:-4], refs[-4]
    load_ref, age_ref, cov_ref = refs[-3:]
    pitch = -(-ages // 8) * 8
    left = lax.broadcasted_iota(jnp.int32, (LANES, LANES), 1) < rank

    def do(start, piece, height):
        steps = steps_of(piece, 0, height)
        for r in range(0, height, 16):
            load_ref[pl.ds(pl.multiple_of(start + r, 16), 16), :] = decode(piece, r, steps[r * 2 // height])

    each_piece(place_ref, pieces, tiles, do)

    def turn(t, carry):
        tile = t + t // (total // CORES - 1)
        value = load_ref[pl.ds(pl.multiple_of(tile * LANES, LANES), LANES), :].T
        swapped = pltpu.roll(value, rank, 1)
        age_ref[pl.ds(2 * t, LANES, stride=pitch), :] = jnp.where(left, value, swapped)
        age_ref[pl.ds(2 * t + 1, LANES, stride=pitch), :] = jnp.where(left, swapped, value)
        return carry

    lax.fori_loop(0, ages * rank // LANES, turn, 0, unroll=True)

    def outer(d, carry):
        start = pl.multiple_of(d * pitch, 8)
        mine = age_ref[pl.ds(start, LANES), :]
        high = mine.astype(jnp.bfloat16).astype(jnp.float32)
        low = mine - high
        mixed = jnp.where(left, high, low).astype(jnp.bfloat16)
        product = lax.dot_general(
            jnp.concatenate([mixed, mixed], axis=1),
            jnp.concatenate([high.astype(jnp.bfloat16), low.astype(jnp.bfloat16)], axis=1),
            AFTER,
            preferred_element_type=jnp.float32,
        )
        cov_ref[pl.ds(start, pitch), :] = product[:pitch]
        return carry

    lax.fori_loop(0, LANES, outer, 0, unroll=16)

    def store(m, carry):
        base = pl.multiple_of(m * (2 * ages), 8)
        for p in range(2):
            value = cov_ref[pl.ds(2 * m + p, LANES, stride=pitch), :].T
            out_ref[pl.ds(base + p * ages, ages), :] = value[:ages]
        return carry

    lax.fori_loop(0, ages // 2, store, 0, unroll=True)
    for i in range(ages):
        row = i * (ages + 1)
        out_ref[row:row + 1, :] += load_ref[(total - 1) * LANES + i:(total - 1) * LANES + i + 1, :]


def covariance(places, pieces, tiles, total, ages, rank):
    pitch = -(-ages // 8) * 8
    shape = (ages * ages, LANES)
    tall = (LANES * pitch + LANES - pitch, LANES)
    return pl.pallas_call(
        functools.partial(covariance_kernel, tiles, total, ages, rank),
        grid_spec=pltpu.PrefetchScalarGridSpec(
            num_scalar_prefetch=1,
            grid=(1,),
            in_specs=[pl.BlockSpec(p.shape, lambda i, s: (0, 0)) for p in pieces],
            out_specs=pl.BlockSpec(shape, lambda i, s: (0, 0)),
            scratch_shapes=[
                pltpu.VMEM((total * LANES, LANES), jnp.float32),
                pltpu.VMEM(tall, jnp.float32),
                pltpu.VMEM(tall, jnp.float32),
            ],
        ),
        out_shape=jax.ShapeDtypeStruct(shape, jnp.float32),
        compiler_params=params(),
        cost_estimate=cost(LANES * ages * ages * rank * 140, shape[0] * shape[1] * 4),
        name="covariance",
    )(places, *pieces)


def shards(groups, parts, estimates, factors, variances, intersection_tracts, intersection_weights):
    xs = groups // CORES
    ys = parts // DEPTH
    rows = estimates.shape[0]
    ages = variances.shape[1]
    rank = factors.shape[1] // ages
    geo = lax.axis_index("geo")
    dist = lax.axis_index("dist")
    x, core = geo // CORES, geo % CORES
    z, y = dist // ys, dist % ys

    def move(value, dx, dc, dy=0):
        if (dx, dc, dy) == (0, 0, 0):
            return value
        perm = []
        for g in range(groups):
            for d in range(parts):
                to = (g // CORES + dx) % xs * CORES + (g + dc) % CORES
                perm.append((g * parts + d, to * parts + d // ys * ys + (d + dy) % ys))
        return lax.ppermute(value, ("geo", "dist"), perm)

    def z_swap(value, bits):
        perm = [(a * ys + b, (a ^ bits) * ys + b) for a in range(DEPTH) for b in range(ys)]
        return lax.ppermute(value, "dist", perm)

    last_tile = jnp.pad(variances, ((0, 0), (0, -ages % LANES)))

    def half(array, c, *more):
        width = array.shape[1] // CORES
        return jnp.concatenate([lax.dynamic_slice(array, (0, c * width), (rows, width)), *more], axis=1)

    def start_of(group, tiles):
        return jnp.minimum(group * each_of(tiles), tiles - each_of(tiles))

    def each_of(tiles):
        return -(-tiles // xs)

    def exchange(array, *more):
        return [half(array, core, *more), move(half(array, (core + 1) % CORES, *more), 0, 1)]

    def along_x(both):
        tiles = both[0].shape[1] // LANES
        size = (rows, each_of(tiles) * LANES)

        def part(group):
            return jnp.concatenate([lax.dynamic_slice(b, (0, start_of(group, tiles) * LANES), size) for b in both], axis=0)

        cut = [part((x + dx) % xs) for dx in range(xs)]
        return [move(value, dx, 0) for dx, value in enumerate(cut)], cut[-1]

    load_both = exchange(factors, last_tile)
    load_x, load_cut = along_x(load_both)

    queries = jnp.concatenate([intersection_tracts.T, intersection_weights.T], axis=0)
    queries = after(queries, load_cut)
    queries = jnp.concatenate([queries, z_swap(queries, 2)], axis=1)
    queries = jnp.concatenate([queries, z_swap(queries, 1)], axis=1)
    bases = jnp.stack([
        (((x - dx) % xs * CORES + (core - dc) % CORES) * parts + z * ys + (y - dy) % ys) * rows
        for dy in range(ys) for dx in range(xs) for dc in range(CORES)
    ]).astype(jnp.int32)
    w = build_weights(bases, queries, rows)
    flag = (x == xs - 1).astype(jnp.int32).reshape(1)
    def along_y(value, first, count, *done):
        sent = after(value[:, first * LANES:(first + count) * LANES], *done)
        return [(value, first)] + [(move(sent, 0, 0, dy), 0) for dy in range(1, ys)]

    def later(by_y, tiles):
        return [(value, first + tiles) for value, first in by_y]

    def merge(by_x):
        return [by_y[dy] for dy in range(ys) for by_y in by_x]

    def along_z(data, count, has_var, before=(), before_middle=()):
        own, opposite, sent = partial_sums(flag, after(w, *before), data, count, has_var)
        near = z_swap(sent, 1)
        middle = combine(after(opposite, *before_middle), (near, 1))
        return own, near, middle, z_swap(middle, 2)

    def spread(own, near, far):
        mine = combine(own, (near, 0), (far, 0))
        along = [move(mine, dx, 0) for dx in range(xs)]
        return mine, [move(along[dx], 0, dc) for dx in range(xs) for dc in range(CORES)]

    def places(tiles):
        starts, lasts = [], []
        for dx in range(xs):
            for dc in range(CORES):
                group = (x - dx) % xs
                starts.append((core - dc) % CORES * tiles + start_of(group, tiles))
                lasts.append(group == xs - 1)
        return jnp.stack(starts + lasts).astype(jnp.int32)

    mean_width = estimates.shape[1] // LANES // CORES
    load_width = factors.shape[1] // LANES // CORES + 1
    load_tiles = split(each_of(load_width), LOAD_FIRST)
    mean_tiles = split(each_of(mean_width), MEAN_FIRST)
    (first_a, first_b), (first_c, first_d) = load_tiles, mean_tiles
    mean_x, _ = along_x(exchange(after(estimates, load_both[1])))
    load_y = along_y(load_x[0], 0, first_a + first_b)
    data_a = merge([load_y] + [along_y(value, 0, first_a, w) for value in load_x[1:]])
    data_b = merge([later(load_y, first_a)] + [along_y(value, first_a, first_b) for value in load_x[1:]])
    own_a, near_a, middle_a, far_a = along_z(data_a, first_a, False)
    mean_y = along_y(mean_x[0], 0, first_c + first_d, data_a[-1][0])
    there = data_b[-1][0]
    own_b, near_b, middle_b, far_b = along_z(data_b, first_b, True, (own_a,), (middle_a,))
    data_c = merge([mean_y] + [along_y(value, 0, first_c, there) for value in mean_x[1:]])
    data_d = merge([later(mean_y, first_c)] + [along_y(value, first_c, first_d, there) for value in mean_x[1:]])
    own_c, near_c, middle_c, far_c = along_z(data_c, first_c, False, (middle_b,))
    mine_a, load_a = spread(own_a, near_a, far_a)
    mine_b, load_b = spread(own_b, near_b, far_b)
    own_d, near_d, middle_d, far_d = along_z(data_d, first_d, False, (own_c, far_b), (load_a[-1], load_b[-1]))
    load_pieces = load_a + [after(load_b[0], middle_d)] + load_b[1:]
    cov = covariance(places(load_width), load_pieces, load_tiles, load_width * CORES, ages, rank)
    mine_c, mean_c = spread(after(own_c, cov), near_c, far_c)
    mine_d, mean_d = spread(after(own_d, cov), near_d, far_d)
    mean_pieces = mean_c + mean_d
    mean = marginal(places(mean_width), mean_pieces, mean_tiles, mean_width * CORES)
    return mean, cov.T


def solution(mesh):
    return jax.shard_map(
        functools.partial(shards, mesh.shape["geo"], mesh.shape["dist"]),
        mesh=mesh,
        in_specs=(
            P(("geo", "dist"), None),
            P(("geo", "dist"), None),
            P(("geo", "dist"), None),
            P("dist", None),
            P("dist", None),
        ),
        out_specs=(P("dist", None), P("dist", None)),
        check_vma=False,
    )
```

```python
import functools
import jax
import jax.numpy as jnp
from jax import lax
from jax.experimental import pallas as pl
from jax.experimental.pallas import tpu as pltpu
from jax.sharding import PartitionSpec as P

LANES = 128
CORES = 2
DEPTH = 4
LOAD_FIRST = 8
MEAN_FIRST = 8
SCALES = 16
TOP = 32767.0
VMEM_BYTES = 48 * 1024 * 1024
BEFORE = (((0,), (0,)), ((), ()))
AFTER = (((1,), (1,)), ((), ()))


def params():
    return pltpu.CompilerParams(vmem_limit_bytes=VMEM_BYTES)


def cost(flops, moved):
    return pl.CostEstimate(flops=flops, bytes_accessed=moved, transcendentals=0)


def after(value, *others):
    return lax.optimization_barrier((value, *others))[0]


def split(each, first):
    first = each // 2 if first >= each else first
    return (first, each - first)


def twice(value):
    return jnp.concatenate([value, value], axis=0)


def encode(src, src_base, dst, dst_base, height):
    half = height // 2
    powers = []
    for h in range(2):
        top = jnp.abs(src[pl.ds(src_base + h * half, 8), :])
        for r in range(8, half, 8):
            top = jnp.maximum(top, jnp.abs(src[pl.ds(src_base + h * half + r, 8), :]))
        power = jnp.floor(jnp.log2(jnp.maximum(top, 1e-30))) + 1.0
        gain = twice(jnp.exp2(-power) * TOP)
        for r in range(h * half, (h + 1) * half, 16):
            level = jnp.clip(jnp.round(src[pl.ds(src_base + r, 16), :] * gain), -TOP, TOP)
            dst[pl.ds(dst_base + r, 16), :] = level.astype(jnp.int32).astype(jnp.int16)
        powers.append(power)
    both = jnp.concatenate(powers, axis=0)
    dst[pl.ds(dst_base + height, SCALES), :] = both.astype(jnp.int32).astype(jnp.int16)


def steps_of(coded, base, height):
    power = coded[pl.ds(base + height, SCALES), :].astype(jnp.int32).astype(jnp.float32)
    step = jnp.exp2(power) * (1.0 / TOP)
    return [twice(step[:8]), twice(step[8:])]


def decode(coded, row, step):
    return coded[pl.ds(row, 16), :].astype(jnp.int32).astype(jnp.float32) * step


def weights_kernel(rows, base_ref, query_ref, out_ref):
    each = query_ref.shape[0] // 2
    row_id = lax.broadcasted_iota(jnp.int32, (16, LANES), 0)

    def piece(j, carry):
        for u in range(DEPTH):
            lanes = slice(u * LANES, (u + 1) * LANES)
            for r in range(0, rows, 16):
                tract = row_id + (base_ref[j] + r)
                total = jnp.zeros((16, LANES), jnp.float32)
                for k in range(each):
                    share = query_ref[each + k:each + k + 1, lanes].astype(jnp.float32) * (1.0 / 256.0)
                    total = jnp.where(query_ref[k:k + 1, lanes] == tract, share, total)
                where = pl.ds(pl.multiple_of(j * rows + r, 16), 16)
                out_ref[where, lanes] = total.astype(jnp.bfloat16)
        return carry

    lax.fori_loop(0, out_ref.shape[0] // rows, piece, 0)


def build_weights(bases, queries, rows):
    pieces = bases.shape[0]
    width = queries.shape[1]
    shape = (pieces * rows, width)
    return pl.pallas_call(
        functools.partial(weights_kernel, rows),
        grid_spec=pltpu.PrefetchScalarGridSpec(
            num_scalar_prefetch=1,
            grid=(1,),
            in_specs=[pl.BlockSpec(queries.shape, lambda i, s: (0, 0))],
            out_specs=pl.BlockSpec(shape, lambda i, s: (0, 0)),
        ),
        out_shape=jax.ShapeDtypeStruct(shape, jnp.bfloat16),
        compiler_params=params(),
        cost_estimate=cost(shape[0] * width * queries.shape[0] * 200, shape[0] * width * 2),
        name="build_weights",
    )(bases, queries)


def sums_kernel(offsets, has_var, flag_ref, w_ref, *refs):
    parts = len(offsets)
    data = refs[:parts]
    own_ref, opposite_ref, sent_ref, acc_ref = refs[parts:]
    columns = own_ref.shape[0]
    coded = columns + SCALES
    rows = [0]
    for d in data:
        rows.append(rows[-1] + d.shape[0])

    def weighted(get, t):
        total = None
        for j in range(parts):
            part = lax.dot_general(
                data[j][:, (offsets[j] + t) * LANES:(offsets[j] + t + 1) * LANES],
                get(w_ref[rows[j]:rows[j + 1], :]),
                BEFORE,
                preferred_element_type=jnp.float32,
            )
            total = part if total is None else total + part
        return total

    def put(t, value):
        where = slice(t * LANES, (t + 1) * LANES)
        for u, ref in enumerate((own_ref, opposite_ref, acc_ref.at[0], acc_ref.at[1])):
            ref[where, :] = value[:, u * LANES:(u + 1) * LANES]

    for t in range(columns // LANES):
        put(t, weighted(lambda w: w, t))

    if has_var:
        @pl.when(flag_ref[0] == 1)
        def _():
            def square(w):
                wide = w.astype(jnp.float32)
                return wide * wide

            def high(w):
                return square(w).astype(jnp.bfloat16)

            def low(w):
                s = square(w)
                return (s - s.astype(jnp.bfloat16).astype(jnp.float32)).astype(jnp.bfloat16)

            t = columns // LANES - 1
            put(t, weighted(high, t) + weighted(low, t))

    for u in range(2):
        encode(acc_ref.at[u], 0, sent_ref, u * coded, columns)


def partial_sums(flag, w, data, count, has_var):
    columns = count * LANES
    offsets = tuple(first for _, first in data)
    data = [array for array, _ in data]
    coded = columns + SCALES
    whole = lambda i, s: (0, 0)
    shapes = [
        jax.ShapeDtypeStruct((columns, LANES), jnp.float32),
        jax.ShapeDtypeStruct((columns, LANES), jnp.float32),
        jax.ShapeDtypeStruct((2 * coded, LANES), jnp.int16),
    ]
    return pl.pallas_call(
        functools.partial(sums_kernel, offsets, has_var),
        grid_spec=pltpu.PrefetchScalarGridSpec(
            num_scalar_prefetch=1,
            grid=(1,),
            in_specs=[pl.BlockSpec(w.shape, whole)] + [pl.BlockSpec(d.shape, whole) for d in data],
            out_specs=[pl.BlockSpec(s.shape, whole) for s in shapes],
            scratch_shapes=[pltpu.VMEM((2, columns, LANES), jnp.float32)],
        ),
        out_shape=shapes,
        compiler_params=params(),
        cost_estimate=cost(2 * w.shape[0] * w.shape[1] * columns, 2 * w.shape[0] * columns + columns * LANES * 10),
        name="partial_sums",
    )(flag, w, *data)


def combine_kernel(bases, own_ref, *refs):
    others, out_ref, acc_ref = refs[:-2], refs[-2], refs[-1]
    height = acc_ref.shape[0]
    steps = [steps_of(o, base, height) for o, base in zip(others, bases)]
    for r in range(0, height, 16):
        total = own_ref[r:r + 16, :]
        for o, base, step in zip(others, bases, steps):
            total = total + decode(o, base + r, step[r * 2 // height])
        acc_ref[r:r + 16, :] = total
    encode(acc_ref, 0, out_ref, 0, height)


def combine(own, *others):
    height = own.shape[0]
    shape = (height + SCALES, LANES)
    return pl.pallas_call(
        functools.partial(combine_kernel, [unit * shape[0] for _, unit in others]),
        out_shape=jax.ShapeDtypeStruct(shape, jnp.int16),
        scratch_shapes=[pltpu.VMEM((height, LANES), jnp.float32)],
        compiler_params=params(),
        cost_estimate=cost(height * LANES * 16, height * LANES * 12),
        name="combine",
    )(own, *[array for array, _ in others])


def each_piece(place_ref, pieces, tiles, do):
    groups = place_ref.shape[0] // 2
    for upper in (1, 0):
        for r in range(groups):
            @pl.when(place_ref[groups + r] == upper)
            def _(r=r):
                first = 0
                for c, count in enumerate(tiles):
                    do((place_ref[r] + first) * LANES, pieces[c * groups + r], count * LANES)
                    first += count


def marginal_kernel(tiles, place_ref, *refs):
    pieces, out_ref, tile_ref = refs[:-2], refs[-2], refs[-1]

    def do(start, piece, height):
        steps = steps_of(piece, 0, height)
        for t in range(0, height, LANES):
            for r in range(0, LANES, 16):
                tile_ref[r:r + 16, :] = decode(piece, t + r, steps[(t + r) * 2 // height])
            out_ref[:, pl.ds(pl.multiple_of(start + t, LANES), LANES)] = tile_ref[...].T

    each_piece(place_ref, pieces, tiles, do)


def marginal(places, pieces, tiles, total):
    shape = (LANES, total * LANES)
    return pl.pallas_call(
        functools.partial(marginal_kernel, tiles),
        grid_spec=pltpu.PrefetchScalarGridSpec(
            num_scalar_prefetch=1,
            grid=(1,),
            in_specs=[pl.BlockSpec(p.shape, lambda i, s: (0, 0)) for p in pieces],
            out_specs=pl.BlockSpec(shape, lambda i, s: (0, 0)),
            scratch_shapes=[pltpu.VMEM((LANES, LANES), jnp.float32)],
        ),
        out_shape=jax.ShapeDtypeStruct(shape, jnp.float32),
        compiler_params=params(),
        cost_estimate=cost(shape[0] * shape[1] * 4, shape[0] * shape[1] * 6),
        name="marginal",
    )(places, *pieces)


def covariance_kernel(tiles, total, ages, rank, place_ref, *refs):
    pieces, out_ref = refs[:-4], refs[-4]
    load_ref, age_ref, cov_ref = refs[-3:]
    pitch = -(-ages // 8) * 8
    left = lax.broadcasted_iota(jnp.int32, (LANES, LANES), 1) < rank

    def do(start, piece, height):
        steps = steps_of(piece, 0, height)
        for r in range(0, height, 16):
            load_ref[pl.ds(pl.multiple_of(start + r, 16), 16), :] = decode(piece, r, steps[r * 2 // height])

    each_piece(place_ref, pieces, tiles, do)

    def turn(t, carry):
        tile = t + t // (total // CORES - 1)
        value = load_ref[pl.ds(pl.multiple_of(tile * LANES, LANES), LANES), :].T
        swapped = pltpu.roll(value, rank, 1)
        age_ref[pl.ds(2 * t, LANES, stride=pitch), :] = jnp.where(left, value, swapped)
        age_ref[pl.ds(2 * t + 1, LANES, stride=pitch), :] = jnp.where(left, swapped, value)
        return carry

    lax.fori_loop(0, ages * rank // LANES, turn, 0, unroll=True)

    def outer(d, carry):
        start = pl.multiple_of(d * pitch, 8)
        mine = age_ref[pl.ds(start, LANES), :]
        high = mine.astype(jnp.bfloat16).astype(jnp.float32)
        low = mine - high
        mixed = jnp.where(left, high, low).astype(jnp.bfloat16)
        product = lax.dot_general(
            jnp.concatenate([mixed, mixed], axis=1),
            jnp.concatenate([high.astype(jnp.bfloat16), low.astype(jnp.bfloat16)], axis=1),
            AFTER,
            preferred_element_type=jnp.float32,
        )
        cov_ref[pl.ds(start, pitch), :] = product[:pitch]
        return carry

    lax.fori_loop(0, LANES, outer, 0, unroll=16)

    def store(m, carry):
        base = pl.multiple_of(m * (2 * ages), 8)
        for p in range(2):
            value = cov_ref[pl.ds(2 * m + p, LANES, stride=pitch), :].T
            out_ref[pl.ds(base + p * ages, ages), :] = value[:ages]
        return carry

    lax.fori_loop(0, ages // 2, store, 0, unroll=True)
    for i in range(ages):
        row = i * (ages + 1)
        out_ref[row:row + 1, :] += load_ref[(total - 1) * LANES + i:(total - 1) * LANES + i + 1, :]


def covariance(places, pieces, tiles, total, ages, rank):
    pitch = -(-ages // 8) * 8
    shape = (ages * ages, LANES)
    tall = (LANES * pitch + LANES - pitch, LANES)
    return pl.pallas_call(
        functools.partial(covariance_kernel, tiles, total, ages, rank),
        grid_spec=pltpu.PrefetchScalarGridSpec(
            num_scalar_prefetch=1,
            grid=(1,),
            in_specs=[pl.BlockSpec(p.shape, lambda i, s: (0, 0)) for p in pieces],
            out_specs=pl.BlockSpec(shape, lambda i, s: (0, 0)),
            scratch_shapes=[
                pltpu.VMEM((total * LANES, LANES), jnp.float32),
                pltpu.VMEM(tall, jnp.float32),
                pltpu.VMEM(tall, jnp.float32),
            ],
        ),
        out_shape=jax.ShapeDtypeStruct(shape, jnp.float32),
        compiler_params=params(),
        cost_estimate=cost(LANES * ages * ages * rank * 140, shape[0] * shape[1] * 4),
        name="covariance",
    )(places, *pieces)


def shards(groups, parts, estimates, factors, variances, intersection_tracts, intersection_weights):
    xs = groups // CORES
    ys = parts // DEPTH
    rows = estimates.shape[0]
    ages = variances.shape[1]
    rank = factors.shape[1] // ages
    geo = lax.axis_index("geo")
    dist = lax.axis_index("dist")
    x, core = geo // CORES, geo % CORES
    z, y = dist // ys, dist % ys

    def move(value, dx, dc, dy=0):
        if (dx, dc, dy) == (0, 0, 0):
            return value
        perm = []
        for g in range(groups):
            for d in range(parts):
                to = (g // CORES + dx) % xs * CORES + (g + dc) % CORES
                perm.append((g * parts + d, to * parts + d // ys * ys + (d + dy) % ys))
        return lax.ppermute(value, ("geo", "dist"), perm)

    def z_swap(value, bits):
        perm = [(a * ys + b, (a ^ bits) * ys + b) for a in range(DEPTH) for b in range(ys)]
        return lax.ppermute(value, "dist", perm)

    last_tile = jnp.pad(variances, ((0, 0), (0, -ages % LANES)))

    def half(array, c, *more):
        width = array.shape[1] // CORES
        return jnp.concatenate([lax.dynamic_slice(array, (0, c * width), (rows, width)), *more], axis=1)

    def start_of(group, tiles):
        return jnp.minimum(group * each_of(tiles), tiles - each_of(tiles))

    def each_of(tiles):
        return -(-tiles // xs)

    def exchange(array, *more):
        return [half(array, core, *more), move(half(array, (core + 1) % CORES, *more), 0, 1)]

    def along_x(both):
        tiles = both[0].shape[1] // LANES
        size = (rows, each_of(tiles) * LANES)

        def part(group):
            return jnp.concatenate([lax.dynamic_slice(b, (0, start_of(group, tiles) * LANES), size) for b in both], axis=0)

        cut = [part((x + dx) % xs) for dx in range(xs)]
        return [move(value, dx, 0) for dx, value in enumerate(cut)], cut[-1]

    load_both = exchange(factors, last_tile)
    load_x, load_cut = along_x(load_both)

    queries = jnp.concatenate([intersection_tracts.T, intersection_weights.T], axis=0)
    queries = after(queries, load_cut)
    queries = jnp.concatenate([queries, z_swap(queries, 2)], axis=1)
    queries = jnp.concatenate([queries, z_swap(queries, 1)], axis=1)
    bases = jnp.stack([
        (((x - dx) % xs * CORES + (core - dc) % CORES) * parts + z * ys + (y - dy) % ys) * rows
        for dy in range(ys) for dx in range(xs) for dc in range(CORES)
    ]).astype(jnp.int32)
    w = build_weights(bases, queries, rows)
    flag = (x == xs - 1).astype(jnp.int32).reshape(1)
    def along_y(value, first, count, *done):
        sent = after(value[:, first * LANES:(first + count) * LANES], *done)
        return [(value, first)] + [(move(sent, 0, 0, dy), 0) for dy in range(1, ys)]

    def later(by_y, tiles):
        return [(value, first + tiles) for value, first in by_y]

    def merge(by_x):
        return [by_y[dy] for dy in range(ys) for by_y in by_x]

    def along_z(data, count, has_var, before=(), before_middle=()):
        own, opposite, sent = partial_sums(flag, after(w, *before), data, count, has_var)
        near = z_swap(sent, 1)
        middle = combine(after(opposite, *before_middle), (near, 1))
        return own, near, middle, z_swap(middle, 2)

    def spread(own, near, far):
        mine = combine(own, (near, 0), (far, 0))
        along = [move(mine, dx, 0) for dx in range(xs)]
        return mine, [move(along[dx], 0, dc) for dx in range(xs) for dc in range(CORES)]

    def places(tiles):
        starts, lasts = [], []
        for dx in range(xs):
            for dc in range(CORES):
                group = (x - dx) % xs
                starts.append((core - dc) % CORES * tiles + start_of(group, tiles))
                lasts.append(group == xs - 1)
        return jnp.stack(starts + lasts).astype(jnp.int32)

    mean_width = estimates.shape[1] // LANES // CORES
    load_width = factors.shape[1] // LANES // CORES + 1
    load_tiles = split(each_of(load_width), LOAD_FIRST)
    mean_tiles = split(each_of(mean_width), MEAN_FIRST)
    (first_a, first_b), (first_c, first_d) = load_tiles, mean_tiles
    mean_x, _ = along_x(exchange(after(estimates, load_both[1])))
    load_y = along_y(load_x[0], 0, first_a + first_b)
    data_a = merge([load_y] + [along_y(value, 0, first_a, w) for value in load_x[1:]])
    data_b = merge([later(load_y, first_a)] + [along_y(value, first_a, first_b) for value in load_x[1:]])
    own_a, near_a, middle_a, far_a = along_z(data_a, first_a, False)
    mean_y = along_y(mean_x[0], 0, first_c + first_d, data_a[-1][0])
    there = data_b[-1][0]
    own_b, near_b, middle_b, far_b = along_z(data_b, first_b, True, (own_a,), (middle_a,))
    data_c = merge([mean_y] + [along_y(value, 0, first_c, there) for value in mean_x[1:]])
    data_d = merge([later(mean_y, first_c)] + [along_y(value, first_c, first_d, there) for value in mean_x[1:]])
    own_c, near_c, middle_c, far_c = along_z(data_c, first_c, False, (middle_b, far_a))
    mine_a, load_a = spread(own_a, near_a, far_a)
    own_d, opposite_d, sent_d = partial_sums(flag, after(w, own_c), data_d, first_d, False)
    near_d = z_swap(sent_d, 1)
    mine_b, load_b = spread(after(own_b, own_d), near_b, far_b)
    load_pieces = load_a + [after(load_b[0], middle_c, own_d)] + load_b[1:]
    cov = covariance(places(load_width), load_pieces, load_tiles, load_width * CORES, ages, rank)
    far_d = z_swap(combine(after(opposite_d, cov), (near_d, 1)), 2)
    mine_c, mean_c = spread(after(own_c, cov), near_c, far_c)
    mine_d, mean_d = spread(own_d, near_d, far_d)
    mean_pieces = mean_c + mean_d
    mean = marginal(places(mean_width), mean_pieces, mean_tiles, mean_width * CORES)
    return mean, cov.T


def solution(mesh):
    return jax.shard_map(
        functools.partial(shards, mesh.shape["geo"], mesh.shape["dist"]),
        mesh=mesh,
        in_specs=(
            P(("geo", "dist"), None),
            P(("geo", "dist"), None),
            P(("geo", "dist"), None),
            P("dist", None),
            P("dist", None),
        ),
        out_specs=(P("dist", None), P("dist", None)),
        check_vma=False,
    )
```

```python
import functools
import jax
import jax.numpy as jnp
from jax import lax
from jax.experimental import pallas as pl
from jax.experimental.pallas import tpu as pltpu
from jax.sharding import PartitionSpec as P

LANES = 128
CORES = 2
DEPTH = 4
LOAD_FIRST = 8
MEAN_FIRST = 8
SCALES = 16
TOP = 32767.0
VMEM_BYTES = 48 * 1024 * 1024
BEFORE = (((0,), (0,)), ((), ()))
AFTER = (((1,), (1,)), ((), ()))


def params():
    return pltpu.CompilerParams(vmem_limit_bytes=VMEM_BYTES)


def cost(flops, moved):
    return pl.CostEstimate(flops=flops, bytes_accessed=moved, transcendentals=0)


def after(value, *others):
    return lax.optimization_barrier((value, *others))[0]


def split(each, first):
    first = each // 2 if first >= each else first
    return (first, each - first)


def twice(value):
    return jnp.concatenate([value, value], axis=0)


def encode(src, src_base, dst, dst_base, height):
    half = height // 2
    powers = []
    for h in range(2):
        top = jnp.abs(src[pl.ds(src_base + h * half, 8), :])
        for r in range(8, half, 8):
            top = jnp.maximum(top, jnp.abs(src[pl.ds(src_base + h * half + r, 8), :]))
        power = jnp.floor(jnp.log2(jnp.maximum(top, 1e-30))) + 1.0
        gain = twice(jnp.exp2(-power) * TOP)
        for r in range(h * half, (h + 1) * half, 16):
            level = jnp.clip(jnp.round(src[pl.ds(src_base + r, 16), :] * gain), -TOP, TOP)
            dst[pl.ds(dst_base + r, 16), :] = level.astype(jnp.int32).astype(jnp.int16)
        powers.append(power)
    both = jnp.concatenate(powers, axis=0)
    dst[pl.ds(dst_base + height, SCALES), :] = both.astype(jnp.int32).astype(jnp.int16)


def steps_of(coded, base, height):
    power = coded[pl.ds(base + height, SCALES), :].astype(jnp.int32).astype(jnp.float32)
    step = jnp.exp2(power) * (1.0 / TOP)
    return [twice(step[:8]), twice(step[8:])]


def decode(coded, row, step):
    return coded[pl.ds(row, 16), :].astype(jnp.int32).astype(jnp.float32) * step


def weights_kernel(rows, base_ref, query_ref, out_ref):
    each = query_ref.shape[0] // 2
    row_id = lax.broadcasted_iota(jnp.int32, (16, LANES), 0)

    def piece(j, carry):
        for u in range(DEPTH):
            lanes = slice(u * LANES, (u + 1) * LANES)
            for r in range(0, rows, 16):
                tract = row_id + (base_ref[j] + r)
                total = jnp.zeros((16, LANES), jnp.float32)
                for k in range(each):
                    share = query_ref[each + k:each + k + 1, lanes].astype(jnp.float32) * (1.0 / 256.0)
                    total = jnp.where(query_ref[k:k + 1, lanes] == tract, share, total)
                where = pl.ds(pl.multiple_of(j * rows + r, 16), 16)
                out_ref[where, lanes] = total.astype(jnp.bfloat16)
        return carry

    lax.fori_loop(0, out_ref.shape[0] // rows, piece, 0)


def build_weights(bases, queries, rows):
    pieces = bases.shape[0]
    width = queries.shape[1]
    shape = (pieces * rows, width)
    return pl.pallas_call(
        functools.partial(weights_kernel, rows),
        grid_spec=pltpu.PrefetchScalarGridSpec(
            num_scalar_prefetch=1,
            grid=(1,),
            in_specs=[pl.BlockSpec(queries.shape, lambda i, s: (0, 0))],
            out_specs=pl.BlockSpec(shape, lambda i, s: (0, 0)),
        ),
        out_shape=jax.ShapeDtypeStruct(shape, jnp.bfloat16),
        compiler_params=params(),
        cost_estimate=cost(shape[0] * width * queries.shape[0] * 200, shape[0] * width * 2),
        name="build_weights",
    )(bases, queries)


def sums_kernel(offsets, has_var, flag_ref, w_ref, *refs):
    parts = len(offsets)
    data = refs[:parts]
    own_ref, opposite_ref, sent_ref, acc_ref = refs[parts:]
    columns = own_ref.shape[0]
    coded = columns + SCALES
    rows = [0]
    for d in data:
        rows.append(rows[-1] + d.shape[0])

    def weighted(get, t):
        total = None
        for j in range(parts):
            part = lax.dot_general(
                data[j][:, (offsets[j] + t) * LANES:(offsets[j] + t + 1) * LANES],
                get(w_ref[rows[j]:rows[j + 1], :]),
                BEFORE,
                preferred_element_type=jnp.float32,
            )
            total = part if total is None else total + part
        return total

    def put(t, value):
        where = slice(t * LANES, (t + 1) * LANES)
        for u, ref in enumerate((own_ref, opposite_ref, acc_ref.at[0], acc_ref.at[1])):
            ref[where, :] = value[:, u * LANES:(u + 1) * LANES]

    for t in range(columns // LANES):
        put(t, weighted(lambda w: w, t))

    if has_var:
        @pl.when(flag_ref[0] == 1)
        def _():
            def square(w):
                wide = w.astype(jnp.float32)
                return wide * wide

            def high(w):
                return square(w).astype(jnp.bfloat16)

            def low(w):
                s = square(w)
                return (s - s.astype(jnp.bfloat16).astype(jnp.float32)).astype(jnp.bfloat16)

            t = columns // LANES - 1
            put(t, weighted(high, t) + weighted(low, t))

    for u in range(2):
        encode(acc_ref.at[u], 0, sent_ref, u * coded, columns)


def partial_sums(flag, w, data, count, has_var):
    columns = count * LANES
    offsets = tuple(first for _, first in data)
    data = [array for array, _ in data]
    coded = columns + SCALES
    whole = lambda i, s: (0, 0)
    shapes = [
        jax.ShapeDtypeStruct((columns, LANES), jnp.float32),
        jax.ShapeDtypeStruct((columns, LANES), jnp.float32),
        jax.ShapeDtypeStruct((2 * coded, LANES), jnp.int16),
    ]
    return pl.pallas_call(
        functools.partial(sums_kernel, offsets, has_var),
        grid_spec=pltpu.PrefetchScalarGridSpec(
            num_scalar_prefetch=1,
            grid=(1,),
            in_specs=[pl.BlockSpec(w.shape, whole)] + [pl.BlockSpec(d.shape, whole) for d in data],
            out_specs=[pl.BlockSpec(s.shape, whole) for s in shapes],
            scratch_shapes=[pltpu.VMEM((2, columns, LANES), jnp.float32)],
        ),
        out_shape=shapes,
        compiler_params=params(),
        cost_estimate=cost(2 * w.shape[0] * w.shape[1] * columns, 2 * w.shape[0] * columns + columns * LANES * 10),
        name="partial_sums",
    )(flag, w, *data)


def combine_kernel(bases, own_ref, *refs):
    others, out_ref, acc_ref = refs[:-2], refs[-2], refs[-1]
    height = acc_ref.shape[0]
    steps = [steps_of(o, base, height) for o, base in zip(others, bases)]
    for r in range(0, height, 16):
        total = own_ref[r:r + 16, :]
        for o, base, step in zip(others, bases, steps):
            total = total + decode(o, base + r, step[r * 2 // height])
        acc_ref[r:r + 16, :] = total
    encode(acc_ref, 0, out_ref, 0, height)


def combine(own, *others):
    height = own.shape[0]
    shape = (height + SCALES, LANES)
    return pl.pallas_call(
        functools.partial(combine_kernel, [unit * shape[0] for _, unit in others]),
        out_shape=jax.ShapeDtypeStruct(shape, jnp.int16),
        scratch_shapes=[pltpu.VMEM((height, LANES), jnp.float32)],
        compiler_params=params(),
        cost_estimate=cost(height * LANES * 16, height * LANES * 12),
        name="combine",
    )(own, *[array for array, _ in others])


def each_piece(place_ref, pieces, tiles, do):
    groups = place_ref.shape[0] // 2
    for upper in (1, 0):
        for r in range(groups):
            @pl.when(place_ref[groups + r] == upper)
            def _(r=r):
                first = 0
                for c, count in enumerate(tiles):
                    do((place_ref[r] + first) * LANES, pieces[c * groups + r], count * LANES)
                    first += count


def marginal_kernel(tiles, place_ref, *refs):
    pieces, out_ref, tile_ref = refs[:-2], refs[-2], refs[-1]

    def do(start, piece, height):
        steps = steps_of(piece, 0, height)
        for t in range(0, height, LANES):
            for r in range(0, LANES, 16):
                tile_ref[r:r + 16, :] = decode(piece, t + r, steps[(t + r) * 2 // height])
            out_ref[:, pl.ds(pl.multiple_of(start + t, LANES), LANES)] = tile_ref[...].T

    each_piece(place_ref, pieces, tiles, do)


def marginal(places, pieces, tiles, total):
    shape = (LANES, total * LANES)
    return pl.pallas_call(
        functools.partial(marginal_kernel, tiles),
        grid_spec=pltpu.PrefetchScalarGridSpec(
            num_scalar_prefetch=1,
            grid=(1,),
            in_specs=[pl.BlockSpec(p.shape, lambda i, s: (0, 0)) for p in pieces],
            out_specs=pl.BlockSpec(shape, lambda i, s: (0, 0)),
            scratch_shapes=[pltpu.VMEM((LANES, LANES), jnp.float32)],
        ),
        out_shape=jax.ShapeDtypeStruct(shape, jnp.float32),
        compiler_params=params(),
        cost_estimate=cost(shape[0] * shape[1] * 4, shape[0] * shape[1] * 6),
        name="marginal",
    )(places, *pieces)


def covariance_kernel(tiles, total, ages, rank, place_ref, *refs):
    pieces, out_ref = refs[:-4], refs[-4]
    load_ref, age_ref, cov_ref = refs[-3:]
    pitch = -(-ages // 8) * 8
    left = lax.broadcasted_iota(jnp.int32, (LANES, LANES), 1) < rank

    def do(start, piece, height):
        steps = steps_of(piece, 0, height)
        for r in range(0, height, 16):
            load_ref[pl.ds(pl.multiple_of(start + r, 16), 16), :] = decode(piece, r, steps[r * 2 // height])

    each_piece(place_ref, pieces, tiles, do)

    def turn(t, carry):
        tile = t + t // (total // CORES - 1)
        value = load_ref[pl.ds(pl.multiple_of(tile * LANES, LANES), LANES), :].T
        swapped = pltpu.roll(value, rank, 1)
        age_ref[pl.ds(2 * t, LANES, stride=pitch), :] = jnp.where(left, value, swapped)
        age_ref[pl.ds(2 * t + 1, LANES, stride=pitch), :] = jnp.where(left, swapped, value)
        return carry

    lax.fori_loop(0, ages * rank // LANES, turn, 0, unroll=True)

    def outer(d, carry):
        start = pl.multiple_of(d * pitch, 8)
        mine = age_ref[pl.ds(start, LANES), :]
        high = mine.astype(jnp.bfloat16).astype(jnp.float32)
        low = mine - high
        mixed = jnp.where(left, high, low).astype(jnp.bfloat16)
        product = lax.dot_general(
            jnp.concatenate([mixed, mixed], axis=1),
            jnp.concatenate([high.astype(jnp.bfloat16), low.astype(jnp.bfloat16)], axis=1),
            AFTER,
            preferred_element_type=jnp.float32,
        )
        cov_ref[pl.ds(start, pitch), :] = product[:pitch]
        return carry

    lax.fori_loop(0, LANES, outer, 0, unroll=16)

    def store(m, carry):
        base = pl.multiple_of(m * (2 * ages), 8)
        for p in range(2):
            value = cov_ref[pl.ds(2 * m + p, LANES, stride=pitch), :].T
            out_ref[pl.ds(base + p * ages, ages), :] = value[:ages]
        return carry

    lax.fori_loop(0, ages // 2, store, 0, unroll=True)
    for i in range(ages):
        row = i * (ages + 1)
        out_ref[row:row + 1, :] += load_ref[(total - 1) * LANES + i:(total - 1) * LANES + i + 1, :]


def covariance(places, pieces, tiles, total, ages, rank):
    pitch = -(-ages // 8) * 8
    shape = (ages * ages, LANES)
    tall = (LANES * pitch + LANES - pitch, LANES)
    return pl.pallas_call(
        functools.partial(covariance_kernel, tiles, total, ages, rank),
        grid_spec=pltpu.PrefetchScalarGridSpec(
            num_scalar_prefetch=1,
            grid=(1,),
            in_specs=[pl.BlockSpec(p.shape, lambda i, s: (0, 0)) for p in pieces],
            out_specs=pl.BlockSpec(shape, lambda i, s: (0, 0)),
            scratch_shapes=[
                pltpu.VMEM((total * LANES, LANES), jnp.float32),
                pltpu.VMEM(tall, jnp.float32),
                pltpu.VMEM(tall, jnp.float32),
            ],
        ),
        out_shape=jax.ShapeDtypeStruct(shape, jnp.float32),
        compiler_params=params(),
        cost_estimate=cost(LANES * ages * ages * rank * 16, shape[0] * shape[1] * 4),
        name="covariance",
    )(places, *pieces)


def shards(groups, parts, estimates, factors, variances, intersection_tracts, intersection_weights):
    xs = groups // CORES
    ys = parts // DEPTH
    rows = estimates.shape[0]
    ages = variances.shape[1]
    rank = factors.shape[1] // ages
    geo = lax.axis_index("geo")
    dist = lax.axis_index("dist")
    x, core = geo // CORES, geo % CORES
    z, y = dist // ys, dist % ys

    def move(value, dx, dc, dy=0):
        if (dx, dc, dy) == (0, 0, 0):
            return value
        perm = []
        for g in range(groups):
            for d in range(parts):
                to = (g // CORES + dx) % xs * CORES + (g + dc) % CORES
                perm.append((g * parts + d, to * parts + d // ys * ys + (d + dy) % ys))
        return lax.ppermute(value, ("geo", "dist"), perm)

    def z_swap(value, bits):
        perm = [(a * ys + b, (a ^ bits) * ys + b) for a in range(DEPTH) for b in range(ys)]
        return lax.ppermute(value, "dist", perm)

    last_tile = jnp.pad(variances, ((0, 0), (0, -ages % LANES)))

    def half(array, c, *more):
        width = array.shape[1] // CORES
        return jnp.concatenate([lax.dynamic_slice(array, (0, c * width), (rows, width)), *more], axis=1)

    def start_of(group, tiles):
        return jnp.minimum(group * each_of(tiles), tiles - each_of(tiles))

    def each_of(tiles):
        return -(-tiles // xs)

    def exchange(array, *more):
        return [half(array, core, *more), move(half(array, (core + 1) % CORES, *more), 0, 1)]

    def along_x(both, first, count):
        tiles = both[0].shape[1] // LANES
        size = (rows, count * LANES)

        def part(group):
            start = (start_of(group, tiles) + first) * LANES
            return jnp.concatenate([lax.dynamic_slice(b, (0, start), size) for b in both], axis=0)

        cut = [part((x + dx) % xs) for dx in range(xs)]
        return [move(value, dx, 0) for dx, value in enumerate(cut)], cut[-1]

    load_both = exchange(factors, last_tile)
    load_tiles = split(each_of(load_both[0].shape[1] // LANES), LOAD_FIRST)
    xa, cut_a = along_x(load_both, 0, load_tiles[0])
    xb, _ = along_x(load_both, *load_tiles)

    queries = jnp.concatenate([intersection_tracts.T, intersection_weights.T], axis=0)
    queries = after(queries, cut_a)
    queries = jnp.concatenate([queries, z_swap(queries, 2)], axis=1)
    queries = jnp.concatenate([queries, z_swap(queries, 1)], axis=1)
    bases = jnp.stack([
        (((x - dx) % xs * CORES + (core - dc) % CORES) * parts + z * ys + (y - dy) % ys) * rows
        for dy in range(ys) for dx in range(xs) for dc in range(CORES)
    ]).astype(jnp.int32)
    w = build_weights(bases, queries, rows)
    flag = (x == xs - 1).astype(jnp.int32).reshape(1)
    def along_y(value, first, count, *done):
        sent = after(value[:, first * LANES:(first + count) * LANES], *done)
        return [(value, first)] + [(move(sent, 0, 0, dy), 0) for dy in range(1, ys)]

    def later(by_y, tiles):
        return [(value, first + tiles) for value, first in by_y]

    def merge(by_x):
        return [by_y[dy] for dy in range(ys) for by_y in by_x]

    def along_z(data, count, has_var, before=(), before_middle=()):
        own, opposite, sent = partial_sums(flag, after(w, *before), data, count, has_var)
        near = z_swap(sent, 1)
        middle = combine(after(opposite, *before_middle), (near, 1))
        return own, near, middle, z_swap(middle, 2)

    def spread(own, near, far):
        mine = combine(own, (near, 0), (far, 0))
        along = [move(mine, dx, 0) for dx in range(xs)]
        return mine, [move(along[dx], 0, dc) for dx in range(xs) for dc in range(CORES)]

    def places(tiles):
        starts, lasts = [], []
        for dx in range(xs):
            for dc in range(CORES):
                group = (x - dx) % xs
                starts.append((core - dc) % CORES * tiles + start_of(group, tiles))
                lasts.append(group == xs - 1)
        return jnp.stack(starts + lasts).astype(jnp.int32)

    mean_width = estimates.shape[1] // LANES // CORES
    load_width = factors.shape[1] // LANES // CORES + 1
    mean_tiles = split(each_of(mean_width), MEAN_FIRST)
    (first_a, first_b), (first_c, first_d) = load_tiles, mean_tiles
    mean_x, _ = along_x(exchange(after(estimates, load_both[1])), 0, first_c + first_d)
    data_a = merge([along_y(xa[0], 0, first_a)] + [along_y(value, 0, first_a, w) for value in xa[1:]])
    data_b = merge([along_y(value, 0, first_b, xa[-1]) for value in xb])
    own_a, near_a, middle_a, far_a = along_z(data_a, first_a, False)
    mean_y = along_y(mean_x[0], 0, first_c + first_d, data_a[-1][0])
    there = data_b[-1][0]
    own_b, near_b, middle_b, far_b = along_z(data_b, first_b, True, (own_a,), (middle_a,))
    data_c = merge([mean_y] + [along_y(value, 0, first_c, there) for value in mean_x[1:]])
    data_d = merge([later(mean_y, first_c)] + [along_y(value, first_c, first_d, there) for value in mean_x[1:]])
    own_c, near_c, middle_c, far_c = along_z(data_c, first_c, False, (middle_b, far_a))
    mine_a, load_a = spread(own_a, near_a, far_a)
    own_d, opposite_d, sent_d = partial_sums(flag, after(w, own_c), data_d, first_d, False)
    near_d = z_swap(sent_d, 1)
    mine_b, load_b = spread(after(own_b, own_d), near_b, far_b)
    load_pieces = load_a + [after(load_b[0], middle_c, own_d)] + load_b[1:]
    cov = covariance(places(load_width), load_pieces, load_tiles, load_width * CORES, ages, rank)
    far_d = z_swap(combine(after(opposite_d, cov), (near_d, 1)), 2)
    mine_c, mean_c = spread(after(own_c, cov), near_c, far_c)
    mine_d, mean_d = spread(own_d, near_d, far_d)
    mean_pieces = mean_c + mean_d
    mean = marginal(places(mean_width), mean_pieces, mean_tiles, mean_width * CORES)
    return mean, cov.T


def solution(mesh):
    return jax.shard_map(
        functools.partial(shards, mesh.shape["geo"], mesh.shape["dist"]),
        mesh=mesh,
        in_specs=(
            P(("geo", "dist"), None),
            P(("geo", "dist"), None),
            P(("geo", "dist"), None),
            P("dist", None),
            P("dist", None),
        ),
        out_specs=(P("dist", None), P("dist", None)),
        check_vma=False,
    )
```

```python
import functools
import jax
import jax.numpy as jnp
from jax import lax
from jax.experimental import pallas as pl
from jax.experimental.pallas import tpu as pltpu
from jax.sharding import PartitionSpec as P

LANES = 128
CORES = 2
DEPTH = 4
LOAD_FIRST = 8
MEAN_FIRST = 8
SCALES = 16
TOP = 32767.0
VMEM_BYTES = 48 * 1024 * 1024
BEFORE = (((0,), (0,)), ((), ()))
AFTER = (((1,), (1,)), ((), ()))


def params():
    return pltpu.CompilerParams(vmem_limit_bytes=VMEM_BYTES)


def cost(flops, moved):
    return pl.CostEstimate(flops=flops, bytes_accessed=moved, transcendentals=0)


def after(value, *others):
    return lax.optimization_barrier((value, *others))[0]


def split(each, first):
    first = each // 2 if first >= each else first
    return (first, each - first)


def twice(value):
    return jnp.concatenate([value, value], axis=0)


def encode(src, src_base, dst, dst_base, height):
    half = height // 2
    powers = []
    for h in range(2):
        top = jnp.abs(src[pl.ds(src_base + h * half, 8), :])
        for r in range(8, half, 8):
            top = jnp.maximum(top, jnp.abs(src[pl.ds(src_base + h * half + r, 8), :]))
        power = jnp.floor(jnp.log2(jnp.maximum(top, 1e-30))) + 1.0
        gain = twice(jnp.exp2(-power) * TOP)
        for r in range(h * half, (h + 1) * half, 16):
            level = jnp.clip(jnp.round(src[pl.ds(src_base + r, 16), :] * gain), -TOP, TOP)
            dst[pl.ds(dst_base + r, 16), :] = level.astype(jnp.int32).astype(jnp.int16)
        powers.append(power)
    both = jnp.concatenate(powers, axis=0)
    dst[pl.ds(dst_base + height, SCALES), :] = both.astype(jnp.int32).astype(jnp.int16)


def steps_of(coded, base, height):
    power = coded[pl.ds(base + height, SCALES), :].astype(jnp.int32).astype(jnp.float32)
    step = jnp.exp2(power) * (1.0 / TOP)
    return [twice(step[:8]), twice(step[8:])]


def decode(coded, row, step):
    return coded[pl.ds(row, 16), :].astype(jnp.int32).astype(jnp.float32) * step


def weights_kernel(rows, base_ref, query_ref, out_ref):
    each = query_ref.shape[0] // 2
    row_id = lax.broadcasted_iota(jnp.int32, (16, LANES), 0)

    def piece(j, carry):
        for u in range(DEPTH):
            lanes = slice(u * LANES, (u + 1) * LANES)
            for r in range(0, rows, 16):
                tract = row_id + (base_ref[j] + r)
                total = jnp.zeros((16, LANES), jnp.float32)
                for k in range(each):
                    share = query_ref[each + k:each + k + 1, lanes].astype(jnp.float32) * (1.0 / 256.0)
                    total = jnp.where(query_ref[k:k + 1, lanes] == tract, share, total)
                where = pl.ds(pl.multiple_of(j * rows + r, 16), 16)
                out_ref[where, lanes] = total.astype(jnp.bfloat16)
        return carry

    lax.fori_loop(0, out_ref.shape[0] // rows, piece, 0)


def build_weights(bases, queries, rows):
    pieces = bases.shape[0]
    width = queries.shape[1]
    shape = (pieces * rows, width)
    return pl.pallas_call(
        functools.partial(weights_kernel, rows),
        grid_spec=pltpu.PrefetchScalarGridSpec(
            num_scalar_prefetch=1,
            grid=(1,),
            in_specs=[pl.BlockSpec(queries.shape, lambda i, s: (0, 0))],
            out_specs=pl.BlockSpec(shape, lambda i, s: (0, 0)),
        ),
        out_shape=jax.ShapeDtypeStruct(shape, jnp.bfloat16),
        compiler_params=params(),
        cost_estimate=cost(shape[0] * width * queries.shape[0] * 200, shape[0] * width * 2),
        name="build_weights",
    )(bases, queries)


def sums_kernel(offsets, has_var, flag_ref, w_ref, *refs):
    parts = len(offsets)
    data = refs[:parts]
    own_ref, opposite_ref, sent_ref, acc_ref = refs[parts:]
    columns = own_ref.shape[0]
    coded = columns + SCALES
    rows = [0]
    for d in data:
        rows.append(rows[-1] + d.shape[0])

    def weighted(get, t):
        total = None
        for j in range(parts):
            part = lax.dot_general(
                data[j][:, (offsets[j] + t) * LANES:(offsets[j] + t + 1) * LANES],
                get(w_ref[rows[j]:rows[j + 1], :]),
                BEFORE,
                preferred_element_type=jnp.float32,
            )
            total = part if total is None else total + part
        return total

    def put(t, value):
        where = slice(t * LANES, (t + 1) * LANES)
        for u, ref in enumerate((own_ref, opposite_ref, acc_ref.at[0], acc_ref.at[1])):
            ref[where, :] = value[:, u * LANES:(u + 1) * LANES]

    for t in range(columns // LANES):
        put(t, weighted(lambda w: w, t))

    if has_var:
        @pl.when(flag_ref[0] == 1)
        def _():
            def square(w):
                wide = w.astype(jnp.float32)
                return wide * wide

            def high(w):
                return square(w).astype(jnp.bfloat16)

            def low(w):
                s = square(w)
                return (s - s.astype(jnp.bfloat16).astype(jnp.float32)).astype(jnp.bfloat16)

            t = columns // LANES - 1
            put(t, weighted(high, t) + weighted(low, t))

    for u in range(2):
        encode(acc_ref.at[u], 0, sent_ref, u * coded, columns)


def partial_sums(flag, w, data, count, has_var):
    columns = count * LANES
    offsets = tuple(first for _, first in data)
    data = [array for array, _ in data]
    coded = columns + SCALES
    whole = lambda i, s: (0, 0)
    shapes = [
        jax.ShapeDtypeStruct((columns, LANES), jnp.float32),
        jax.ShapeDtypeStruct((columns, LANES), jnp.float32),
        jax.ShapeDtypeStruct((2 * coded, LANES), jnp.int16),
    ]
    return pl.pallas_call(
        functools.partial(sums_kernel, offsets, has_var),
        grid_spec=pltpu.PrefetchScalarGridSpec(
            num_scalar_prefetch=1,
            grid=(1,),
            in_specs=[pl.BlockSpec(w.shape, whole)] + [pl.BlockSpec(d.shape, whole) for d in data],
            out_specs=[pl.BlockSpec(s.shape, whole) for s in shapes],
            scratch_shapes=[pltpu.VMEM((2, columns, LANES), jnp.float32)],
        ),
        out_shape=shapes,
        compiler_params=params(),
        cost_estimate=cost(2 * w.shape[0] * w.shape[1] * columns, 2 * w.shape[0] * columns + columns * LANES * 10),
        name="partial_sums",
    )(flag, w, *data)


def combine_kernel(bases, own_ref, *refs):
    others, out_ref, acc_ref = refs[:-2], refs[-2], refs[-1]
    height = acc_ref.shape[0]
    steps = [steps_of(o, base, height) for o, base in zip(others, bases)]
    for r in range(0, height, 16):
        total = own_ref[r:r + 16, :]
        for o, base, step in zip(others, bases, steps):
            total = total + decode(o, base + r, step[r * 2 // height])
        acc_ref[r:r + 16, :] = total
    encode(acc_ref, 0, out_ref, 0, height)


def combine(own, *others):
    height = own.shape[0]
    shape = (height + SCALES, LANES)
    return pl.pallas_call(
        functools.partial(combine_kernel, [unit * shape[0] for _, unit in others]),
        out_shape=jax.ShapeDtypeStruct(shape, jnp.int16),
        scratch_shapes=[pltpu.VMEM((height, LANES), jnp.float32)],
        compiler_params=params(),
        cost_estimate=cost(height * LANES * 16, height * LANES * 12),
        name="combine",
    )(own, *[array for array, _ in others])


def each_piece(place_ref, pieces, tiles, do):
    groups = place_ref.shape[0] // 2
    for upper in (1, 0):
        for r in range(groups):
            @pl.when(place_ref[groups + r] == upper)
            def _(r=r):
                first = 0
                for c, count in enumerate(tiles):
                    do((place_ref[r] + first) * LANES, pieces[c * groups + r], count * LANES)
                    first += count


def marginal_kernel(tiles, place_ref, *refs):
    pieces, out_ref, tile_ref = refs[:-2], refs[-2], refs[-1]

    def do(start, piece, height):
        steps = steps_of(piece, 0, height)
        for t in range(0, height, LANES):
            for r in range(0, LANES, 16):
                tile_ref[r:r + 16, :] = decode(piece, t + r, steps[(t + r) * 2 // height])
            out_ref[:, pl.ds(pl.multiple_of(start + t, LANES), LANES)] = tile_ref[...].T

    each_piece(place_ref, pieces, tiles, do)


def marginal(places, pieces, tiles, total):
    shape = (LANES, total * LANES)
    return pl.pallas_call(
        functools.partial(marginal_kernel, tiles),
        grid_spec=pltpu.PrefetchScalarGridSpec(
            num_scalar_prefetch=1,
            grid=(1,),
            in_specs=[pl.BlockSpec(p.shape, lambda i, s: (0, 0)) for p in pieces],
            out_specs=pl.BlockSpec(shape, lambda i, s: (0, 0)),
            scratch_shapes=[pltpu.VMEM((LANES, LANES), jnp.float32)],
        ),
        out_shape=jax.ShapeDtypeStruct(shape, jnp.float32),
        compiler_params=params(),
        cost_estimate=cost(shape[0] * shape[1] * 4, shape[0] * shape[1] * 6),
        name="marginal",
    )(places, *pieces)


def covariance_kernel(tiles, total, ages, rank, place_ref, *refs):
    pieces, out_ref = refs[:-4], refs[-4]
    load_ref, age_ref, cov_ref = refs[-3:]
    pitch = -(-ages // 8) * 8
    left = lax.broadcasted_iota(jnp.int32, (LANES, LANES), 1) < rank

    def do(start, piece, height):
        steps = steps_of(piece, 0, height)
        for r in range(0, height, 16):
            load_ref[pl.ds(pl.multiple_of(start + r, 16), 16), :] = decode(piece, r, steps[r * 2 // height])

    each_piece(place_ref, pieces, tiles, do)

    def turn(t, carry):
        tile = t + t // (total // CORES - 1)
        value = load_ref[pl.ds(pl.multiple_of(tile * LANES, LANES), LANES), :].T
        swapped = pltpu.roll(value, rank, 1)
        age_ref[pl.ds(2 * t, LANES, stride=pitch), :] = jnp.where(left, value, swapped)
        age_ref[pl.ds(2 * t + 1, LANES, stride=pitch), :] = jnp.where(left, swapped, value)
        return carry

    lax.fori_loop(0, ages * rank // LANES, turn, 0, unroll=True)

    def outer(d, carry):
        start = pl.multiple_of(d * pitch, 8)
        mine = age_ref[pl.ds(start, LANES), :]
        high = mine.astype(jnp.bfloat16).astype(jnp.float32)
        low = mine - high
        mixed = jnp.where(left, high, low).astype(jnp.bfloat16)
        product = lax.dot_general(
            jnp.concatenate([mixed, mixed], axis=1),
            jnp.concatenate([high.astype(jnp.bfloat16), low.astype(jnp.bfloat16)], axis=1),
            AFTER,
            preferred_element_type=jnp.float32,
        )
        cov_ref[pl.ds(start, pitch), :] = product[:pitch]
        return carry

    lax.fori_loop(0, LANES, outer, 0, unroll=16)

    def store(m, carry):
        base = pl.multiple_of(m * (2 * ages), 8)
        for p in range(2):
            value = cov_ref[pl.ds(2 * m + p, LANES, stride=pitch), :].T
            out_ref[pl.ds(base + p * ages, ages), :] = value[:ages]
        return carry

    lax.fori_loop(0, ages // 2, store, 0, unroll=True)
    for i in range(ages):
        row = i * (ages + 1)
        out_ref[row:row + 1, :] += load_ref[(total - 1) * LANES + i:(total - 1) * LANES + i + 1, :]


def covariance(places, pieces, tiles, total, ages, rank):
    pitch = -(-ages // 8) * 8
    shape = (ages * ages, LANES)
    tall = (LANES * pitch + LANES - pitch, LANES)
    return pl.pallas_call(
        functools.partial(covariance_kernel, tiles, total, ages, rank),
        grid_spec=pltpu.PrefetchScalarGridSpec(
            num_scalar_prefetch=1,
            grid=(1,),
            in_specs=[pl.BlockSpec(p.shape, lambda i, s: (0, 0)) for p in pieces],
            out_specs=pl.BlockSpec(shape, lambda i, s: (0, 0)),
            scratch_shapes=[
                pltpu.VMEM((total * LANES, LANES), jnp.float32),
                pltpu.VMEM(tall, jnp.float32),
                pltpu.VMEM(tall, jnp.float32),
            ],
        ),
        out_shape=jax.ShapeDtypeStruct(shape, jnp.float32),
        compiler_params=params(),
        cost_estimate=cost(LANES * ages * ages * rank * 16, shape[0] * shape[1] * 4),
        name="covariance",
    )(places, *pieces)


def shards(groups, parts, estimates, factors, variances, intersection_tracts, intersection_weights):
    xs = groups // CORES
    ys = parts // DEPTH
    rows = estimates.shape[0]
    ages = variances.shape[1]
    rank = factors.shape[1] // ages
    geo = lax.axis_index("geo")
    dist = lax.axis_index("dist")
    x, core = geo // CORES, geo % CORES
    z, y = dist // ys, dist % ys

    def move(value, dx, dc, dy=0):
        if (dx, dc, dy) == (0, 0, 0):
            return value
        perm = []
        for g in range(groups):
            for d in range(parts):
                to = (g // CORES + dx) % xs * CORES + (g + dc) % CORES
                perm.append((g * parts + d, to * parts + d // ys * ys + (d + dy) % ys))
        return lax.ppermute(value, ("geo", "dist"), perm)

    def z_swap(value, bits):
        perm = [(a * ys + b, (a ^ bits) * ys + b) for a in range(DEPTH) for b in range(ys)]
        return lax.ppermute(value, "dist", perm)

    last_tile = jnp.pad(variances, ((0, 0), (0, -ages % LANES)))

    def half(array, c, *more):
        width = array.shape[1] // CORES
        return jnp.concatenate([lax.dynamic_slice(array, (0, c * width), (rows, width)), *more], axis=1)

    def start_of(group, tiles):
        return jnp.minimum(group * each_of(tiles), tiles - each_of(tiles))

    def each_of(tiles):
        return -(-tiles // xs)

    def exchange(array, *more):
        return [half(array, core, *more), move(half(array, (core + 1) % CORES, *more), 0, 1)]

    def along_x(both, first, count):
        tiles = both[0].shape[1] // LANES
        size = (rows, count * LANES)

        def part(group):
            start = (start_of(group, tiles) + first) * LANES
            return jnp.concatenate([lax.dynamic_slice(b, (0, start), size) for b in both], axis=0)

        cut = [part((x + dx) % xs) for dx in range(xs)]
        return [move(value, dx, 0) for dx, value in enumerate(cut)], cut[-1]

    load_both = exchange(factors, last_tile)
    load_tiles = split(each_of(load_both[0].shape[1] // LANES), LOAD_FIRST)
    xa, cut_a = along_x(load_both, 0, load_tiles[0])
    xb, _ = along_x(load_both, *load_tiles)

    queries = jnp.concatenate([intersection_tracts.T, intersection_weights.T], axis=0)
    queries = after(queries, cut_a)
    queries = jnp.concatenate([queries, z_swap(queries, 2)], axis=1)
    queries = jnp.concatenate([queries, z_swap(queries, 1)], axis=1)
    bases = jnp.stack([
        (((x - dx) % xs * CORES + (core - dc) % CORES) * parts + z * ys + (y - dy) % ys) * rows
        for dy in range(ys) for dx in range(xs) for dc in range(CORES)
    ]).astype(jnp.int32)
    w = build_weights(bases, queries, rows)
    flag = (x == xs - 1).astype(jnp.int32).reshape(1)
    def along_y(value, first, count, *done):
        sent = after(value[:, first * LANES:(first + count) * LANES], *done)
        return [(value, first)] + [(move(sent, 0, 0, dy), 0) for dy in range(1, ys)]

    def later(by_y, tiles):
        return [(value, first + tiles) for value, first in by_y]

    def merge(by_x):
        return [by_y[dy] for dy in range(ys) for by_y in by_x]

    def along_z(data, count, has_var, before=(), before_middle=()):
        own, opposite, sent = partial_sums(flag, after(w, *before), data, count, has_var)
        near = z_swap(sent, 1)
        middle = combine(after(opposite, *before_middle), (near, 1))
        return own, near, middle, z_swap(middle, 2)

    def spread(own, near, far):
        mine = combine(own, (near, 0), (far, 0))
        along = [move(mine, dx, 0) for dx in range(xs)]
        return mine, [move(along[dx], 0, dc) for dx in range(xs) for dc in range(CORES)]

    def places(tiles):
        starts, lasts = [], []
        for dx in range(xs):
            for dc in range(CORES):
                group = (x - dx) % xs
                starts.append((core - dc) % CORES * tiles + start_of(group, tiles))
                lasts.append(group == xs - 1)
        return jnp.stack(starts + lasts).astype(jnp.int32)

    mean_width = estimates.shape[1] // LANES // CORES
    load_width = factors.shape[1] // LANES // CORES + 1
    mean_tiles = split(each_of(mean_width), MEAN_FIRST)
    (first_a, first_b), (first_c, first_d) = load_tiles, mean_tiles
    mean_x, _ = along_x(exchange(after(estimates, load_both[1])), 0, first_c + first_d)
    data_a = merge([along_y(xa[0], 0, first_a)] + [along_y(value, 0, first_a, w) for value in xa[1:]])
    data_b = merge([along_y(value, 0, first_b, xa[-1]) for value in xb])
    own_a, near_a, middle_a, far_a = along_z(data_a, first_a, False)
    mean_y = along_y(mean_x[0], 0, first_c + first_d, data_a[-1][0])
    there = data_b[-1][0]
    own_b, near_b, middle_b, far_b = along_z(data_b, first_b, True, (own_a,), (middle_a,))
    data_c = merge([mean_y] + [along_y(value, 0, first_c, there) for value in mean_x[1:]])
    data_d = merge([later(mean_y, first_c)] + [along_y(value, first_c, first_d, there) for value in mean_x[1:]])
    own_c, near_c, middle_c, far_c = along_z(data_c, first_c, False, (middle_b, far_a))
    mine_a, load_a = spread(own_a, near_a, far_a)
    own_d, near_d, middle_d, far_d = along_z(data_d, first_d, False, (own_c,), (middle_c,))
    mine_b, load_b = spread(after(own_b, middle_c), near_b, far_b)
    load_pieces = load_a + [after(load_b[0], middle_d)] + load_b[1:]
    cov = covariance(places(load_width), load_pieces, load_tiles, load_width * CORES, ages, rank)
    mine_c, mean_c = spread(own_c, near_c, far_c)
    mine_d, mean_d = spread(after(own_d, cov), near_d, far_d)
    mean_pieces = mean_c + mean_d
    mean = marginal(places(mean_width), mean_pieces, mean_tiles, mean_width * CORES)
    return mean, cov.T


def solution(mesh):
    return jax.shard_map(
        functools.partial(shards, mesh.shape["geo"], mesh.shape["dist"]),
        mesh=mesh,
        in_specs=(
            P(("geo", "dist"), None),
            P(("geo", "dist"), None),
            P(("geo", "dist"), None),
            P("dist", None),
            P("dist", None),
        ),
        out_specs=(P("dist", None), P("dist", None)),
        check_vma=False,
    )
```

```python
import functools
import jax
import jax.numpy as jnp
from jax import lax
from jax.experimental import pallas as pl
from jax.experimental.pallas import tpu as pltpu
from jax.sharding import PartitionSpec as P

LANES = 128
CORES = 2
DEPTH = 4
LOAD_FIRST = 8
MEAN_FIRST = 8
SCALES = 16
TOP = 32767.0
VMEM_BYTES = 48 * 1024 * 1024
BEFORE = (((0,), (0,)), ((), ()))
AFTER = (((1,), (1,)), ((), ()))


def params():
    return pltpu.CompilerParams(vmem_limit_bytes=VMEM_BYTES)


def cost(flops, moved):
    return pl.CostEstimate(flops=flops, bytes_accessed=moved, transcendentals=0)


def after(value, *others):
    return lax.optimization_barrier((value, *others))[0]


def split(each, first):
    first = each // 2 if first >= each else first
    return (first, each - first)


def twice(value):
    return jnp.concatenate([value, value], axis=0)


def encode(src, src_base, dst, dst_base, height):
    half = height // 2
    powers = []
    for h in range(2):
        top = jnp.abs(src[pl.ds(src_base + h * half, 8), :])
        for r in range(8, half, 8):
            top = jnp.maximum(top, jnp.abs(src[pl.ds(src_base + h * half + r, 8), :]))
        power = jnp.floor(jnp.log2(jnp.maximum(top, 1e-30))) + 1.0
        gain = twice(jnp.exp2(-power) * TOP)
        for r in range(h * half, (h + 1) * half, 16):
            level = jnp.clip(jnp.round(src[pl.ds(src_base + r, 16), :] * gain), -TOP, TOP)
            dst[pl.ds(dst_base + r, 16), :] = level.astype(jnp.int32).astype(jnp.int16)
        powers.append(power)
    both = jnp.concatenate(powers, axis=0)
    dst[pl.ds(dst_base + height, SCALES), :] = both.astype(jnp.int32).astype(jnp.int16)


def steps_of(coded, base, height):
    power = coded[pl.ds(base + height, SCALES), :].astype(jnp.int32).astype(jnp.float32)
    step = jnp.exp2(power) * (1.0 / TOP)
    return [twice(step[:8]), twice(step[8:])]


def decode(coded, row, step):
    return coded[pl.ds(row, 16), :].astype(jnp.int32).astype(jnp.float32) * step


def weights_kernel(rows, base_ref, query_ref, out_ref):
    each = query_ref.shape[0] // 2
    row_id = lax.broadcasted_iota(jnp.int32, (16, LANES), 0)

    def piece(j, carry):
        for u in range(DEPTH):
            lanes = slice(u * LANES, (u + 1) * LANES)
            for r in range(0, rows, 16):
                tract = row_id + (base_ref[j] + r)
                total = jnp.zeros((16, LANES), jnp.float32)
                for k in range(each):
                    share = query_ref[each + k:each + k + 1, lanes].astype(jnp.float32) * (1.0 / 256.0)
                    total = jnp.where(query_ref[k:k + 1, lanes] == tract, share, total)
                where = pl.ds(pl.multiple_of(j * rows + r, 16), 16)
                out_ref[where, lanes] = total.astype(jnp.bfloat16)
        return carry

    lax.fori_loop(0, out_ref.shape[0] // rows, piece, 0)


def build_weights(bases, queries, rows):
    pieces = bases.shape[0]
    width = queries.shape[1]
    shape = (pieces * rows, width)
    return pl.pallas_call(
        functools.partial(weights_kernel, rows),
        grid_spec=pltpu.PrefetchScalarGridSpec(
            num_scalar_prefetch=1,
            grid=(1,),
            in_specs=[pl.BlockSpec(queries.shape, lambda i, s: (0, 0))],
            out_specs=pl.BlockSpec(shape, lambda i, s: (0, 0)),
        ),
        out_shape=jax.ShapeDtypeStruct(shape, jnp.bfloat16),
        compiler_params=params(),
        cost_estimate=cost(shape[0] * width * queries.shape[0] * 200, shape[0] * width * 2),
        name="build_weights",
    )(bases, queries)


def sums_kernel(offsets, has_var, flag_ref, w_ref, *refs):
    parts = len(offsets)
    data = refs[:parts]
    own_ref, opposite_ref, sent_ref, acc_ref = refs[parts:]
    columns = own_ref.shape[0]
    coded = columns + SCALES
    rows = [0]
    for d in data:
        rows.append(rows[-1] + d.shape[0])

    def weighted(get, t):
        total = None
        for j in range(parts):
            part = lax.dot_general(
                data[j][:, (offsets[j] + t) * LANES:(offsets[j] + t + 1) * LANES],
                get(w_ref[rows[j]:rows[j + 1], :]),
                BEFORE,
                preferred_element_type=jnp.float32,
            )
            total = part if total is None else total + part
        return total

    def put(t, value):
        where = slice(t * LANES, (t + 1) * LANES)
        for u, ref in enumerate((own_ref, opposite_ref, acc_ref.at[0], acc_ref.at[1])):
            ref[where, :] = value[:, u * LANES:(u + 1) * LANES]

    for t in range(columns // LANES):
        put(t, weighted(lambda w: w, t))

    if has_var:
        @pl.when(flag_ref[0] == 1)
        def _():
            def square(w):
                wide = w.astype(jnp.float32)
                return wide * wide

            def high(w):
                return square(w).astype(jnp.bfloat16)

            def low(w):
                s = square(w)
                return (s - s.astype(jnp.bfloat16).astype(jnp.float32)).astype(jnp.bfloat16)

            t = columns // LANES - 1
            put(t, weighted(high, t) + weighted(low, t))

    for u in range(2):
        encode(acc_ref.at[u], 0, sent_ref, u * coded, columns)


def partial_sums(flag, w, data, count, has_var):
    columns = count * LANES
    offsets = tuple(first for _, first in data)
    data = [array for array, _ in data]
    coded = columns + SCALES
    whole = lambda i, s: (0, 0)
    shapes = [
        jax.ShapeDtypeStruct((columns, LANES), jnp.float32),
        jax.ShapeDtypeStruct((columns, LANES), jnp.float32),
        jax.ShapeDtypeStruct((2 * coded, LANES), jnp.int16),
    ]
    return pl.pallas_call(
        functools.partial(sums_kernel, offsets, has_var),
        grid_spec=pltpu.PrefetchScalarGridSpec(
            num_scalar_prefetch=1,
            grid=(1,),
            in_specs=[pl.BlockSpec(w.shape, whole)] + [pl.BlockSpec(d.shape, whole) for d in data],
            out_specs=[pl.BlockSpec(s.shape, whole) for s in shapes],
            scratch_shapes=[pltpu.VMEM((2, columns, LANES), jnp.float32)],
        ),
        out_shape=shapes,
        compiler_params=params(),
        cost_estimate=cost(2 * w.shape[0] * w.shape[1] * columns, 2 * w.shape[0] * columns + columns * LANES * 10),
        name="partial_sums",
    )(flag, w, *data)


def combine_kernel(bases, own_ref, *refs):
    others, out_ref, acc_ref = refs[:-2], refs[-2], refs[-1]
    height = acc_ref.shape[0]
    steps = [steps_of(o, base, height) for o, base in zip(others, bases)]
    for r in range(0, height, 16):
        total = own_ref[r:r + 16, :]
        for o, base, step in zip(others, bases, steps):
            total = total + decode(o, base + r, step[r * 2 // height])
        acc_ref[r:r + 16, :] = total
    encode(acc_ref, 0, out_ref, 0, height)


def combine(own, *others):
    height = own.shape[0]
    shape = (height + SCALES, LANES)
    return pl.pallas_call(
        functools.partial(combine_kernel, [unit * shape[0] for _, unit in others]),
        out_shape=jax.ShapeDtypeStruct(shape, jnp.int16),
        scratch_shapes=[pltpu.VMEM((height, LANES), jnp.float32)],
        compiler_params=params(),
        cost_estimate=cost(height * LANES * 16, height * LANES * 12),
        name="combine",
    )(own, *[array for array, _ in others])


def each_piece(place_ref, pieces, tiles, do):
    groups = place_ref.shape[0] // 2
    for upper in (1, 0):
        for r in range(groups):
            @pl.when(place_ref[groups + r] == upper)
            def _(r=r):
                first = 0
                for c, count in enumerate(tiles):
                    do((place_ref[r] + first) * LANES, pieces[c * groups + r], count * LANES)
                    first += count


def marginal_kernel(tiles, place_ref, *refs):
    pieces, out_ref, tile_ref = refs[:-2], refs[-2], refs[-1]

    def do(start, piece, height):
        steps = steps_of(piece, 0, height)
        for t in range(0, height, LANES):
            for r in range(0, LANES, 16):
                tile_ref[r:r + 16, :] = decode(piece, t + r, steps[(t + r) * 2 // height])
            out_ref[:, pl.ds(pl.multiple_of(start + t, LANES), LANES)] = tile_ref[...].T

    each_piece(place_ref, pieces, tiles, do)


def marginal(places, pieces, tiles, total):
    shape = (LANES, total * LANES)
    return pl.pallas_call(
        functools.partial(marginal_kernel, tiles),
        grid_spec=pltpu.PrefetchScalarGridSpec(
            num_scalar_prefetch=1,
            grid=(1,),
            in_specs=[pl.BlockSpec(p.shape, lambda i, s: (0, 0)) for p in pieces],
            out_specs=pl.BlockSpec(shape, lambda i, s: (0, 0)),
            scratch_shapes=[pltpu.VMEM((LANES, LANES), jnp.float32)],
        ),
        out_shape=jax.ShapeDtypeStruct(shape, jnp.float32),
        compiler_params=params(),
        cost_estimate=cost(shape[0] * shape[1] * 4, shape[0] * shape[1] * 6),
        name="marginal",
    )(places, *pieces)


def covariance_kernel(tiles, total, ages, rank, place_ref, *refs):
    pieces, out_ref = refs[:-4], refs[-4]
    load_ref, age_ref, cov_ref = refs[-3:]
    pitch = -(-ages // 8) * 8
    left = lax.broadcasted_iota(jnp.int32, (LANES, LANES), 1) < rank

    def do(start, piece, height):
        steps = steps_of(piece, 0, height)
        for r in range(0, height, 16):
            load_ref[pl.ds(pl.multiple_of(start + r, 16), 16), :] = decode(piece, r, steps[r * 2 // height])

    each_piece(place_ref, pieces, tiles, do)

    def turn(t, carry):
        tile = t + t // (total // CORES - 1)
        value = load_ref[pl.ds(pl.multiple_of(tile * LANES, LANES), LANES), :].T
        swapped = pltpu.roll(value, rank, 1)
        age_ref[pl.ds(2 * t, LANES, stride=pitch), :] = jnp.where(left, value, swapped)
        age_ref[pl.ds(2 * t + 1, LANES, stride=pitch), :] = jnp.where(left, swapped, value)
        return carry

    lax.fori_loop(0, ages * rank // LANES, turn, 0, unroll=True)

    def outer(d, carry):
        start = pl.multiple_of(d * pitch, 8)
        mine = age_ref[pl.ds(start, LANES), :]
        high = mine.astype(jnp.bfloat16).astype(jnp.float32)
        low = mine - high
        mixed = jnp.where(left, high, low).astype(jnp.bfloat16)
        product = lax.dot_general(
            jnp.concatenate([mixed, mixed], axis=1),
            jnp.concatenate([high.astype(jnp.bfloat16), low.astype(jnp.bfloat16)], axis=1),
            AFTER,
            preferred_element_type=jnp.float32,
        )
        cov_ref[pl.ds(start, pitch), :] = product[:pitch]
        return carry

    lax.fori_loop(0, LANES, outer, 0, unroll=16)

    def store(m, carry):
        base = pl.multiple_of(m * (2 * ages), 8)
        for p in range(2):
            value = cov_ref[pl.ds(2 * m + p, LANES, stride=pitch), :].T
            out_ref[pl.ds(base + p * ages, ages), :] = value[:ages]
        return carry

    lax.fori_loop(0, ages // 2, store, 0, unroll=True)
    for i in range(ages):
        row = i * (ages + 1)
        out_ref[row:row + 1, :] += load_ref[(total - 1) * LANES + i:(total - 1) * LANES + i + 1, :]


def covariance(places, pieces, tiles, total, ages, rank):
    pitch = -(-ages // 8) * 8
    shape = (ages * ages, LANES)
    tall = (LANES * pitch + LANES - pitch, LANES)
    return pl.pallas_call(
        functools.partial(covariance_kernel, tiles, total, ages, rank),
        grid_spec=pltpu.PrefetchScalarGridSpec(
            num_scalar_prefetch=1,
            grid=(1,),
            in_specs=[pl.BlockSpec(p.shape, lambda i, s: (0, 0)) for p in pieces],
            out_specs=pl.BlockSpec(shape, lambda i, s: (0, 0)),
            scratch_shapes=[
                pltpu.VMEM((total * LANES, LANES), jnp.float32),
                pltpu.VMEM(tall, jnp.float32),
                pltpu.VMEM(tall, jnp.float32),
            ],
        ),
        out_shape=jax.ShapeDtypeStruct(shape, jnp.float32),
        compiler_params=params(),
        cost_estimate=cost(LANES * ages * ages * rank * 16, shape[0] * shape[1] * 4),
        name="covariance",
    )(places, *pieces)


def shards(groups, parts, estimates, factors, variances, intersection_tracts, intersection_weights):
    xs = groups // CORES
    ys = parts // DEPTH
    rows = estimates.shape[0]
    ages = variances.shape[1]
    rank = factors.shape[1] // ages
    geo = lax.axis_index("geo")
    dist = lax.axis_index("dist")
    x, core = geo // CORES, geo % CORES
    z, y = dist // ys, dist % ys

    def move(value, dx, dc, dy=0):
        if (dx, dc, dy) == (0, 0, 0):
            return value
        perm = []
        for g in range(groups):
            for d in range(parts):
                to = (g // CORES + dx) % xs * CORES + (g + dc) % CORES
                perm.append((g * parts + d, to * parts + d // ys * ys + (d + dy) % ys))
        return lax.ppermute(value, ("geo", "dist"), perm)

    def z_swap(value, bits):
        perm = [(a * ys + b, (a ^ bits) * ys + b) for a in range(DEPTH) for b in range(ys)]
        return lax.ppermute(value, "dist", perm)

    last_tile = jnp.pad(variances, ((0, 0), (0, -ages % LANES)))

    def half(array, c, *more):
        width = array.shape[1] // CORES
        return jnp.concatenate([lax.dynamic_slice(array, (0, c * width), (rows, width)), *more], axis=1)

    def start_of(group, tiles):
        return jnp.minimum(group * each_of(tiles), tiles - each_of(tiles))

    def each_of(tiles):
        return -(-tiles // xs)

    def exchange(array, *more):
        return [half(array, core, *more), move(half(array, (core + 1) % CORES, *more), 0, 1)]

    def along_x(both, first, count):
        tiles = both[0].shape[1] // LANES
        size = (rows, count * LANES)

        def part(group):
            start = (start_of(group, tiles) + first) * LANES
            return jnp.concatenate([lax.dynamic_slice(b, (0, start), size) for b in both], axis=0)

        cut = [part((x + dx) % xs) for dx in range(xs)]
        return [move(value, dx, 0) for dx, value in enumerate(cut)], cut[-1]

    load_both = exchange(factors, last_tile)
    load_tiles = split(each_of(load_both[0].shape[1] // LANES), LOAD_FIRST)
    xa, cut_a = along_x(load_both, 0, load_tiles[0])
    xb, _ = along_x(load_both, *load_tiles)

    queries = jnp.concatenate([intersection_tracts.T, intersection_weights.T], axis=0)
    queries = after(queries, cut_a)
    queries = jnp.concatenate([queries, z_swap(queries, 2)], axis=1)
    queries = jnp.concatenate([queries, z_swap(queries, 1)], axis=1)
    bases = jnp.stack([
        (((x - dx) % xs * CORES + (core - dc) % CORES) * parts + z * ys + (y - dy) % ys) * rows
        for dy in range(ys) for dx in range(xs) for dc in range(CORES)
    ]).astype(jnp.int32)
    w = build_weights(bases, queries, rows)
    flag = (x == xs - 1).astype(jnp.int32).reshape(1)
    def along_y(value, first, count, *done):
        sent = after(value[:, first * LANES:(first + count) * LANES], *done)
        return [(value, first)] + [(move(sent, 0, 0, dy), 0) for dy in range(1, ys)]

    def later(by_y, tiles):
        return [(value, first + tiles) for value, first in by_y]

    def merge(by_x):
        return [by_y[dy] for dy in range(ys) for by_y in by_x]

    def along_z(data, count, has_var, before=(), before_middle=()):
        own, opposite, sent = partial_sums(flag, after(w, *before), data, count, has_var)
        near = z_swap(sent, 1)
        middle = combine(after(opposite, *before_middle), (near, 1))
        return own, near, middle, z_swap(middle, 2)

    def spread(own, near, far):
        mine = combine(own, (near, 0), (far, 0))
        along = [move(mine, dx, 0) for dx in range(xs)]
        return mine, [move(along[dx], 0, dc) for dx in range(xs) for dc in range(CORES)]

    def places(tiles):
        starts, lasts = [], []
        for dx in range(xs):
            for dc in range(CORES):
                group = (x - dx) % xs
                starts.append((core - dc) % CORES * tiles + start_of(group, tiles))
                lasts.append(group == xs - 1)
        return jnp.stack(starts + lasts).astype(jnp.int32)

    mean_width = estimates.shape[1] // LANES // CORES
    load_width = factors.shape[1] // LANES // CORES + 1
    mean_tiles = split(each_of(mean_width), MEAN_FIRST)
    (first_a, first_b), (first_c, first_d) = load_tiles, mean_tiles
    mean_x, _ = along_x(exchange(after(estimates, load_both[1])), 0, first_c + first_d)
    data_a = merge([along_y(xa[0], 0, first_a)] + [along_y(value, 0, first_a, w) for value in xa[1:]])
    data_b = merge([along_y(value, 0, first_b, xa[-1]) for value in xb])
    own_a, near_a, middle_a, far_a = along_z(data_a, first_a, False)
    mean_y = along_y(mean_x[0], 0, first_c + first_d, data_a[-1][0])
    there = data_b[-1][0]
    own_b, near_b, middle_b, far_b = along_z(data_b, first_b, True, (own_a,), (middle_a,))
    data_c = merge([mean_y] + [along_y(value, 0, first_c, there) for value in mean_x[1:]])
    data_d = merge([later(mean_y, first_c)] + [along_y(value, first_c, first_d, there) for value in mean_x[1:]])
    own_c, near_c, middle_c, far_c = along_z(data_c, first_c, False, (middle_b, far_a, far_b))
    mine_a, load_a = spread(own_a, near_a, far_a)
    mine_b, load_b = spread(after(own_b, own_c), near_b, far_b)
    own_d, opposite_d, sent_d = partial_sums(flag, after(w, own_c), data_d, first_d, False)
    near_d = z_swap(sent_d, 1)
    load_pieces = load_a + [after(load_b[0], middle_c, own_d)] + load_b[1:]
    cov = covariance(places(load_width), load_pieces, load_tiles, load_width * CORES, ages, rank)
    far_d = z_swap(combine(after(opposite_d, cov), (near_d, 1)), 2)
    mine_c, mean_c = spread(after(own_c, cov), near_c, far_c)
    mine_d, mean_d = spread(own_d, near_d, far_d)
    mean_pieces = mean_c + mean_d
    mean = marginal(places(mean_width), mean_pieces, mean_tiles, mean_width * CORES)
    return mean, cov.T


def solution(mesh):
    return jax.shard_map(
        functools.partial(shards, mesh.shape["geo"], mesh.shape["dist"]),
        mesh=mesh,
        in_specs=(
            P(("geo", "dist"), None),
            P(("geo", "dist"), None),
            P(("geo", "dist"), None),
            P("dist", None),
            P("dist", None),
        ),
        out_specs=(P("dist", None), P("dist", None)),
        check_vma=False,
    )
```

```python
import functools
import jax
import jax.numpy as jnp
from jax import lax
from jax.experimental import pallas as pl
from jax.experimental.pallas import tpu as pltpu
from jax.sharding import PartitionSpec as P

LANES = 128
CORES = 2
DEPTH = 4
LOAD_FIRST = 8
MEAN_FIRST = 8
SCALES = 16
TOP = 32767.0
VMEM_BYTES = 48 * 1024 * 1024
BEFORE = (((0,), (0,)), ((), ()))
AFTER = (((1,), (1,)), ((), ()))


def params():
    return pltpu.CompilerParams(vmem_limit_bytes=VMEM_BYTES)


def cost(flops, moved):
    return pl.CostEstimate(flops=flops, bytes_accessed=moved, transcendentals=0)


def after(value, *others):
    return lax.optimization_barrier((value, *others))[0]


def split(each, first):
    first = each // 2 if first >= each else first
    return (first, each - first)


def twice(value):
    return jnp.concatenate([value, value], axis=0)


def encode(src, src_base, dst, dst_base, height):
    half = height // 2
    powers = []
    for h in range(2):
        top = jnp.abs(src[pl.ds(src_base + h * half, 8), :])
        for r in range(8, half, 8):
            top = jnp.maximum(top, jnp.abs(src[pl.ds(src_base + h * half + r, 8), :]))
        power = jnp.floor(jnp.log2(jnp.maximum(top, 1e-30))) + 1.0
        gain = twice(jnp.exp2(-power) * TOP)
        for r in range(h * half, (h + 1) * half, 16):
            level = jnp.clip(jnp.round(src[pl.ds(src_base + r, 16), :] * gain), -TOP, TOP)
            dst[pl.ds(dst_base + r, 16), :] = level.astype(jnp.int32).astype(jnp.int16)
        powers.append(power)
    both = jnp.concatenate(powers, axis=0)
    dst[pl.ds(dst_base + height, SCALES), :] = both.astype(jnp.int32).astype(jnp.int16)


def steps_of(coded, base, height):
    power = coded[pl.ds(base + height, SCALES), :].astype(jnp.int32).astype(jnp.float32)
    step = jnp.exp2(power) * (1.0 / TOP)
    return [twice(step[:8]), twice(step[8:])]


def decode(coded, row, step):
    return coded[pl.ds(row, 16), :].astype(jnp.int32).astype(jnp.float32) * step


def weights_kernel(rows, base_ref, query_ref, out_ref):
    each = query_ref.shape[0] // 2
    row_id = lax.broadcasted_iota(jnp.int32, (16, LANES), 0)

    def piece(j, carry):
        for u in range(DEPTH):
            lanes = slice(u * LANES, (u + 1) * LANES)
            for r in range(0, rows, 16):
                tract = row_id + (base_ref[j] + r)
                total = jnp.zeros((16, LANES), jnp.float32)
                for k in range(each):
                    share = query_ref[each + k:each + k + 1, lanes].astype(jnp.float32) * (1.0 / 256.0)
                    total = jnp.where(query_ref[k:k + 1, lanes] == tract, share, total)
                where = pl.ds(pl.multiple_of(j * rows + r, 16), 16)
                out_ref[where, lanes] = total.astype(jnp.bfloat16)
        return carry

    lax.fori_loop(0, out_ref.shape[0] // rows, piece, 0)


def build_weights(bases, queries, rows):
    pieces = bases.shape[0]
    width = queries.shape[1]
    shape = (pieces * rows, width)
    return pl.pallas_call(
        functools.partial(weights_kernel, rows),
        grid_spec=pltpu.PrefetchScalarGridSpec(
            num_scalar_prefetch=1,
            grid=(1,),
            in_specs=[pl.BlockSpec(queries.shape, lambda i, s: (0, 0))],
            out_specs=pl.BlockSpec(shape, lambda i, s: (0, 0)),
        ),
        out_shape=jax.ShapeDtypeStruct(shape, jnp.bfloat16),
        compiler_params=params(),
        cost_estimate=cost(shape[0] * width * queries.shape[0] * 200, shape[0] * width * 2),
        name="build_weights",
    )(bases, queries)


def sums_kernel(offsets, has_var, flag_ref, w_ref, *refs):
    parts = len(offsets)
    data = refs[:parts]
    own_ref, opposite_ref, sent_ref, acc_ref = refs[parts:]
    columns = own_ref.shape[0]
    coded = columns + SCALES
    rows = [0]
    for d in data:
        rows.append(rows[-1] + d.shape[0])

    def weighted(get, t):
        total = None
        for j in range(parts):
            part = lax.dot_general(
                data[j][:, (offsets[j] + t) * LANES:(offsets[j] + t + 1) * LANES],
                get(w_ref[rows[j]:rows[j + 1], :]),
                BEFORE,
                preferred_element_type=jnp.float32,
            )
            total = part if total is None else total + part
        return total

    def put(t, value):
        where = slice(t * LANES, (t + 1) * LANES)
        for u, ref in enumerate((own_ref, opposite_ref, acc_ref.at[0], acc_ref.at[1])):
            ref[where, :] = value[:, u * LANES:(u + 1) * LANES]

    for t in range(columns // LANES):
        put(t, weighted(lambda w: w, t))

    if has_var:
        @pl.when(flag_ref[0] == 1)
        def _():
            def square(w):
                wide = w.astype(jnp.float32)
                return wide * wide

            def high(w):
                return square(w).astype(jnp.bfloat16)

            def low(w):
                s = square(w)
                return (s - s.astype(jnp.bfloat16).astype(jnp.float32)).astype(jnp.bfloat16)

            t = columns // LANES - 1
            put(t, weighted(high, t) + weighted(low, t))

    for u in range(2):
        encode(acc_ref.at[u], 0, sent_ref, u * coded, columns)


def partial_sums(flag, w, data, count, has_var):
    columns = count * LANES
    offsets = tuple(first for _, first in data)
    data = [array for array, _ in data]
    coded = columns + SCALES
    whole = lambda i, s: (0, 0)
    shapes = [
        jax.ShapeDtypeStruct((columns, LANES), jnp.float32),
        jax.ShapeDtypeStruct((columns, LANES), jnp.float32),
        jax.ShapeDtypeStruct((2 * coded, LANES), jnp.int16),
    ]
    return pl.pallas_call(
        functools.partial(sums_kernel, offsets, has_var),
        grid_spec=pltpu.PrefetchScalarGridSpec(
            num_scalar_prefetch=1,
            grid=(1,),
            in_specs=[pl.BlockSpec(w.shape, whole)] + [pl.BlockSpec(d.shape, whole) for d in data],
            out_specs=[pl.BlockSpec(s.shape, whole) for s in shapes],
            scratch_shapes=[pltpu.VMEM((2, columns, LANES), jnp.float32)],
        ),
        out_shape=shapes,
        compiler_params=params(),
        cost_estimate=cost(2 * w.shape[0] * w.shape[1] * columns, 2 * w.shape[0] * columns + columns * LANES * 10),
        name="partial_sums",
    )(flag, w, *data)


def combine_kernel(bases, own_ref, *refs):
    others, out_ref, acc_ref = refs[:-2], refs[-2], refs[-1]
    height = acc_ref.shape[0]
    steps = [steps_of(o, base, height) for o, base in zip(others, bases)]
    for r in range(0, height, 16):
        total = own_ref[r:r + 16, :]
        for o, base, step in zip(others, bases, steps):
            total = total + decode(o, base + r, step[r * 2 // height])
        acc_ref[r:r + 16, :] = total
    encode(acc_ref, 0, out_ref, 0, height)


def combine(own, *others):
    height = own.shape[0]
    shape = (height + SCALES, LANES)
    return pl.pallas_call(
        functools.partial(combine_kernel, [unit * shape[0] for _, unit in others]),
        out_shape=jax.ShapeDtypeStruct(shape, jnp.int16),
        scratch_shapes=[pltpu.VMEM((height, LANES), jnp.float32)],
        compiler_params=params(),
        cost_estimate=cost(height * LANES * 16, height * LANES * 12),
        name="combine",
    )(own, *[array for array, _ in others])


def each_piece(place_ref, pieces, tiles, do):
    groups = place_ref.shape[0] // 2
    for upper in (1, 0):
        for r in range(groups):
            @pl.when(place_ref[groups + r] == upper)
            def _(r=r):
                first = 0
                for c, count in enumerate(tiles):
                    do((place_ref[r] + first) * LANES, pieces[c * groups + r], count * LANES)
                    first += count


def marginal_kernel(tiles, place_ref, *refs):
    pieces, out_ref, tile_ref = refs[:-2], refs[-2], refs[-1]

    def do(start, piece, height):
        steps = steps_of(piece, 0, height)
        for t in range(0, height, LANES):
            for r in range(0, LANES, 16):
                tile_ref[r:r + 16, :] = decode(piece, t + r, steps[(t + r) * 2 // height])
            out_ref[:, pl.ds(pl.multiple_of(start + t, LANES), LANES)] = tile_ref[...].T

    each_piece(place_ref, pieces, tiles, do)


def marginal(places, pieces, tiles, total):
    shape = (LANES, total * LANES)
    return pl.pallas_call(
        functools.partial(marginal_kernel, tiles),
        grid_spec=pltpu.PrefetchScalarGridSpec(
            num_scalar_prefetch=1,
            grid=(1,),
            in_specs=[pl.BlockSpec(p.shape, lambda i, s: (0, 0)) for p in pieces],
            out_specs=pl.BlockSpec(shape, lambda i, s: (0, 0)),
            scratch_shapes=[pltpu.VMEM((LANES, LANES), jnp.float32)],
        ),
        out_shape=jax.ShapeDtypeStruct(shape, jnp.float32),
        compiler_params=params(),
        cost_estimate=cost(shape[0] * shape[1] * 4, shape[0] * shape[1] * 6),
        name="marginal",
    )(places, *pieces)


def covariance_kernel(tiles, total, ages, rank, place_ref, *refs):
    pieces, out_ref = refs[:-4], refs[-4]
    load_ref, age_ref, cov_ref = refs[-3:]
    pitch = -(-ages // 8) * 8
    left = lax.broadcasted_iota(jnp.int32, (LANES, LANES), 1) < rank

    def do(start, piece, height):
        steps = steps_of(piece, 0, height)
        for r in range(0, height, 16):
            load_ref[pl.ds(pl.multiple_of(start + r, 16), 16), :] = decode(piece, r, steps[r * 2 // height])

    each_piece(place_ref, pieces, tiles, do)

    def turn(t, carry):
        tile = t + t // (total // CORES - 1)
        value = load_ref[pl.ds(pl.multiple_of(tile * LANES, LANES), LANES), :].T
        swapped = pltpu.roll(value, rank, 1)
        age_ref[pl.ds(2 * t, LANES, stride=pitch), :] = jnp.where(left, value, swapped)
        age_ref[pl.ds(2 * t + 1, LANES, stride=pitch), :] = jnp.where(left, swapped, value)
        return carry

    lax.fori_loop(0, ages * rank // LANES, turn, 0, unroll=True)

    def outer(d, carry):
        start = pl.multiple_of(d * pitch, 8)
        mine = age_ref[pl.ds(start, LANES), :]
        high = mine.astype(jnp.bfloat16).astype(jnp.float32)
        low = mine - high
        mixed = jnp.where(left, high, low).astype(jnp.bfloat16)
        product = lax.dot_general(
            jnp.concatenate([mixed, mixed], axis=1),
            jnp.concatenate([high.astype(jnp.bfloat16), low.astype(jnp.bfloat16)], axis=1),
            AFTER,
            preferred_element_type=jnp.float32,
        )
        cov_ref[pl.ds(start, pitch), :] = product[:pitch]
        return carry

    lax.fori_loop(0, LANES, outer, 0, unroll=16)

    def store(m, carry):
        base = pl.multiple_of(m * (2 * ages), 8)
        for p in range(2):
            value = cov_ref[pl.ds(2 * m + p, LANES, stride=pitch), :].T
            out_ref[pl.ds(base + p * ages, ages), :] = value[:ages]
        return carry

    lax.fori_loop(0, ages // 2, store, 0, unroll=True)
    for i in range(ages):
        row = i * (ages + 1)
        out_ref[row:row + 1, :] += load_ref[(total - 1) * LANES + i:(total - 1) * LANES + i + 1, :]


def covariance(places, pieces, tiles, total, ages, rank):
    pitch = -(-ages // 8) * 8
    shape = (ages * ages, LANES)
    tall = (LANES * pitch + LANES - pitch, LANES)
    return pl.pallas_call(
        functools.partial(covariance_kernel, tiles, total, ages, rank),
        grid_spec=pltpu.PrefetchScalarGridSpec(
            num_scalar_prefetch=1,
            grid=(1,),
            in_specs=[pl.BlockSpec(p.shape, lambda i, s: (0, 0)) for p in pieces],
            out_specs=pl.BlockSpec(shape, lambda i, s: (0, 0)),
            scratch_shapes=[
                pltpu.VMEM((total * LANES, LANES), jnp.float32),
                pltpu.VMEM(tall, jnp.float32),
                pltpu.VMEM(tall, jnp.float32),
            ],
        ),
        out_shape=jax.ShapeDtypeStruct(shape, jnp.float32),
        compiler_params=params(),
        cost_estimate=cost(LANES * ages * ages * rank * 16, shape[0] * shape[1] * 4),
        name="covariance",
    )(places, *pieces)


def shards(groups, parts, estimates, factors, variances, intersection_tracts, intersection_weights):
    xs = groups // CORES
    ys = parts // DEPTH
    rows = estimates.shape[0]
    ages = variances.shape[1]
    rank = factors.shape[1] // ages
    geo = lax.axis_index("geo")
    dist = lax.axis_index("dist")
    x, core = geo // CORES, geo % CORES
    z, y = dist // ys, dist % ys

    def move(value, dx, dc, dy=0):
        if (dx, dc, dy) == (0, 0, 0):
            return value
        perm = []
        for g in range(groups):
            for d in range(parts):
                to = (g // CORES + dx) % xs * CORES + (g + dc) % CORES
                perm.append((g * parts + d, to * parts + d // ys * ys + (d + dy) % ys))
        return lax.ppermute(value, ("geo", "dist"), perm)

    def z_swap(value, bits):
        perm = [(a * ys + b, (a ^ bits) * ys + b) for a in range(DEPTH) for b in range(ys)]
        return lax.ppermute(value, "dist", perm)

    last_tile = jnp.pad(variances, ((0, 0), (0, -ages % LANES)))

    def half(array, c, *more):
        width = array.shape[1] // CORES
        return jnp.concatenate([lax.dynamic_slice(array, (0, c * width), (rows, width)), *more], axis=1)

    def start_of(group, tiles):
        return jnp.minimum(group * each_of(tiles), tiles - each_of(tiles))

    def each_of(tiles):
        return -(-tiles // xs)

    def exchange(array, *more):
        return [half(array, core, *more), move(half(array, (core + 1) % CORES, *more), 0, 1)]

    def along_x(both, first, count):
        tiles = both[0].shape[1] // LANES
        size = (rows, count * LANES)

        def part(group):
            start = (start_of(group, tiles) + first) * LANES
            return jnp.concatenate([lax.dynamic_slice(b, (0, start), size) for b in both], axis=0)

        cut = [part((x + dx) % xs) for dx in range(xs)]
        return [move(value, dx, 0) for dx, value in enumerate(cut)], cut[-1]

    load_both = exchange(factors, last_tile)
    load_tiles = split(each_of(load_both[0].shape[1] // LANES), LOAD_FIRST)
    xa, cut_a = along_x(load_both, 0, load_tiles[0])
    xb, _ = along_x(load_both, *load_tiles)

    queries = jnp.concatenate([intersection_tracts.T, intersection_weights.T], axis=0)
    queries = after(queries, cut_a)
    queries = jnp.concatenate([queries, z_swap(queries, 2)], axis=1)
    queries = jnp.concatenate([queries, z_swap(queries, 1)], axis=1)
    bases = jnp.stack([
        (((x - dx) % xs * CORES + (core - dc) % CORES) * parts + z * ys + (y - dy) % ys) * rows
        for dy in range(ys) for dx in range(xs) for dc in range(CORES)
    ]).astype(jnp.int32)
    w = build_weights(bases, queries, rows)
    flag = (x == xs - 1).astype(jnp.int32).reshape(1)
    def along_y(value, first, count, *done):
        sent = after(value[:, first * LANES:(first + count) * LANES], *done)
        return [(value, first)] + [(move(sent, 0, 0, dy), 0) for dy in range(1, ys)]

    def later(by_y, tiles):
        return [(value, first + tiles) for value, first in by_y]

    def merge(by_x):
        return [by_y[dy] for dy in range(ys) for by_y in by_x]

    def along_z(data, count, has_var, before=(), before_middle=()):
        own, opposite, sent = partial_sums(flag, after(w, *before), data, count, has_var)
        near = z_swap(sent, 1)
        middle = combine(after(opposite, *before_middle), (near, 1))
        return own, near, middle, z_swap(middle, 2)

    def spread(own, near, far):
        mine = combine(own, (near, 0), (far, 0))
        along = [move(mine, dx, 0) for dx in range(xs)]
        return mine, [move(along[dx], 0, dc) for dx in range(xs) for dc in range(CORES)]

    def places(tiles):
        starts, lasts = [], []
        for dx in range(xs):
            for dc in range(CORES):
                group = (x - dx) % xs
                starts.append((core - dc) % CORES * tiles + start_of(group, tiles))
                lasts.append(group == xs - 1)
        return jnp.stack(starts + lasts).astype(jnp.int32)

    mean_width = estimates.shape[1] // LANES // CORES
    load_width = factors.shape[1] // LANES // CORES + 1
    mean_tiles = split(each_of(mean_width), MEAN_FIRST)
    (first_a, first_b), (first_c, first_d) = load_tiles, mean_tiles
    mean_x, _ = along_x(exchange(after(estimates, load_both[1])), 0, first_c + first_d)
    data_a = merge([along_y(xa[0], 0, first_a)] + [along_y(value, 0, first_a, w) for value in xa[1:]])
    data_b = merge([along_y(value, 0, first_b, xa[-1]) for value in xb])
    own_a, near_a, middle_a, far_a = along_z(data_a, first_a, False)
    mean_y = along_y(mean_x[0], 0, first_c + first_d, data_a[-1][0])
    there = data_b[-1][0]
    own_b, near_b, middle_b, far_b = along_z(data_b, first_b, True, (own_a,), (middle_a,))
    data_c = merge([mean_y] + [along_y(value, 0, first_c, there) for value in mean_x[1:]])
    data_d = merge([later(mean_y, first_c)] + [along_y(value, first_c, first_d, there) for value in mean_x[1:]])
    own_c, near_c, middle_c, far_c = along_z(data_c, first_c, False, (middle_b, far_a, far_b))
    mine_a, load_a = spread(own_a, near_a, far_a)
    mine_b, load_b = spread(after(own_b, own_c), near_b, far_b)
    own_d, opposite_d, sent_d = partial_sums(flag, after(w, own_c), data_d, first_d, False)
    near_d = z_swap(sent_d, 1)
    middle_d = combine(after(opposite_d, middle_c), (near_d, 1))
    far_d = z_swap(middle_d, 2)
    load_pieces = load_a + [after(load_b[0], middle_d)] + load_b[1:]
    cov = covariance(places(load_width), load_pieces, load_tiles, load_width * CORES, ages, rank)
    mine_c, mean_c = spread(after(own_c, cov), near_c, far_c)
    mine_d, mean_d = spread(after(own_d, cov), near_d, far_d)
    mean_pieces = mean_c + mean_d
    mean = marginal(places(mean_width), mean_pieces, mean_tiles, mean_width * CORES)
    return mean, cov.T


def solution(mesh):
    return jax.shard_map(
        functools.partial(shards, mesh.shape["geo"], mesh.shape["dist"]),
        mesh=mesh,
        in_specs=(
            P(("geo", "dist"), None),
            P(("geo", "dist"), None),
            P(("geo", "dist"), None),
            P("dist", None),
            P("dist", None),
        ),
        out_specs=(P("dist", None), P("dist", None)),
        check_vma=False,
    )
```
